32 devices in a mesh: fsdp: 32 (over z, y, x, core).
Axes of the slice: x: 2, y: 2, z: 4, core: 2. Of those that a mesh axis runs over, the one named last changes fastest.
Arguments:
- tokens: bfloat16 [2, 64, 197, 384], P(None, 'fsdp'), may hold values from -6 to 6
- cotangent: bfloat16 [2, 64, 197, 384], P(None, 'fsdp'), may hold values from -6 to 6
- image_valid: int32 [2, 64], P(None, 'fsdp'), may hold values 0 or 1
- routes: int32 [2, 64, 197, 2], P(None, 'fsdp'), may hold values from 0 to 3, all different within a row; in each aligned block of 394 rows (0 to 393, 394 to 787, ..., all dimensions but the last counted through in order) at most 264 rows name the same one
- norm_gains: bfloat16 [1536], P('fsdp'), may hold values from 0.099609375 to 1.8984375
- attend_in_one: bfloat16 [442368], P('fsdp'), may hold values from -0.3125 to 0.3125
- attend_out_one: bfloat16 [147456], P('fsdp'), may hold values from -2.5 to 2.5
- widen_one: bfloat16 [589824], P('fsdp'), may hold values from -0.3125 to 0.3125
- narrow_one: bfloat16 [589824], P('fsdp'), may hold values from -0.15625 to 0.15625
- router: bfloat16 [1536], P('fsdp'), may hold values from -0.15625 to 0.15625
- attend_in_two: bfloat16 [442368], P('fsdp'), may hold values from -0.3125 to 0.3125
- attend_out_two: bfloat16 [147456], P('fsdp'), may hold values from -2.5 to 2.5
- experts_widen: bfloat16 [2359296], P('fsdp'), may hold values from -0.3125 to 0.3125
- experts_narrow: bfloat16 [2359296], P('fsdp'), may hold values from -0.3125 to 0.3125
Outputs:
- block_out: bfloat16 [2, 64, 197, 384], P(None, 'fsdp')
- delta_tokens: bfloat16 [2, 64, 197, 384], P(None, 'fsdp')
- delta_gains: float32 [1536], P('fsdp')
- delta_attend_in_one: float32 [442368], P('fsdp')
- delta_attend_out_one: float32 [147456], P('fsdp')
- delta_widen_one: float32 [589824], P('fsdp')
- delta_narrow_one: float32 [589824], P('fsdp')
- delta_router: float32 [1536], P('fsdp')
- delta_attend_in_two: float32 [442368], P('fsdp')
- delta_attend_out_two: float32 [147456], P('fsdp')
- delta_experts_widen: float32 [2359296], P('fsdp')
- delta_experts_narrow: float32 [2359296], P('fsdp')
The draws below stay inside these ranges and needn't reach their ends.
Inputs may be any that keep to these rules, and one draw needn't show every extreme that they name: In every micro-batch, at most 264 of the 788 routes of one device's images name the same expert, and in some such blocks one expert is named exactly 264 times; a token's two experts differ.
All inputs are finite; a program needn't handle non-finite values. No bound on the sum of `image_valid` on one device may be relied on, other than what follows from the above.
Results may differ from the reference program's by a relative error of at most 0.019.
Values may be sent and summed in bfloat16 or wider, within the bound.
A program may use at most 192 MiB of HBM per device.

```python
import math
import jax
import jax.numpy as jnp
import numpy as np
from jax import lax

D = 384
HEADS = 6
HDIM = 64
FF = 1536
EXPERTS = 4
SEQ = 197
MICRO = 2
IMG_DEV = 2
CAP = 264
IMAGES = 64
N_FSDP = 32


def set_ends(entries, key, low, largest):
    longest = entries.shape.index(max(entries.shape))
    spots = []
    for shift in (0, 1):
        where = [jax.random.randint(jax.random.fold_in(key, axis), (), 0, length) for axis, length in enumerate(entries.shape)]
        where[longest] = (where[longest] + shift) % entries.shape[longest]
        spots.append(tuple(where))
    return entries.at[spots[0]].set(low).at[spots[1]].set(largest)


def block_scale(key, extent, cuts, least, top_value):
    factor_of, own = 1.0, jax.random.fold_in(key, 6)
    for dim, shards_of in cuts:
        heights = jnp.exp(jax.random.uniform(jax.random.fold_in(own, dim), (shards_of,), jnp.float32, least / len(cuts), top_value / len(cuts)))
        factor_of = factor_of * jnp.repeat(heights, extent[dim] // shards_of).reshape([-1 if axis == dim else 1 for axis in range(len(extent))])
    return factor_of


def routed_block(rng, own, number, rows, count, top, most, lean):
    order = jax.random.permutation(rng, count)
    packed, ordinary = portions_of(count, rows * top, most, lean, True), portions_of(count, rows * top, most, lean, False)
    places = jnp.arange(count)

    def named(sizes, rotation):
        used = int((sizes > 0).sum())
        fixed = max(1, used // 4)
        shifted = fixed + (places - fixed + rotation * (used - fixed)) % max(1, count - fixed)
        return jnp.zeros((count,), jnp.int32).at[order[jnp.where(places < fixed, places, shifted)]].set(jnp.asarray(sizes, jnp.int32))

    sizes = jnp.where(number % 4 == 0, named(packed, number // 4), named(ordinary, number - number // 4 - 1))
    mixed = jax.random.permutation(jax.random.fold_in(own, 3), count)
    donor, sink = mixed[0:count // 2 * 2:2], mixed[1:count // 2 * 2:2]
    margin = jnp.minimum(sizes[donor] - 1, most - sizes[sink]) // 2
    margin = jnp.where((donor == order[0]) | (sink == order[0]) | (sizes[sink] == 0), 0, jnp.maximum(margin, 0))
    shifted = jax.random.randint(jax.random.fold_in(own, 4), (count // 2,), 0, 1 << 20) % (margin + 1)
    sizes = sizes.at[donor].add(-shifted).at[sink].add(shifted)
    items = jnp.searchsorted(jnp.cumsum(sizes), jnp.arange(rows * top), side="right").astype(jnp.int32)
    table = items.reshape(top, rows).T
    table = table[jax.random.permutation(jax.random.fold_in(own, 1), rows)]
    rotation = jax.random.randint(jax.random.fold_in(own, 2), (rows, 1), 0, top)
    return jnp.take_along_axis(table, (jnp.arange(top)[None, :] + rotation) % top, axis=1)


def portions_of(number_of, total, most, lean, full):
    loads = [(1 << 20) // math.isqrt(rank ** lean) + 1 for rank in range(1, number_of + 1)]
    largest = most if full else min(most, max(-(-total // number_of), total * loads[0] // sum(loads)))
    least = 1 if total - largest >= number_of - 1 else 0
    counts, surplus = [largest] + [least] * (number_of - 1), total - largest - least * (number_of - 1)
    while surplus > 0:
        movable = [i for i in range(1, number_of) if counts[i] < largest] or [i for i in range(1, number_of) if counts[i] < most]
        whole, left = sum([loads[i] for i in movable]), surplus
        for i in movable:
            extra = min(most - counts[i], max(1, left * loads[i] // whole), surplus)
            counts[i] = counts[i] + extra
            surplus = surplus - extra
    return np.array(counts)


def normal_values(key, shape, deviation, most, split=(), kind=jnp.bfloat16):
    level = block_scale(key, shape, split, -0.22, 0.18) if split else 1.0
    array = jax.random.normal(key, shape, jnp.float32) * deviation * level
    return jnp.minimum(jnp.maximum(array, -most), most).astype(kind)


def setup_inputs(seed: int = 0) -> dict:
    key_list = jax.random.split(jax.random.key(seed), 15)
    tokens = normal_values(key_list[0], (MICRO, IMAGES, SEQ, D), 1.0, 6.0, ((1, 32),))
    cotangent = normal_values(key_list[1], (MICRO, IMAGES, SEQ, D), 1.0, 6.0, ((1, 32),))
    image_valid = set_ends((jax.random.randint(key_list[2], (MICRO, IMAGES), 0, 4) < 3).astype(jnp.int32), jax.random.fold_in(key_list[2], 1), 0, 1)
    routes_keys = jax.random.split(jax.random.fold_in(key_list[3], 1), MICRO * IMAGES * SEQ // (IMG_DEV * SEQ))
    routes_turns = jax.random.permutation(jax.random.fold_in(key_list[3], 3), MICRO * IMAGES * SEQ // (IMG_DEV * SEQ))
    routes = jax.vmap(lambda own, number: routed_block(jax.random.fold_in(key_list[3], 2), own, number, IMG_DEV * SEQ, EXPERTS, 2, CAP, 1))(routes_keys, routes_turns).reshape((MICRO, IMAGES, SEQ, 2))
    norm_gains = jnp.clip(1.0 + 0.18 * jax.random.normal(key_list[4], (4 * D,), jnp.float32), 0.099609375, 1.8984375).astype(jnp.bfloat16)
    attend_in_one = normal_values(key_list[5], (3 * D * D,), D ** -0.5, 0.3125, ((0, 32),))
    attend_out_one = normal_values(key_list[6], (D * D,), (D // 64) ** -0.5, 2.5, ((0, 32),))
    widen_one = normal_values(key_list[7], (D * FF,), D ** -0.5, 0.3125, ((0, 32),))
    narrow_one = normal_values(key_list[8], (FF * D,), FF ** -0.5, 0.15625, ((0, 32),))
    router = normal_values(key_list[9], (D * EXPERTS,), (4 * D) ** -0.5, 0.15625, ((0, 32),))
    attend_in_two = normal_values(key_list[10], (3 * D * D,), D ** -0.5, 0.3125, ((0, 32),))
    attend_out_two = normal_values(key_list[11], (D * D,), (D // 64) ** -0.5, 2.5, ((0, 32),))
    experts_widen = normal_values(key_list[12], (EXPERTS * D * FF,), D ** -0.5, 0.3125, ((0, 32),))
    experts_narrow = normal_values(key_list[13], (EXPERTS * FF * D,), (FF // 4) ** -0.5, 0.3125, ((0, 32),))
    return {"tokens": tokens, "cotangent": cotangent, "image_valid": image_valid, "routes": routes, "norm_gains": norm_gains, "attend_in_one": attend_in_one, "attend_out_one": attend_out_one, "widen_one": widen_one, "narrow_one": narrow_one, "router": router, "attend_in_two": attend_in_two, "attend_out_two": attend_out_two, "experts_widen": experts_widen, "experts_narrow": experts_narrow}


EPSILON = 1e-06

@jax.custom_vjp
def low(v):
    return lax.optimization_barrier(v.astype(jnp.bfloat16)).astype(jnp.float32)

@jax.custom_vjp
def low_back(v):
    return v

def low_keep(v):
    return (low(v), None)

def low_pass(kept, grad):
    return (grad,)

def back_keep(v):
    return (v, None)

def back_low(kept, grad):
    return (low(grad),)
low.defvjp(low_keep, low_pass)
low_back.defvjp(back_keep, back_low)

def normalize(states, gain_row):
    centred = states - lax.optimization_barrier(jnp.mean(states, axis=-1, keepdims=True))
    variance = lax.optimization_barrier(jnp.mean(centred * centred, axis=-1, keepdims=True))
    return centred * lax.rsqrt(variance + EPSILON) * gain_row

def route_slots(route_block):
    route_count = route_block.shape[0] * 2
    expert_ids = route_block.reshape(route_count).astype(jnp.int32)
    one_hot = (expert_ids[:, None] == jnp.arange(EXPERTS, dtype=jnp.int32)[None, :]).astype(jnp.int32)
    before = jnp.cumsum(one_hot, axis=0) - one_hot
    position = lax.optimization_barrier(jnp.sum(before * one_hot, axis=1)).astype(jnp.int32)
    slot_index = (expert_ids * CAP + position).astype(jnp.int32)
    slot_route = jnp.full((EXPERTS * CAP,), route_count, jnp.int32).at[slot_index].set(jnp.arange(route_count, dtype=jnp.int32))
    return (slot_index.reshape(route_block.shape[0], 2), slot_route)

def attention_part(states, gain_row, attend_in, attend_out):
    highest = lax.Precision.HIGHEST
    normed = low(normalize(states, gain_row))
    qkv_rows = low_back(low(jnp.dot(normed, attend_in, precision=highest)))
    images = states.shape[0] // SEQ
    stacked = qkv_rows.reshape(images, SEQ, 3, HEADS, HDIM)
    scores = jnp.einsum('bqhd,bkhd->bhqk', stacked[:, :, 0], stacked[:, :, 1], precision=highest) * HDIM ** (-0.5)
    scores = low_back(scores)
    softmaxed = low(jax.nn.softmax(scores, axis=-1))
    attended = jnp.einsum('bhqk,bkhd->bqhd', softmaxed, stacked[:, :, 2], precision=highest)
    attended = low_back(low(attended.reshape(states.shape)))
    return states + low_back(jnp.dot(attended, attend_out, precision=highest))

def dense_part(states, gain_row, widen, narrow):
    highest = lax.Precision.HIGHEST
    normed = low(normalize(states, gain_row))
    inner_act = low_back(jnp.dot(normed, widen, precision=highest))
    hidden = low(jax.nn.gelu(inner_act, approximate=True))
    return states + low_back(jnp.dot(hidden, narrow, precision=highest))

def expert_part(states, gain_row, router_weight, widen_weight, narrow_weight, route_block):
    highest = lax.Precision.HIGHEST
    normed = low(normalize(states, gain_row))
    logits = low_back(jnp.dot(normed, router_weight, precision=highest))
    router_probs = jax.nn.softmax(logits, axis=-1)
    gate_values = jnp.take_along_axis(router_probs, route_block, axis=1)
    slot_index, slot_route = route_slots(route_block)
    padded = jnp.concatenate([normed, jnp.zeros((1, D), jnp.float32)], axis=0)
    dispatched = padded[slot_route // 2].reshape(EXPERTS, CAP, D)
    inner_act = low_back(jnp.einsum('ecd,edf->ecf', dispatched, widen_weight, precision=highest))
    hidden = low(jax.nn.gelu(inner_act, approximate=True))
    returned = low_back(jnp.einsum('ecf,efd->ecd', hidden, narrow_weight, precision=highest))
    picked = returned.reshape(EXPERTS * CAP, D)[slot_index]
    return states + lax.optimization_barrier(jnp.sum(gate_values[:, :, None] * picked, axis=1))

def block_forward(token_block, route_block, valid_block, weights):
    gain_rows, in_one, out_one, widen_one, narrow_one, router_weight, in_two, out_two, widen_experts, narrow_experts = weights
    states = token_block.reshape(-1, D)
    states = attention_part(states, gain_rows[0], in_one, out_one)
    states = dense_part(states, gain_rows[1], widen_one, narrow_one)
    states = attention_part(states, gain_rows[2], in_two, out_two)
    states = expert_part(states, gain_rows[3], router_weight, widen_experts, narrow_experts, route_block)
    valid_rows = jnp.repeat(valid_block, SEQ)[:, None]
    return (states * valid_rows).reshape(token_block.shape)

def forward(tokens_float, weights, routes, valid_float):
    block_count = MICRO * N_FSDP
    token_blocks = tokens_float.reshape(block_count, IMG_DEV, SEQ, D)
    route_blocks = routes.reshape(block_count, IMG_DEV * SEQ, 2)
    valid_blocks = valid_float.reshape(block_count, IMG_DEV)

    def block_step(inputs):
        return block_forward(inputs[0], inputs[1], inputs[2], weights)
    results = lax.map(jax.checkpoint(block_step), (token_blocks, route_blocks, valid_blocks))
    return results.reshape(tokens_float.shape)

def reference(tokens, cotangent, image_valid, routes, norm_gains, attend_in_one, attend_out_one, widen_one, narrow_one, router, attend_in_two, attend_out_two, experts_widen, experts_narrow):
    weights = (norm_gains.astype(jnp.float32).reshape(4, D), attend_in_one.astype(jnp.float32).reshape(D, 3 * D), attend_out_one.astype(jnp.float32).reshape(D, D), widen_one.astype(jnp.float32).reshape(D, FF), narrow_one.astype(jnp.float32).reshape(FF, D), router.astype(jnp.float32).reshape(D, EXPERTS), attend_in_two.astype(jnp.float32).reshape(D, 3 * D), attend_out_two.astype(jnp.float32).reshape(D, D), experts_widen.astype(jnp.float32).reshape(EXPERTS, D, FF), experts_narrow.astype(jnp.float32).reshape(EXPERTS, FF, D))
    valid_float = image_valid.astype(jnp.float32)

    def whole(tokens_float, weight_list):
        return forward(tokens_float, weight_list, routes, valid_float)
    outputs, pullback = jax.vjp(whole, tokens.astype(jnp.float32), weights)
    delta_input, delta_weights = pullback(cotangent.astype(jnp.float32))
    return (outputs.astype(jnp.bfloat16), delta_input.astype(jnp.bfloat16), delta_weights[0].reshape(-1), delta_weights[1].reshape(-1), delta_weights[2].reshape(-1), delta_weights[3].reshape(-1), delta_weights[4].reshape(-1), delta_weights[5].reshape(-1), delta_weights[6].reshape(-1), delta_weights[7].reshape(-1), delta_weights[8].reshape(-1), delta_weights[9].reshape(-1))
```

```python
import functools
import math

import jax
import jax.numpy as jnp
import numpy as np
from jax import lax
from jax.experimental import pallas as pl
from jax.experimental.pallas import tpu as pltpu
from jax.sharding import PartitionSpec as P

D = 384
HEADS = 6
HDIM = 64
FF = 1536
EXPERTS = 4
SEQ = 197
PAD = 208
PAIRS = HEADS // 2
SHARDS = 32
ROWS = D // SHARDS
LANES = 128
EPSILON = 1e-06
BF = jnp.bfloat16
F32 = jnp.float32
MESH = pl.DeviceIdType.MESH
C0 = math.sqrt(2.0 / math.pi)
C1 = 0.044715


def dot_nn(a, b):
    return lax.dot_general(a, b, (((1,), (0,)), ((), ())), preferred_element_type=F32)


def dot_nt(a, b):
    return lax.dot_general(a, b, (((1,), (1,)), ((), ())), preferred_element_type=F32)


def dot_tn(a, b):
    return lax.dot_general(a, b, (((0,), (0,)), ((), ())), preferred_element_type=F32)


def normed(x):
    centred = x - jnp.mean(x, axis=-1, keepdims=True)
    rstd = lax.rsqrt(jnp.mean(centred * centred, axis=-1, keepdims=True) + EPSILON)
    return centred * rstd, rstd


def norm_back(x, gain, dhn):
    xhat, rstd = normed(x)
    dxhat = dhn * gain
    mean_d = jnp.mean(dxhat, axis=-1, keepdims=True)
    mean_dx = jnp.mean(dxhat * xhat, axis=-1, keepdims=True)
    return rstd * (dxhat - mean_d - xhat * mean_dx), jnp.sum(dhn * xhat, axis=0, keepdims=True)


def gelu_both(u):
    u2 = u * u
    t = jnp.tanh(u * (C0 + (C0 * C1) * u2))
    h = 0.5 + 0.5 * t
    z = u * h
    return z, h + z * (1.0 - h) * (2.0 * C0 + (6.0 * C0 * C1) * u2)


def rows_of(i, size=PAD):
    return pl.ds(pl.multiple_of(i * size, 16), size)


def loop(count, body, ticks=()):
    def step(i, carry):
        body(i)
        for k, tick in enumerate(ticks):
            pl.when(i == k)(tick)
        return carry

    lax.fori_loop(0, count, step, 0)


def attention_forward(images, x_in, x_out, gain, win, wout, hn_ref, qkv_ref, pb_ref, o_ref, ticks=()):
    low_half = lax.broadcasted_iota(jnp.int32, (PAD, LANES), 1) < HDIM
    real_key = lax.broadcasted_iota(jnp.int32, (2 * PAD, PAD), 1) < SEQ

    def image(i):
        r = rows_of(i)
        x = x_in[r, :].astype(F32)
        xhat, _ = normed(x)
        hn = (xhat * gain).astype(BF)
        hn_ref[r, :] = hn
        for j in range(3):
            cols = pl.ds(D * j, D)
            qkv_ref[r, cols] = dot_nn(hn, win[:, cols]).astype(BF)
        for p in range(PAIRS):
            q2 = qkv_ref[r, pl.ds(LANES * p, LANES)]
            k2 = qkv_ref[r, pl.ds(D + LANES * p, LANES)]
            v2 = qkv_ref[r, pl.ds(2 * D + LANES * p, LANES)]
            zero = jnp.zeros_like(q2)
            qs = jnp.concatenate([jnp.where(low_half, q2, zero), jnp.where(low_half, zero, q2)], axis=0)
            s = dot_nt(qs, k2) * HDIM ** (-0.5)
            s = jnp.where(real_key, s, -1e30)
            w = jnp.exp(s - jnp.max(s, axis=-1, keepdims=True))
            soft = w * (1.0 / jnp.sum(w, axis=-1, keepdims=True))
            pb = soft.astype(BF)
            pb_ref[i * PAIRS + p] = pb
            o2 = dot_nn(pb, v2)
            o_ref[r, pl.ds(LANES * p, LANES)] = jnp.where(low_half, o2[:PAD], o2[PAD:]).astype(BF)
        x_out[r, :] = x + dot_nn(o_ref[r, :], wout[...])

    loop(images, image, ticks)


def attention_backward(
    images, b_ref, x_in, gain, win, wout, hn_ref, qkv_ref, pb_ref, o_ref, da_ref, dqkv_ref, dgain_ref, dwin, dwout, ticks=()
):
    low_half = lax.broadcasted_iota(jnp.int32, (PAD, LANES), 1) < HDIM
    dgain_ref[...] = jnp.zeros_like(dgain_ref)

    def image(i):
        r = rows_of(i)
        b = b_ref[r, :]
        da = b.astype(BF)
        da_ref[r, :] = da
        do = dot_nt(da, wout[...]).astype(BF)
        for p in range(PAIRS):
            cols = [pl.ds(D * j + LANES * p, LANES) for j in range(3)]
            q2, k2, v2 = (qkv_ref[r, c] for c in cols)
            do2 = do[:, LANES * p : LANES * (p + 1)]
            zero = jnp.zeros_like(q2)
            qs = jnp.concatenate([jnp.where(low_half, q2, zero), jnp.where(low_half, zero, q2)], axis=0)
            dos = jnp.concatenate([jnp.where(low_half, do2, zero), jnp.where(low_half, zero, do2)], axis=0)
            pb = pb_ref[i * PAIRS + p]
            soft = pb.astype(F32)
            dp = dot_nt(dos, v2)
            ds = (soft * (dp - jnp.sum(dp * soft, axis=-1, keepdims=True))).astype(BF)
            dq = dot_nn(ds, k2) * HDIM ** (-0.5)
            dqkv_ref[r, cols[0]] = jnp.where(low_half, dq[:PAD], dq[PAD:]).astype(BF)
            dqkv_ref[r, cols[1]] = (dot_tn(ds, qs) * HDIM ** (-0.5)).astype(BF)
            dqkv_ref[r, cols[2]] = dot_tn(pb, dos).astype(BF)
        dhn = dot_nt(dqkv_ref[r, pl.ds(0, 3 * D)], win[...])
        dx, dg = norm_back(x_in[r, :].astype(F32), gain, dhn)
        b_ref[r, :] = b + dx
        dgain_ref[...] += dg

    loop(images, image, ticks)
    dwout[...] = dot_tn(o_ref[...], da_ref[...]).astype(BF)
    hn = hn_ref[...]
    for j in range(3):
        cols = pl.ds(D * j, D)
        dwin[:, cols] = dot_tn(hn, dqkv_ref[:, cols]).astype(BF)


def piece_rows(buf, z, row, cols=None):
    block = buf[z, :, :, :, row : row + 48, :]
    return block.reshape(8 * 48, D)


def narrow_tile(w1b, j):
    return piece_rows(w1b, j, 96)


def row_block(images):
    return 2 * PAD if images % 2 == 0 else PAD


def dense_forward(images, x_in, x_out, gain, wid, w1b, hn_ref, z_ref, g_ref, ticks=()):
    size = row_block(images)

    def block(i):
        r = rows_of(i, size)
        x = x_in[r, :]
        hn = (normed(x)[0] * gain).astype(BF)
        hn_ref[r, :] = hn
        for j in range(4):
            cols = pl.ds(D * j, D)
            z, g = gelu_both(dot_nn(hn, wid[:, cols]))
            z = z.astype(BF)
            z_ref[r, cols] = z
            g_ref[r, cols] = g.astype(BF)
            x += dot_nn(z, narrow_tile(w1b, j))
        x_out[r, :] = x

    loop(images * PAD // size, block, ticks)


def dense_backward(images, b_ref, x_in, gain, wid, w1b, hn_ref, z_ref, g_ref, da_ref, dgain_ref, dwid, ticks=()):
    size = row_block(images)
    dgain_ref[...] = jnp.zeros_like(dgain_ref)

    def block(i):
        r = rows_of(i, size)
        b = b_ref[r, :]
        da = b.astype(BF)
        da_ref[r, pl.ds(0, D)] = da
        dhn = jnp.zeros((size, D), F32)
        for j in range(4):
            cols = pl.ds(D * j, D)
            du = (dot_nt(da, narrow_tile(w1b, j)) * g_ref[r, cols].astype(F32)).astype(BF)
            g_ref[r, cols] = du
            dhn += dot_nt(du, wid[:, cols])
        dx, dg = norm_back(x_in[r, :], gain, dhn)
        b_ref[r, :] = b + dx
        dgain_ref[...] += dg

    loop(images * PAD // size, block, ticks)
    hn, da = hn_ref[...], da_ref[:, pl.ds(0, D)]

    def tile(j):
        cols = pl.ds(pl.multiple_of(D * j, LANES), D)
        dwid[:, cols] = dot_tn(hn, g_ref[:, cols]).astype(BF)
        w1b[j, :, :, :, 96:144, :] = dot_tn(z_ref[:, cols], da).astype(BF).reshape(2, 2, 2, 48, D)

    loop(4, tile)


def router_forward(images, x_in, x_out, gain, router, routes_ref, hn_ref, table_ref):
    lane = lax.broadcasted_iota(jnp.int32, (SEQ, LANES), 1) - EXPERTS
    low_lane = lax.broadcasted_iota(jnp.int32, (PAD, LANES), 1) < EXPERTS

    def image(i):
        r = rows_of(i)
        x = x_in[r, :]
        hn = (normed(x)[0] * gain).astype(BF)
        hn_ref[r, :] = hn
        x_out[r, :] = x
        logits = jnp.where(low_lane, dot_nt(hn, router), -1e30)
        w = jnp.exp(logits - jnp.max(logits, axis=-1, keepdims=True))
        probs = w * (1.0 / jnp.sum(w, axis=-1, keepdims=True))
        table_ref[r, :] = probs
        named = routes_ref[i]
        hot = (lane == named[:, 0:1]) | (lane == named[:, 1:2])
        table_ref[pl.ds(pl.multiple_of(i * PAD, 16), SEQ), :] = jnp.where(hot, 1.0, probs[:SEQ])

    loop(images, image)


def expert_step(
    images, e, x_out, b_ref, dhn_ref, uw, vw, hn_ref, table_ref, z_ref, g_ref, dy_ref, ticks=(), late=(), before=None
):
    size = row_block(images)
    lane = lax.broadcasted_iota(jnp.int32, (size, LANES), 1)

    def u_tile(j):
        return uw[e, :, :, :, :, pl.ds(D * j, D)].reshape(D, D)

    def v_tile(j):
        return vw[e, j // 2, j % 2].reshape(D, D)

    def block(i):
        r = rows_of(i, size)
        hn = hn_ref[r, :]
        y = jnp.zeros((size, D), F32)
        for j in range(4):
            cols = pl.ds(D * j, D)
            z, g = gelu_both(dot_nn(hn, u_tile(j)))
            z = z.astype(BF)
            z_ref[r, cols] = z
            g_ref[r, cols] = g.astype(BF)
            y += dot_nn(z, v_tile(j))
        table = table_ref[r, :]
        hot = jnp.sum(jnp.where(lane == e + EXPERTS, table, 0.0), axis=-1, keepdims=True)
        gate = hot * jnp.sum(jnp.where(lane == e, table, 0.0), axis=-1, keepdims=True)
        b = b_ref[r, :]
        x_out[r, :] += gate * y
        dgate = hot * jnp.sum(b * y, axis=-1, keepdims=True)
        table_ref[r, :] = jnp.where(lane == e + 2 * EXPERTS, dgate, table)
        dy = (gate * b).astype(BF)
        dy_ref[r, :] = dy
        dhn = dhn_ref[r, :]
        for j in range(4):
            cols = pl.ds(D * j, D)
            du = (dot_nt(dy, v_tile(j)) * g_ref[r, cols].astype(F32)).astype(BF)
            g_ref[r, cols] = du
            dhn += dot_nt(du, u_tile(j))
        dhn_ref[r, :] = dhn

    loop(images * PAD // size, block, ticks)
    if before is not None:
        before()
    hn, dy = hn_ref[...], dy_ref[...]

    def tile(j):
        cols = pl.ds(pl.multiple_of(D * j, LANES), D)
        uw[e, :, :, :, :, cols] = dot_tn(hn, g_ref[:, cols]).astype(BF).reshape(2, 2, 2, 48, D)
        vw[e, j // 2, j % 2] = dot_tn(z_ref[:, cols], dy).astype(BF).reshape(2, 192, D)

    loop(4, tile, late)


def router_backward(images, b_ref, x_in, gain, router, dhn_ref, table_ref, hn_ref, drouter_ref, dgain_ref, ticks=()):
    dgain_ref[...] = jnp.zeros_like(dgain_ref)
    drouter_ref[...] = jnp.zeros_like(drouter_ref)
    low_lane = lax.broadcasted_iota(jnp.int32, (PAD, LANES), 1) < EXPERTS

    def image(i):
        r = rows_of(i)
        table = table_ref[r, :]
        probs = jnp.where(low_lane, table, 0.0)
        dprobs = pltpu.roll(table, LANES - 2 * EXPERTS, 1)
        dlogits = (probs * (dprobs - jnp.sum(dprobs * probs, axis=-1, keepdims=True))).astype(BF)
        drouter_ref[...] += dot_tn(dlogits, hn_ref[r, :])
        dhn = dhn_ref[r, :] + dot_nn(dlogits, router)
        dx, dg = norm_back(x_in[r, :], gain, dhn)
        b_ref[r, :] += dx
        dgain_ref[...] += dg

    loop(images, image, ticks)


def chunk_spots(matrices):
    return [(m, c) for m in matrices for c in range(m.shape[1] // D)]


def decode(buf, row, perm_t, matrices):
    spots = chunk_spots(matrices)

    def group(g):
        full = dot_nn(perm_t, piece_rows(buf, g, row)).astype(BF)
        r = rows_of(g, 96)
        for k, (m, c) in enumerate(spots):
            m[r, pl.ds(D * c, D)] = full[96 * k : 96 * (k + 1)]

    loop(4, group)


def encode(buf, row, perm, matrices):
    spots = chunk_spots(matrices)

    def group(g):
        r = rows_of(g, 96)
        parts = jnp.concatenate([m[r, pl.ds(D * c, D)] for m, c in spots], axis=0)
        buf[g, :, :, :, row : row + 48, :] = dot_nn(perm, parts).astype(BF).reshape(2, 2, 2, 48, D)

    loop(4, group)


def decode_small(w1a, gains_ref, router_ref):
    block = w1a[:, :, :, :, 48:64, :].reshape(-1, D)
    spot = lax.broadcasted_iota(jnp.int32, (8, block.shape[0]), 1)
    row = lax.broadcasted_iota(jnp.int32, (8, block.shape[0]), 0)
    pick = (spot % 16 == 0) & (spot // 128 == row)
    gains_ref[...] = dot_nn(jnp.where(pick, 1.0, 0.0).astype(BF), block)
    spot = lax.broadcasted_iota(jnp.int32, (LANES, block.shape[0]), 1)
    row = lax.broadcasted_iota(jnp.int32, (LANES, block.shape[0]), 0)
    pick = (spot % 16 == row + 1) & (row < EXPERTS)
    router_ref[...] = dot_nn(jnp.where(pick, 1.0, 0.0).astype(BF), block).astype(BF)


def encode_small(w1a, gs_ref):
    rest = jnp.zeros((16 - 1 - EXPERTS, D), F32)
    for g in range(4):
        block = jnp.concatenate([gs_ref[pl.ds(g, 1), :], gs_ref[pl.ds(4, EXPERTS), :], rest], axis=0).astype(BF)
        for d in range(8):
            w1a[g, d // 4, d // 2 % 2, d % 2, 48:64, :] = block


def permutation():
    spots = np.arange(D)
    c, d, r = spots // 48, spots // 12 % 4, spots % 12
    table = np.zeros((D, D), np.float32)
    table[spots, d * 96 + c * 12 + r] = 1.0
    return table


class Copy:
    def __init__(self, net, k, ends, mask):
        self.net, self.k, self.ends, self.mask = net, k, ends, mask

    def make(self):
        src, dst = self.ends()
        return pltpu.make_async_remote_copy(
            src_ref=src, dst_ref=dst, send_sem=self.net.send_sem.at[self.k], recv_sem=self.net.recv_sem.at[self.k],
            device_id=(self.net.partner(self.mask),), device_id_type=MESH)

    def start(self):
        self.make().start()

    def wait_recv(self):
        self.make().wait_recv()

    def wait_send(self):
        self.make().wait_send()


class Net:
    masks = (1, 2, 4, 8, 16, 24)

    def __init__(self, send_sem, recv_sem):
        self.send_sem, self.recv_sem, self.count = send_sem, recv_sem, 0
        me = lax.axis_index("fsdp")
        self.c, self.x, self.y, self.z = me % 2, me // 2 % 2, me // 4 % 2, me // 8
        self.zs = [self.flip_z(d) for d in range(4)]
        self.partners = {m: self.partner_of(m) for m in self.masks}

    def partner(self, mask):
        return self.partners[mask]

    def partner_of(self, mask):
        c = 1 - self.c if mask & 1 else self.c
        x = 1 - self.x if mask & 2 else self.x
        y = 1 - self.y if mask & 4 else self.y
        return self.zs[mask >> 3] * 8 + y * 4 + x * 2 + c

    def flip_z(self, d):
        lo, hi = self.z % 2, self.z // 2
        lo = 1 - lo if d & 1 else lo
        hi = 1 - hi if d & 2 else hi
        return hi * 2 + lo

    def barrier(self):
        sem = pltpu.get_barrier_semaphore()
        for m in self.masks:
            pl.semaphore_signal(sem, inc=1, device_id=(self.partner(m),), device_id_type=MESH)
        pl.semaphore_wait(sem, len(self.masks))

    def copy(self, ends, mask):
        k = self.count
        self.count += 1
        return Copy(self, k, ends, mask)


def halves(rows, w):
    if w == D:
        cut = (rows // 32 + 1) * 16 if rows % 32 else rows // 2
        return (pl.ds(0, cut), pl.ds(0, w)), (pl.ds(cut, rows - cut), pl.ds(0, w))
    return (pl.ds(0, rows), pl.ds(0, w // 2)), (pl.ds(0, rows), pl.ds(w // 2, w // 2))


class Gather:
    def __init__(self, net, buf):
        x, y, c = net.x, net.y, net.c
        a, b = halves(*buf.shape[-2:])

        def copy(d, yy, xx, half, mask):
            def ends():
                ref = buf.at[net.zs[d], yy, xx, c]
                ref = ref if half is None else ref.at[half[0], half[1]]
                return ref, ref

            return net.copy(ends, mask)

        def pair(d):
            def ends():
                ref = buf.at[net.zs[d], :, :, c]
                return ref, ref

            return net.copy(ends, 1)

        slots = range(4)
        self.along_z = [None] + [copy(0, y, x, None, d << 3) for d in (1, 2, 3)]
        self.to_y = [copy(d, y, x, a, 4) for d in slots]
        self.to_x = [copy(d, y, x, b, 2) for d in slots]
        self.own_x = [copy(d, y, x, a, 2) for d in slots]
        self.own_y = [copy(d, y, x, b, 4) for d in slots]
        self.far_x = [copy(d, 1 - y, x, a, 2) for d in slots]
        self.far_y = [copy(d, y, 1 - x, b, 4) for d in slots]
        self.pair = [pair(d) for d in slots]

    def send_z(self, d):
        self.along_z[d].start()

    def plane(self, d):
        if d:
            self.along_z[d].wait_recv()
        self.to_y[d].start()
        self.to_x[d].start()
        self.own_x[d].start()
        self.own_y[d].start()

    def across(self, d):
        self.to_y[d].wait_recv()
        self.far_x[d].start()
        self.to_x[d].wait_recv()
        self.far_y[d].start()

    def core(self, d):
        for copy in (self.own_x, self.own_y, self.far_x, self.far_y):
            copy[d].wait_recv()
        self.pair[d].start()

    def here(self, d):
        self.pair[d].wait_recv()

    def sent(self, d):
        for copy in (self.to_y, self.to_x, self.own_x, self.own_y, self.far_x, self.far_y, self.pair):
            copy[d].wait_send()
        if d == 0:
            for k in (1, 2, 3):
                self.along_z[k].wait_send()


class Reduce:
    def __init__(self, net, part, slots, bufs, r4):
        self.net, self.part, self.slots, self.r4 = net, part, slots, r4
        self.recv1, self.r2a, self.r2b, self.r3a, self.r3b = bufs
        x, y, c = net.x, net.y, net.c
        self.a, self.b = halves(*part.shape[-2:])
        planes = pl.ds(0, 4) if len(slots) == 4 else pl.ds(net.zs[slots[0]], 1)
        self.planes = range(4) if len(slots) == 4 else [net.zs[slots[0]]]
        a, b = self.a, self.b

        def one(yy, xx):
            return net.copy(lambda: (part.at[planes, yy, xx, 1 - c], self.recv1.at[:, yy, xx]), 1)

        self.s1 = {(fy, fx): one(1 - y if fy else y, 1 - x if fx else x) for fx in (1, 0) for fy in (1, 0)}

        def two_a(yy):
            return net.copy(lambda: (part.at[planes, yy, 1 - x, c, a[0], a[1]], self.r2a.at[:, yy]), 2)

        def two_b(xx):
            return net.copy(lambda: (part.at[planes, 1 - y, xx, c, b[0], b[1]], self.r2b.at[:, xx]), 4)

        self.s2a = [two_a(1 - y), two_a(y)]
        self.s2b = [two_b(1 - x), two_b(x)]
        self.s3a = net.copy(lambda: (part.at[planes, 1 - y, x, c, a[0], a[1]], self.r3a), 4)
        self.s3b = net.copy(lambda: (part.at[planes, y, 1 - x, c, b[0], b[1]], self.r3b), 2)

        def four(d):
            return net.copy(lambda: (part.at[net.zs[d], y, x, c], r4.at[d - 1]), d << 3)

        self.s4 = {d: four(d) for d in slots if d}

    def add(self, ref, other):
        ref[...] = (ref[...].astype(F32) + other[...].astype(F32)).astype(BF)

    def one(self):
        for copy in self.s1.values():
            copy.start()

    def two(self):
        net = self.net
        x, y, c = net.x, net.y, net.c

        def add_all(fy, fx):
            self.s1[fy, fx].wait_recv()
            yy, xx = (1 - y if fy else y), (1 - x if fx else x)
            for k, z in enumerate(self.planes):
                self.add(self.part.at[z, yy, xx, c], self.recv1.at[k, yy, xx])

        add_all(1, 1)
        self.s2a[0].start()
        self.s2b[0].start()
        add_all(0, 1)
        self.s2a[1].start()
        add_all(1, 0)
        self.s2b[1].start()
        add_all(0, 0)

    def three(self):
        net = self.net
        x, y, c = net.x, net.y, net.c
        a, b = self.a, self.b

        def add_half(yy, xx, half, buf, spot):
            for k, z in enumerate(self.planes):
                self.add(self.part.at[z, yy, xx, c, half[0], half[1]], buf.at[k, spot])

        self.s2a[0].wait_recv()
        add_half(1 - y, x, a, self.r2a, 1 - y)
        self.s3a.start()
        self.s2b[0].wait_recv()
        add_half(y, 1 - x, b, self.r2b, 1 - x)
        self.s3b.start()
        self.s2a[1].wait_recv()
        add_half(y, x, a, self.r2a, y)
        self.s2b[1].wait_recv()
        add_half(y, x, b, self.r2b, x)

    def four(self):
        net = self.net
        x, y, c = net.x, net.y, net.c
        for copy, half, buf in ((self.s3a, self.a, self.r3a), (self.s3b, self.b, self.r3b)):
            copy.wait_recv()
            for k, z in enumerate(self.planes):
                self.add(self.part.at[z, y, x, c, half[0], half[1]], buf.at[k])
        for copy in self.s4.values():
            copy.start()

    def sent(self):
        for copy in [*self.s1.values(), *self.s2a, *self.s2b, self.s3a, self.s3b, *self.s4.values()]:
            copy.wait_send()


def finish(net, part, reduces, r4, out):
    total = part[net.z, net.y, net.x, net.c].astype(F32)
    for job in reduces:
        for d, copy in job.s4.items():
            copy.wait_recv()
            total += r4[d - 1].astype(F32)
    out[...] = total


def reduce_buffers(rows, w, planes):
    a, b = halves(rows, w)
    sa, sb = (a[0].size, a[1].size), (b[0].size, b[1].size)
    shapes = [(planes, 2, 2, rows, w), (planes, 2) + sa, (planes, 2) + sb, (planes,) + sa, (planes,) + sb]
    return [pltpu.VMEM(s, BF) for s in shapes]


def block_kernel(remote, names, *refs):
    r = dict(zip(names, refs))
    images = r["tok"].shape[0] // PAD
    w1a, w1b, uw, vw = arrays = [r[k] for k in ("w1a", "w1b", "uw", "vw")]
    sem = r["sem"]
    cot_load = pltpu.make_async_copy(r["cot"], r["dy"], sem.at[4])
    cot_load.start()

    if remote:
        net = Net(r["send_sem"], r["recv_sem"])
        loads = [
            pltpu.make_async_copy(r[k + "_in"], buf.at[net.z, net.y, net.x, net.c], sem.at[j])
            for j, (k, buf) in enumerate(zip(("w1a", "w1b", "uw", "vw"), arrays))
        ]
        for copy in loads:
            copy.start()
        net.barrier()
        ga, gb, gu, gv = gathers = [Gather(net, buf) for buf in arrays]
        experts = [net.zs[d] for d in range(4)]
        loads[0].wait()
        for d in (1, 2, 3):
            ga.send_z(d)
        ga.plane(0)
        loads[1].wait()
        for d in (1, 2, 3):
            gb.send_z(d)
        loads[2].wait()
        loads[3].wait()
    else:
        loads = [
            pltpu.make_async_copy(r[k + "_in"], buf, sem.at[j])
            for j, (k, buf) in enumerate(zip(("w1a", "w1b", "uw", "vw"), arrays))
        ]
        for copy in loads:
            copy.start()
        experts = range(4)
    x0, x1, x2, x3, x4, b, dhn = (r[k] for k in ("tok", "x1", "x2", "x3", "x4", "b", "dhn"))
    valid, cot = r["valid"], r["dy"]
    cot_load.wait()
    for i in range(images):
        rows = pl.ds(PAD * i, PAD)
        b[rows, :] = cot[rows, :].astype(F32) * valid[i].astype(F32)
    dhn[...] = jnp.zeros_like(dhn)
    table = r["table"]
    perm, perm_t = r["perm"], r["perm_t"]
    win1, wout1, wid1, win2, wout2 = (r[k] for k in ("win1", "wout1", "wid1", "win2", "wout2"))

    def none():
        return None

    def batch(*steps):
        def tick():
            for step in steps:
                step()

        return tick if remote else none

    if remote:
        ga.across(0)
        for d in (1, 2, 3):
            ga.plane(d)
        gb.plane(0)
        for d in (1, 2, 3):
            ga.across(d)
        ga.core(0)
        gb.across(0)
        for d in (1, 2, 3):
            gb.plane(d)
        for d in (1, 2, 3):
            ga.core(d)
        for d in range(4):
            for g in (gu, gv):
                if d:
                    g.send_z(d)
        for d in range(4):
            ga.here(d)
    else:
        loads[0].wait()

    def both(step, d):
        return batch(lambda: getattr(gu, step)(d), lambda: getattr(gv, step)(d))

    decode(w1a, 0, perm_t[...], (win1, wout1))
    decode_small(w1a, r["gains"], r["router"])
    gains = [r["gains"][pl.ds(k, 1), :] for k in range(4)]
    router = r["router"][...]
    ticks = [
        batch(lambda: gb.across(1), lambda: gb.across(2)),
        batch(lambda: gb.across(3), lambda: gb.core(0), lambda: gb.core(1), both("plane", 0)),
        batch(lambda: gb.core(2), lambda: gb.core(3), both("across", 0)),
        batch(both("plane", 1)),
    ]
    attention_forward(images, x0, x1, gains[0], win1, wout1, r["hn1"], r["qkv1"], r["pb1"], r["o1"], ticks)
    if remote:
        for d in range(4):
            gb.here(d)
    else:
        loads[1].wait()
    decode(w1b, 48, perm_t[...], (wid1,))
    decode(w1b, 0, perm_t[...], (win2, wout2))
    ticks = [batch(both("across", 1), both("core", 0)), batch(both("plane", 2))]
    dense_forward(images, x1, x2, gains[1], wid1, w1b, r["hn2"], r["z1"], r["g1"], ticks)
    ticks = [batch(both("across", 2)), batch(both("core", 1)), batch(both("plane", 3)), batch(both("across", 3))]
    attention_forward(images, x2, x3, gains[2], win2, wout2, r["hn3"], r["qkv2"], r["pb2"], r["o2"], ticks)
    router_forward(images, x3, x4, gains[3], router, r["routes"], r["hn4"], table)

    if remote:
        buffers = iter(r["rs"])
        take = lambda: [next(buffers) for _ in range(5)]
        bufs_u, bufs_v = [take(), take()], [take(), take()]
        ru = [Reduce(net, uw, [d], bufs_u[d % 2], r["r4u"]) for d in range(4)]
        rv = [Reduce(net, vw, [d], bufs_v[d % 2], r["r4v"]) for d in range(4)]
        rb = Reduce(net, w1b, [0, 1, 2, 3], take(), r["r4b"])
        ra = Reduce(net, w1a, [0, 1, 2, 3], take(), r["r4a"])
    else:
        loads[2].wait()
        loads[3].wait()

    def reduce_step(step, d):
        return batch(lambda: getattr(ru[d], step)(), lambda: getattr(rv[d], step)())

    def run_expert(d, ticks, late):
        if remote:
            gu.here(d)
            gv.here(d)
        before = batch(lambda: gu.sent(d), lambda: gv.sent(d))
        expert_step(
            images, experts[d], x4, b, dhn, uw, vw, r["hn4"], table, r["ze"], r["ge"], r["dy"], ticks, late, before
        )
        reduce_step("one", d)()

    run_expert(0, [both("core", 2), both("core", 3)], [])
    run_expert(1, [reduce_step("two", 0), reduce_step("three", 0)], [reduce_step("four", 0)])
    run_expert(2, [reduce_step("two", 1), reduce_step("three", 1)], [reduce_step("four", 1)])
    run_expert(3, [reduce_step("two", 2), reduce_step("three", 2)], [reduce_step("four", 2)])
    gs, dgain, drouter = r["gs"], r["dgain"], r["drouter"]
    gs[...] = jnp.zeros_like(gs)
    router_backward(images, b, x3, gains[3], router, dhn, table, r["hn4"], drouter, dgain)
    for i in range(images):
        rows = pl.ds(PAD * i, PAD)
        r["hn4"][rows, :] = (x4[rows, :] * valid[i].astype(F32)).astype(BF)
    out_store = pltpu.make_async_copy(r["hn4"], r["out"], sem.at[5])
    out_store.start()
    gs[pl.ds(4, EXPERTS), :] = drouter[pl.ds(0, EXPERTS), :]
    gs[pl.ds(3, 1), :] = dgain[...]
    dqkv, da = r["ze"], r["dy"]
    ticks = [reduce_step("two", 3), none, reduce_step("three", 3)]
    attention_backward(images, b, x2, gains[2], win2, wout2, r["hn3"], r["qkv2"], r["pb2"], r["o2"], da, dqkv, dgain, win2, wout2, ticks)
    gs[pl.ds(2, 1), :] = dgain[...]
    batch(*(lambda d=d: gb.sent(d) for d in range(4)))()
    encode(w1b, 0, perm[...], (win2, wout2))
    ticks = [reduce_step("four", 3)]
    dense_backward(images, b, x1, gains[1], wid1, w1b, r["hn2"], r["z1"], r["g1"], da, dgain, wid1, ticks)
    gs[pl.ds(1, 1), :] = dgain[...]
    encode(w1b, 48, perm[...], (wid1,))
    if remote:
        rb.one()
    ticks = [batch(lambda: rb.two()), none, batch(lambda: rb.three()), batch(lambda: rb.four())]
    attention_backward(images, b, x0, gains[0], win1, wout1, r["hn1"], r["qkv1"], r["pb1"], r["o1"], da, dqkv, dgain, win1, wout1, ticks)
    gs[pl.ds(0, 1), :] = dgain[...]
    batch(*(lambda d=d: ga.sent(d) for d in range(4)))()
    encode(w1a, 0, perm[...], (win1, wout1))
    encode_small(w1a, gs)
    if remote:
        ra.one()
    r["o1"][...] = b[...].astype(BF)
    delta_store = pltpu.make_async_copy(r["o1"], r["dtok"], sem.at[6])
    delta_store.start()
    if remote:
        finish(net, uw, ru, r["r4u"], r["uw_out"])
        finish(net, vw, rv, r["r4v"], r["vw_out"])
        ra.two()
        finish(net, w1b, [rb], r["r4b"], r["w1b_out"])
        ra.three()
        ra.four()
        finish(net, w1a, [ra], r["r4a"], r["w1a_out"])
        for job in (*ru, *rv, rb, ra):
            job.sent()
    else:
        stores = [
            pltpu.make_async_copy(buf, r[k + "_out"], sem.at[j])
            for j, (k, buf) in enumerate(zip(("w1a", "w1b", "uw", "vw"), arrays))
        ]
        for copy in stores:
            copy.start()
        for copy in stores:
            copy.wait()
    out_store.wait()
    delta_store.wait()


def run_blocks(remote, tok, cot, valid, routes, w1a, w1b, uw, vw):
    t = tok.shape[0]
    images = t // PAD
    v = pltpu.VMEM
    vmem, smem, hbm = (pl.BlockSpec(memory_space=m) for m in (pltpu.VMEM, pltpu.SMEM, pl.ANY))
    table = permutation()
    pieces = [w.shape[-2:] for w in (w1a, w1b, uw, vw)]
    whole = [(4, 2, 2, 2) + s for s in pieces]
    inputs = dict(
        tok=(tok, vmem), cot=(cot, hbm), valid=(valid, smem), routes=(routes, vmem),
        perm=(jnp.asarray(table, BF), vmem), perm_t=(jnp.asarray(table.T, BF), vmem),
        w1a_in=(w1a, hbm), w1b_in=(w1b, hbm), uw_in=(uw, hbm), vw_in=(vw, hbm),
    )
    flat = jax.ShapeDtypeStruct(tok.shape, BF)
    outputs = dict(out=(flat, hbm), dtok=(flat, hbm))
    for name, piece, full in zip(("w1a", "w1b", "uw", "vw"), pieces, whole):
        outputs[name + "_out"] = (jax.ShapeDtypeStruct(piece, F32), vmem) if remote else (jax.ShapeDtypeStruct(full, BF), hbm)
    scratch = dict(
        w1a=v(whole[0], BF), w1b=v(whole[1], BF), uw=v(whole[2], BF), vw=v(whole[3], BF),
        win1=v((D, 3 * D), BF), wout1=v((D, D), BF), wid1=v((D, FF), BF), win2=v((D, 3 * D), BF), wout2=v((D, D), BF),
        x1=v((t, D), F32), x2=v((t, D), F32), x3=v((t, D), F32), x4=v((t, D), F32), b=v((t, D), F32), dhn=v((t, D), F32),
        hn1=v((t, D), BF), hn2=v((t, D), BF), hn3=v((t, D), BF), hn4=v((t, D), BF),
        qkv1=v((t, 3 * D), BF), qkv2=v((t, 3 * D), BF), o1=v((t, D), BF), o2=v((t, D), BF),
        pb1=v((images * PAIRS, 2 * PAD, PAD), BF), pb2=v((images * PAIRS, 2 * PAD, PAD), BF),
        z1=v((t, FF), BF), g1=v((t, FF), BF), ze=v((t, FF), BF), ge=v((t, FF), BF), dy=v((t, D), BF),
        table=v((t, LANES), F32),
        drouter=v((LANES, D), F32), dgain=v((1, D), F32), gs=v((16, D), F32), gains=v((8, D), F32), router=v((LANES, D), BF),
        sem=pltpu.SemaphoreType.DMA((7,)),
    )
    if remote:
        scratch["rs"] = [
            spec
            for piece, planes in [(pieces[2], 1)] * 2 + [(pieces[3], 1)] * 2 + [(pieces[1], 4), (pieces[0], 4)]
            for spec in reduce_buffers(*piece, planes)
        ]
        for k, piece in zip("abuv", pieces):
            scratch["r4" + k] = v((3,) + piece, BF)
        scratch["send_sem"] = pltpu.SemaphoreType.DMA((256,))
        scratch["recv_sem"] = pltpu.SemaphoreType.DMA((256,))
    names = (*inputs, *outputs, *scratch)
    params = dict(collective_id=0, has_side_effects=True) if remote else {}
    return pl.pallas_call(
        functools.partial(block_kernel, remote, names),
        out_shape=tuple(o[0] for o in outputs.values()),
        in_specs=[i[1] for i in inputs.values()],
        out_specs=tuple(o[1] for o in outputs.values()),
        scratch_shapes=list(scratch.values()),
        compiler_params=pltpu.CompilerParams(vmem_limit_bytes=63 * 2**20, **params),
    )(*[i[0] for i in inputs.values()])


def chunked(matrices, rows):
    side = jnp.concatenate([m.reshape(rows, -1) for m in matrices], axis=1)
    return side.reshape(rows, -1, D).transpose(1, 0, 2).reshape(-1, D)


def unchunked(piece):
    return piece.reshape(-1, ROWS, D).transpose(1, 0, 2).reshape(ROWS, -1)


def my_pieces(me, norm_gains, in_one, out_one, widen, narrow, router, in_two, out_two, experts_widen, experts_narrow):
    share = norm_gains.shape[0]
    gain_row = lax.dynamic_update_slice(jnp.zeros((1, D), BF), norm_gains[None, :], (0, me % (D // share) * share))
    router_rows = lax.dynamic_update_slice(jnp.zeros((EXPERTS, D), BF), router.reshape(ROWS, EXPERTS).T, (0, me * ROWS))
    rest = jnp.zeros((16 - 1 - EXPERTS, D), BF)
    return (
        jnp.concatenate([chunked((in_one, out_one), ROWS), gain_row, router_rows, rest], axis=0),
        jnp.concatenate([chunked((in_two, out_two), ROWS), chunked((widen,), ROWS), narrow.reshape(-1, D)], axis=0),
        experts_widen.reshape(-1, FF),
        experts_narrow.reshape(-1, D),
    )


def my_deltas(me, w1a, w1b, uw, vw):
    one, two = unchunked(w1a[0:48]), unchunked(w1b[0:48])
    share = 4 * D // SHARDS
    gains = lax.dynamic_slice(w1a[48], (me % (D // share) * share,), (share,))
    router = lax.dynamic_slice(w1a[49:53], (0, me * ROWS), (EXPERTS, ROWS)).T
    parts = (
        gains, one[:, : 3 * D], one[:, 3 * D :], unchunked(w1b[48:96]), w1b[96:144], router, two[:, : 3 * D], two[:, 3 * D :], uw, vw
    )
    return tuple(p.reshape(-1) for p in parts)


def all_pieces(norm_gains, in_one, out_one, widen, narrow, router, in_two, out_two, experts_widen, experts_narrow):
    def cut(*matrices):
        side = jnp.concatenate([m.reshape(D, -1) for m in matrices], axis=1)
        return side.reshape(SHARDS, ROWS, -1, D).transpose(0, 2, 1, 3).reshape(SHARDS, -1, D)

    small = jnp.zeros((SHARDS, 16, D), BF)
    small = small.at[:: SHARDS // 4, 0].set(norm_gains.reshape(4, D))
    small = small.at[0, 1 : 1 + EXPERTS].set(router.reshape(D, EXPERTS).T)
    parts = (
        jnp.concatenate([cut(in_one, out_one), small], axis=1),
        jnp.concatenate([cut(in_two, out_two), cut(widen), narrow.reshape(SHARDS, -1, D)], axis=1),
        experts_widen.reshape(SHARDS, -1, FF),
        experts_narrow.reshape(SHARDS, -1, D),
    )
    return [p.reshape((4, 2, 2, 2) + p.shape[1:]) for p in parts]


def all_deltas(*parts):
    w1a, w1b, uw, vw = (p.astype(F32).reshape((SHARDS,) + p.shape[-2:]) for p in parts)

    def join(part):
        return part.reshape(SHARDS, -1, ROWS, D).transpose(0, 2, 1, 3).reshape(D, -1)

    one, two = join(w1a[:, 0:48]), join(w1b[:, 0:48])
    whole = (
        w1a[:: SHARDS // 4, 48], one[:, : 3 * D], one[:, 3 * D :], join(w1b[:, 48:96]), w1b[:, 96:144], w1a[0, 49:53].T,
        two[:, : 3 * D], two[:, 3 * D :], uw, vw,
    )
    return [p.reshape(-1) for p in whole]


def on_device(shards, tokens, cotangent, image_valid, routes, *weights):
    images = tokens.shape[0] * tokens.shape[1]

    def padded(array):
        return jnp.pad(array.reshape(images, SEQ, D), ((0, 0), (0, PAD - SEQ), (0, 0))).reshape(images * PAD, D)

    def cut(array):
        return array.reshape(images, PAD, D)[:, :SEQ].reshape(tokens.shape)

    data = (padded(tokens), padded(cotangent), image_valid.reshape(images), routes.reshape(images, SEQ, 2))
    if shards == SHARDS:
        me = lax.axis_index("fsdp")
        out, delta, *sums = run_blocks(True, *data, *my_pieces(me, *weights))
        deltas = my_deltas(me, *sums)
    else:
        whole = [lax.all_gather(w, "fsdp", axis=0, tiled=True) for w in weights]
        out, delta, *sums = run_blocks(False, *data, *all_pieces(*whole))
        deltas = [lax.psum_scatter(d, "fsdp", scatter_dimension=0, tiled=True) for d in all_deltas(*sums)]
    return (cut(out), cut(delta), *deltas)


def solution(mesh):
    split, flat = P(None, "fsdp", None, None), P("fsdp")
    return jax.shard_map(
        functools.partial(on_device, mesh.shape["fsdp"]),
        mesh=mesh,
        in_specs=(split, split, P(None, "fsdp"), split) + (flat,) * 10,
        out_specs=(split, split) + (flat,) * 10,
        check_vma=False,
    )
```

```python
import functools
import math

import jax
import jax.numpy as jnp
import numpy as np
from jax import lax
from jax.experimental import pallas as pl
from jax.experimental.pallas import tpu as pltpu
from jax.sharding import PartitionSpec as P

D = 384
HEADS = 6
HDIM = 64
FF = 1536
EXPERTS = 4
SEQ = 197
PAD = 208
PAIRS = HEADS // 2
SHARDS = 32
ROWS = D // SHARDS
LANES = 128
EPSILON = 1e-06
BF = jnp.bfloat16
F32 = jnp.float32
MESH = pl.DeviceIdType.MESH
C0 = math.sqrt(2.0 / math.pi)
C1 = 0.044715


def dot_nn(a, b):
    return lax.dot_general(a, b, (((1,), (0,)), ((), ())), preferred_element_type=F32)


def dot_nt(a, b):
    return lax.dot_general(a, b, (((1,), (1,)), ((), ())), preferred_element_type=F32)


def dot_tn(a, b):
    return lax.dot_general(a, b, (((0,), (0,)), ((), ())), preferred_element_type=F32)


def normed(x):
    centred = x - jnp.mean(x, axis=-1, keepdims=True)
    rstd = lax.rsqrt(jnp.mean(centred * centred, axis=-1, keepdims=True) + EPSILON)
    return centred * rstd, rstd


def norm_back(x, gain, dhn):
    xhat, rstd = normed(x)
    dxhat = dhn * gain
    mean_d = jnp.mean(dxhat, axis=-1, keepdims=True)
    mean_dx = jnp.mean(dxhat * xhat, axis=-1, keepdims=True)
    return rstd * (dxhat - mean_d - xhat * mean_dx), jnp.sum(dhn * xhat, axis=0, keepdims=True)


def gelu_both(u):
    u2 = u * u
    t = jnp.tanh(u * (C0 + (C0 * C1) * u2))
    h = 0.5 + 0.5 * t
    z = u * h
    return z, h + z * (1.0 - h) * (2.0 * C0 + (6.0 * C0 * C1) * u2)


def rows_of(i, size=PAD):
    return pl.ds(pl.multiple_of(i * size, 16), size)


def loop(count, body, ticks=()):
    def step(i, carry):
        body(i)
        for k, tick in enumerate(ticks):
            pl.when(i == k)(tick)
        return carry

    lax.fori_loop(0, count, step, 0)


def attention_forward(images, x_in, x_out, gain, win, wout, hn_ref, qkv_ref, pb_ref, o_ref, ticks=()):
    low_half = lax.broadcasted_iota(jnp.int32, (PAD, LANES), 1) < HDIM
    real_key = lax.broadcasted_iota(jnp.int32, (2 * PAD, PAD), 1) < SEQ

    def image(i):
        r = rows_of(i)
        x = x_in[r, :].astype(F32)
        xhat, _ = normed(x)
        hn = (xhat * gain).astype(BF)
        hn_ref[r, :] = hn
        for j in range(3):
            cols = pl.ds(D * j, D)
            qkv_ref[r, cols] = dot_nn(hn, win[:, cols]).astype(BF)
        for p in range(PAIRS):
            q2 = qkv_ref[r, pl.ds(LANES * p, LANES)]
            k2 = qkv_ref[r, pl.ds(D + LANES * p, LANES)]
            v2 = qkv_ref[r, pl.ds(2 * D + LANES * p, LANES)]
            zero = jnp.zeros_like(q2)
            qs = jnp.concatenate([jnp.where(low_half, q2, zero), jnp.where(low_half, zero, q2)], axis=0)
            s = dot_nt(qs, k2) * HDIM ** (-0.5)
            s = jnp.where(real_key, s, -1e30)
            w = jnp.exp(s - jnp.max(s, axis=-1, keepdims=True))
            soft = w * (1.0 / jnp.sum(w, axis=-1, keepdims=True))
            pb = soft.astype(BF)
            pb_ref[i * PAIRS + p] = pb
            o2 = dot_nn(pb, v2)
            o_ref[r, pl.ds(LANES * p, LANES)] = jnp.where(low_half, o2[:PAD], o2[PAD:]).astype(BF)
        x_out[r, :] = x + dot_nn(o_ref[r, :], wout[...])

    loop(images, image, ticks)


def attention_backward(
    images, b_ref, x_in, gain, win, wout, hn_ref, qkv_ref, pb_ref, o_ref, da_ref, dqkv_ref, dgain_ref, dwin, dwout, ticks=()
):
    low_half = lax.broadcasted_iota(jnp.int32, (PAD, LANES), 1) < HDIM
    dgain_ref[...] = jnp.zeros_like(dgain_ref)

    def image(i):
        r = rows_of(i)
        b = b_ref[r, :]
        da = b.astype(BF)
        da_ref[r, :] = da
        do = dot_nt(da, wout[...]).astype(BF)
        for p in range(PAIRS):
            cols = [pl.ds(D * j + LANES * p, LANES) for j in range(3)]
            q2, k2, v2 = (qkv_ref[r, c] for c in cols)
            do2 = do[:, LANES * p : LANES * (p + 1)]
            zero = jnp.zeros_like(q2)
            qs = jnp.concatenate([jnp.where(low_half, q2, zero), jnp.where(low_half, zero, q2)], axis=0)
            dos = jnp.concatenate([jnp.where(low_half, do2, zero), jnp.where(low_half, zero, do2)], axis=0)
            pb = pb_ref[i * PAIRS + p]
            soft = pb.astype(F32)
            dp = dot_nt(dos, v2)
            ds = (soft * (dp - jnp.sum(dp * soft, axis=-1, keepdims=True))).astype(BF)
            dq = dot_nn(ds, k2) * HDIM ** (-0.5)
            dqkv_ref[r, cols[0]] = jnp.where(low_half, dq[:PAD], dq[PAD:]).astype(BF)
            dqkv_ref[r, cols[1]] = (dot_tn(ds, qs) * HDIM ** (-0.5)).astype(BF)
            dqkv_ref[r, cols[2]] = dot_tn(pb, dos).astype(BF)
        dhn = dot_nt(dqkv_ref[r, pl.ds(0, 3 * D)], win[...])
        dx, dg = norm_back(x_in[r, :].astype(F32), gain, dhn)
        b_ref[r, :] = b + dx
        dgain_ref[...] += dg

    loop(images, image, ticks)
    dwout[...] = dot_tn(o_ref[...], da_ref[...]).astype(BF)
    hn = hn_ref[...]
    for j in range(3):
        cols = pl.ds(D * j, D)
        dwin[:, cols] = dot_tn(hn, dqkv_ref[:, cols]).astype(BF)


def piece_rows(buf, z, row, cols=None):
    block = buf[z, :, :, :, row : row + 48, :]
    return block.reshape(8 * 48, D)


WIDE = 512
HALF = FF // 2


def narrow_half(w1b, h):
    return w1b[2 * h : 2 * h + 2, :, :, :, 96:144, :].reshape(HALF, D)


def gelu_tiles(hn, wide, z_ref, g_ref, r):
    for j in range(FF // WIDE):
        cols = pl.ds(WIDE * j, WIDE)
        z, g = gelu_both(dot_nn(hn, wide(cols)))
        z_ref[r, cols] = z.astype(BF)
        g_ref[r, cols] = g.astype(BF)


def slope_halves(dy, tall, g_ref, r):
    for h in range(2):
        cols = pl.ds(HALF * h, HALF)
        g_ref[r, cols] = (dot_nt(dy, tall(h)) * g_ref[r, cols].astype(F32)).astype(BF)


def tall_delta(dy_t, z_tile):
    return dot_nn(dy_t, z_tile).astype(BF).T


def row_block(images):
    return 2 * PAD if images % 2 == 0 else PAD


def dense_forward(images, x_in, x_out, gain, wid, w1b, hn_ref, z_ref, g_ref, ticks=()):
    size = row_block(images)

    def block(i):
        r = rows_of(i, size)
        x = x_in[r, :]
        hn = (normed(x)[0] * gain).astype(BF)
        hn_ref[r, :] = hn
        gelu_tiles(hn, lambda cols: wid[:, cols], z_ref, g_ref, r)
        tall = w1b[:, :, :, :, 96:144, :].reshape(FF, D)
        x_out[r, :] = x + dot_nn(z_ref[r, :], tall)

    loop(images * PAD // size, block, ticks)


def dense_backward(images, b_ref, x_in, gain, wid, w1b, hn_ref, z_ref, g_ref, da_ref, dgain_ref, dwid, ticks=()):
    size = row_block(images)
    dgain_ref[...] = jnp.zeros_like(dgain_ref)

    def block(i):
        r = rows_of(i, size)
        b = b_ref[r, :]
        da = b.astype(BF)
        da_ref[r, pl.ds(0, D)] = da
        slope_halves(da, lambda h: narrow_half(w1b, h), g_ref, r)
        dhn = dot_nt(g_ref[r, :], wid[...])
        dx, dg = norm_back(x_in[r, :], gain, dhn)
        b_ref[r, :] = b + dx
        dgain_ref[...] += dg

    loop(images * PAD // size, block, ticks)
    hn_t, da_t = hn_ref[...].T, da_ref[...].T
    for j in range(FF // WIDE):
        cols = pl.ds(WIDE * j, WIDE)
        dwid[:, cols] = dot_nn(hn_t, g_ref[:, cols]).astype(BF)
    for h in range(2):
        delta = tall_delta(da_t, z_ref[:, pl.ds(HALF * h, HALF)])
        w1b[2 * h : 2 * h + 2, :, :, :, 96:144, :] = delta.reshape(2, 2, 2, 2, 48, D)


def router_forward(images, x_in, x_out, gain, router, routes_ref, hn_ref, table_ref):
    lane = lax.broadcasted_iota(jnp.int32, (SEQ, LANES), 1) - EXPERTS
    low_lane = lax.broadcasted_iota(jnp.int32, (PAD, LANES), 1) < EXPERTS

    def image(i):
        r = rows_of(i)
        x = x_in[r, :]
        hn = (normed(x)[0] * gain).astype(BF)
        hn_ref[r, :] = hn
        x_out[r, :] = x
        logits = jnp.where(low_lane, dot_nt(hn, router), -1e30)
        w = jnp.exp(logits - jnp.max(logits, axis=-1, keepdims=True))
        probs = w * (1.0 / jnp.sum(w, axis=-1, keepdims=True))
        table_ref[r, :] = probs
        named = routes_ref[i].T
        hot = (lane == named[:SEQ, 0:1]) | (lane == named[:SEQ, 1:2])
        table_ref[pl.ds(pl.multiple_of(i * PAD, 16), SEQ), :] = jnp.where(hot, 1.0, probs[:SEQ])

    loop(images, image)


def expert_step(
    images, e, x_out, cot_ref, dhn_ref, uw, vw, hn_ref, table_ref, z_ref, g_ref, dy_ref, ticks=(), late=(), before=None
):
    size = row_block(images)
    lane = lax.broadcasted_iota(jnp.int32, (size, LANES), 1)

    def u_tile(cols):
        return uw[e, :, :, :, :, cols].reshape(D, -1)

    def v_half(h):
        return vw[e, h].reshape(HALF, D)

    def block(i):
        r = rows_of(i, size)
        hn = hn_ref[r, :]
        gelu_tiles(hn, u_tile, z_ref, g_ref, r)
        y = dot_nn(z_ref[r, :], vw[e].reshape(FF, D))
        table = table_ref[r, :]
        hot = jnp.sum(jnp.where(lane == e + EXPERTS, table, 0.0), axis=-1, keepdims=True)
        gate = hot * jnp.sum(jnp.where(lane == e, table, 0.0), axis=-1, keepdims=True)
        b = cot_ref[r, :].astype(F32)
        x_out[r, :] += gate * y
        dgate = hot * jnp.sum(b * y, axis=-1, keepdims=True)
        table_ref[r, :] = jnp.where(lane == e + 2 * EXPERTS, dgate, table)
        dy = (gate * b).astype(BF)
        dy_ref[r, :] = dy
        slope_halves(dy, v_half, g_ref, r)
        dhn_ref[r, :] += dot_nt(g_ref[r, :], u_tile(pl.ds(0, FF)))

    loop(images * PAD // size, block, ticks)
    if before is not None:
        before()
    hn_t, dy_t = hn_ref[...].T, dy_ref[...].T
    for j in range(FF // WIDE):
        cols = pl.ds(WIDE * j, WIDE)
        uw[e, :, :, :, :, cols] = dot_nn(hn_t, g_ref[:, cols]).astype(BF).reshape(2, 2, 2, 48, WIDE)
    for tick in late:
        tick()
    for h in range(2):
        vw[e, h] = tall_delta(dy_t, z_ref[:, pl.ds(HALF * h, HALF)]).reshape(2, 2, 192, D)


def router_backward(images, b_ref, cot_ref, x_in, gain, router, dhn_ref, table_ref, hn_ref, drouter_ref, dgain_ref, ticks=()):
    dgain_ref[...] = jnp.zeros_like(dgain_ref)
    drouter_ref[...] = jnp.zeros_like(drouter_ref)
    low_lane = lax.broadcasted_iota(jnp.int32, (PAD, LANES), 1) < EXPERTS

    def image(i):
        r = rows_of(i)
        table = table_ref[r, :]
        probs = jnp.where(low_lane, table, 0.0)
        dprobs = pltpu.roll(table, LANES - 2 * EXPERTS, 1)
        dlogits = (probs * (dprobs - jnp.sum(dprobs * probs, axis=-1, keepdims=True))).astype(BF)
        drouter_ref[...] += dot_tn(dlogits, hn_ref[r, :])
        dhn = dhn_ref[r, :] + dot_nn(dlogits, router)
        dx, dg = norm_back(x_in[r, :], gain, dhn)
        b_ref[r, :] = cot_ref[r, :].astype(F32) + dx
        dgain_ref[...] += dg

    loop(images, image, ticks)


def chunk_spots(matrices):
    return [(m, c) for m in matrices for c in range(m.shape[1] // D)]


def decode(buf, row, perm, matrices):
    spots = chunk_spots(matrices)

    def group(g):
        full = dot_tn(perm, piece_rows(buf, g, row)).astype(BF)
        r = rows_of(g, 96)
        for k, (m, c) in enumerate(spots):
            m[r, pl.ds(D * c, D)] = full[96 * k : 96 * (k + 1)]

    loop(4, group)


def encode(buf, row, perm, matrices):
    spots = chunk_spots(matrices)

    def group(g):
        r = rows_of(g, 96)
        parts = jnp.concatenate([m[r, pl.ds(D * c, D)] for m, c in spots], axis=0)
        buf[g, :, :, :, row : row + 48, :] = dot_nn(perm, parts).astype(BF).reshape(2, 2, 2, 48, D)

    loop(4, group)


def decode_small(w1a, gains_ref, router_ref):
    block = w1a[:, :, :, :, 48:64, :].reshape(-1, D)
    spot = lax.broadcasted_iota(jnp.int32, (8, block.shape[0]), 1)
    row = lax.broadcasted_iota(jnp.int32, (8, block.shape[0]), 0)
    pick = (spot % 16 == 0) & (spot // 128 == row)
    gains_ref[...] = dot_nn(jnp.where(pick, 1.0, 0.0).astype(BF), block)
    spot = lax.broadcasted_iota(jnp.int32, (LANES, block.shape[0]), 1)
    row = lax.broadcasted_iota(jnp.int32, (LANES, block.shape[0]), 0)
    pick = (spot % 16 == row + 1) & (row < EXPERTS)
    router_ref[...] = dot_nn(jnp.where(pick, 1.0, 0.0).astype(BF), block).astype(BF)


def encode_small(w1a, gs_ref):
    rest = jnp.zeros((16 - 1 - EXPERTS, D), F32)
    for g in range(4):
        block = jnp.concatenate([gs_ref[pl.ds(g, 1), :], gs_ref[pl.ds(4, EXPERTS), :], rest], axis=0).astype(BF)
        for d in range(8):
            w1a[g, d // 4, d // 2 % 2, d % 2, 48:64, :] = block


def permutation():
    spots = np.arange(D)
    c, d, r = spots // 48, spots // 12 % 4, spots % 12
    table = np.zeros((D, D), np.float32)
    table[spots, d * 96 + c * 12 + r] = 1.0
    return table


class Copy:
    def __init__(self, net, k, ends, mask):
        self.net, self.k, self.ends, self.mask = net, k, ends, mask

    def make(self):
        src, dst = self.ends()
        return pltpu.make_async_remote_copy(
            src_ref=src, dst_ref=dst, send_sem=self.net.send_sem.at[self.k], recv_sem=self.net.recv_sem.at[self.k],
            device_id=(self.net.partner(self.mask),), device_id_type=MESH)

    def start(self):
        self.make().start()

    def wait_recv(self):
        self.make().wait_recv()

    def wait_send(self):
        self.make().wait_send()


class Net:
    masks = (1, 2, 4, 8, 16, 24)

    def __init__(self, send_sem, recv_sem):
        self.send_sem, self.recv_sem, self.count = send_sem, recv_sem, 0
        me = lax.axis_index("fsdp")
        self.c, self.x, self.y, self.z = me % 2, me // 2 % 2, me // 4 % 2, me // 8
        self.zs = [self.flip_z(d) for d in range(4)]
        self.partners = {m: self.partner_of(m) for m in self.masks}

    def partner(self, mask):
        return self.partners[mask]

    def partner_of(self, mask):
        c = 1 - self.c if mask & 1 else self.c
        x = 1 - self.x if mask & 2 else self.x
        y = 1 - self.y if mask & 4 else self.y
        return self.zs[mask >> 3] * 8 + y * 4 + x * 2 + c

    def flip_z(self, d):
        lo, hi = self.z % 2, self.z // 2
        lo = 1 - lo if d & 1 else lo
        hi = 1 - hi if d & 2 else hi
        return hi * 2 + lo

    def barrier(self):
        sem = pltpu.get_barrier_semaphore()
        for m in self.masks:
            pl.semaphore_signal(sem, inc=1, device_id=(self.partner(m),), device_id_type=MESH)
        pl.semaphore_wait(sem, len(self.masks))

    def copy(self, ends, mask):
        k = self.count
        self.count += 1
        return Copy(self, k, ends, mask)


def halves(rows, w):
    if w == D:
        cut = (rows // 32 + 1) * 16 if rows % 32 else rows // 2
        return (pl.ds(0, cut), pl.ds(0, w)), (pl.ds(cut, rows - cut), pl.ds(0, w))
    return (pl.ds(0, rows), pl.ds(0, w // 2)), (pl.ds(0, rows), pl.ds(w // 2, w // 2))


class Gather:
    def __init__(self, net, buf):
        x, y, c = net.x, net.y, net.c
        a, b = halves(*buf.shape[-2:])

        def copy(d, yy, xx, half, mask):
            def ends():
                ref = buf.at[net.zs[d], yy, xx, c]
                ref = ref if half is None else ref.at[half[0], half[1]]
                return ref, ref

            return net.copy(ends, mask)

        def pair(d):
            def ends():
                ref = buf.at[net.zs[d], :, :, c]
                return ref, ref

            return net.copy(ends, 1)

        slots = range(4)
        self.along_z = [None] + [copy(0, y, x, None, d << 3) for d in (1, 2, 3)]
        self.to_y = [copy(d, y, x, a, 4) for d in slots]
        self.to_x = [copy(d, y, x, b, 2) for d in slots]
        self.own_x = [copy(d, y, x, a, 2) for d in slots]
        self.own_y = [copy(d, y, x, b, 4) for d in slots]
        self.far_x = [copy(d, 1 - y, x, a, 2) for d in slots]
        self.far_y = [copy(d, y, 1 - x, b, 4) for d in slots]
        self.pair = [pair(d) for d in slots]

    def send_z(self, d):
        self.along_z[d].start()

    def plane(self, d):
        if d:
            self.along_z[d].wait_recv()
        self.to_y[d].start()
        self.to_x[d].start()
        self.own_x[d].start()
        self.own_y[d].start()

    def across(self, d):
        self.to_y[d].wait_recv()
        self.far_x[d].start()
        self.to_x[d].wait_recv()
        self.far_y[d].start()

    def core(self, d):
        for copy in (self.own_x, self.own_y, self.far_x, self.far_y):
            copy[d].wait_recv()
        self.pair[d].start()

    def here(self, d):
        self.pair[d].wait_recv()

    def sent(self, d):
        for copy in (self.to_y, self.to_x, self.own_x, self.own_y, self.far_x, self.far_y, self.pair):
            copy[d].wait_send()
        if d == 0:
            for k in (1, 2, 3):
                self.along_z[k].wait_send()


class Reduce:
    def __init__(self, net, part, slots, bufs, r4):
        self.net, self.part, self.slots, self.r4 = net, part, slots, r4
        self.recv1, self.r2a, self.r2b, self.r3a, self.r3b = bufs
        x, y, c = net.x, net.y, net.c
        self.a, self.b = halves(*part.shape[-2:])
        planes = pl.ds(0, 4) if len(slots) == 4 else pl.ds(net.zs[slots[0]], 1)
        self.planes = range(4) if len(slots) == 4 else [net.zs[slots[0]]]
        a, b = self.a, self.b

        def one(yy, xx):
            return net.copy(lambda: (part.at[planes, yy, xx, 1 - c], self.recv1.at[:, yy, xx]), 1)

        self.s1 = {(fy, fx): one(1 - y if fy else y, 1 - x if fx else x) for fx in (1, 0) for fy in (1, 0)}

        def two_a(yy):
            return net.copy(lambda: (part.at[planes, yy, 1 - x, c, a[0], a[1]], self.r2a.at[:, yy]), 2)

        def two_b(xx):
            return net.copy(lambda: (part.at[planes, 1 - y, xx, c, b[0], b[1]], self.r2b.at[:, xx]), 4)

        self.s2a = [two_a(1 - y), two_a(y)]
        self.s2b = [two_b(1 - x), two_b(x)]
        self.s3a = net.copy(lambda: (part.at[planes, 1 - y, x, c, a[0], a[1]], self.r3a), 4)
        self.s3b = net.copy(lambda: (part.at[planes, y, 1 - x, c, b[0], b[1]], self.r3b), 2)

        def four(d):
            return net.copy(lambda: (part.at[net.zs[d], y, x, c], r4.at[d - 1]), d << 3)

        self.s4 = {d: four(d) for d in slots if d}

    def add(self, ref, other):
        ref[...] = (ref[...].astype(F32) + other[...].astype(F32)).astype(BF)

    def one(self):
        for copy in self.s1.values():
            copy.start()

    def two(self):
        net = self.net
        x, y, c = net.x, net.y, net.c

        def add_all(fy, fx):
            self.s1[fy, fx].wait_recv()
            yy, xx = (1 - y if fy else y), (1 - x if fx else x)
            for k, z in enumerate(self.planes):
                self.add(self.part.at[z, yy, xx, c], self.recv1.at[k, yy, xx])

        add_all(1, 1)
        self.s2a[0].start()
        self.s2b[0].start()
        add_all(0, 1)
        self.s2a[1].start()
        add_all(1, 0)
        self.s2b[1].start()
        add_all(0, 0)

    def three(self):
        net = self.net
        x, y, c = net.x, net.y, net.c
        a, b = self.a, self.b

        def add_half(yy, xx, half, buf, spot):
            for k, z in enumerate(self.planes):
                self.add(self.part.at[z, yy, xx, c, half[0], half[1]], buf.at[k, spot])

        self.s2a[0].wait_recv()
        add_half(1 - y, x, a, self.r2a, 1 - y)
        self.s3a.start()
        self.s2b[0].wait_recv()
        add_half(y, 1 - x, b, self.r2b, 1 - x)
        self.s3b.start()
        self.s2a[1].wait_recv()
        add_half(y, x, a, self.r2a, y)
        self.s2b[1].wait_recv()
        add_half(y, x, b, self.r2b, x)

    def four(self):
        net = self.net
        x, y, c = net.x, net.y, net.c
        for copy, half, buf in ((self.s3a, self.a, self.r3a), (self.s3b, self.b, self.r3b)):
            copy.wait_recv()
            for k, z in enumerate(self.planes):
                self.add(self.part.at[z, y, x, c, half[0], half[1]], buf.at[k])
        for copy in self.s4.values():
            copy.start()

    def sent(self):
        for copy in [*self.s1.values(), *self.s2a, *self.s2b, self.s3a, self.s3b, *self.s4.values()]:
            copy.wait_send()


def finish(net, part, reduces, r4, stage, row, out, sem):
    total = part[net.z, net.y, net.x, net.c].astype(F32)
    for job in reduces:
        for d, copy in job.s4.items():
            copy.wait_recv()
            total += r4[d - 1].astype(F32)
    count, w = part.shape[-2:]
    copies = []
    for k in range(w // D):
        rows, cols = pl.ds(row + count * k, count), pl.ds(D * k, D)
        stage[rows, :] = total[:, D * k : D * (k + 1)]
        copies.append(pltpu.make_async_copy(stage.at[rows, :], out.at[:, cols], sem.at[k]))
        copies[-1].start()
    return copies


def reduce_buffers(rows, w, planes):
    a, b = halves(rows, w)
    sa, sb = (a[0].size, a[1].size), (b[0].size, b[1].size)
    shapes = [(planes, 2, 2, rows, w), (planes, 2) + sa, (planes, 2) + sb, (planes,) + sa, (planes,) + sb]
    return [pltpu.VMEM(s, BF) for s in shapes]


def block_kernel(remote, names, *refs):
    r = dict(zip(names, refs))
    images = r["tok"].shape[0] // PAD
    w1a, w1b, uw, vw = arrays = [r[k] for k in ("w1a", "w1b", "uw", "vw")]
    sem = r["sem"]
    cot_load = pltpu.make_async_copy(r["cot"], r["cotv"], sem.at[4])
    cot_load.start()

    if remote:
        net = Net(r["send_sem"], r["recv_sem"])
        loads = [
            pltpu.make_async_copy(r[k + "_in"], buf.at[net.z, net.y, net.x, net.c], sem.at[j])
            for j, (k, buf) in enumerate(zip(("w1a", "w1b", "uw", "vw"), arrays))
        ]
        for copy in loads:
            copy.start()
        net.barrier()
        ga, gb, gu, gv = gathers = [Gather(net, buf) for buf in arrays]
        experts = [net.zs[d] for d in range(4)]
        loads[0].wait()
        for d in (1, 2, 3):
            ga.send_z(d)
        ga.plane(0)
        loads[1].wait()
        for d in (1, 2, 3):
            gb.send_z(d)
        loads[2].wait()
        loads[3].wait()
    else:
        loads = [
            pltpu.make_async_copy(r[k + "_in"], buf, sem.at[j])
            for j, (k, buf) in enumerate(zip(("w1a", "w1b", "uw", "vw"), arrays))
        ]
        for copy in loads:
            copy.start()
        experts = range(4)
    x0, x1, x2, x3, b, dhn = (r[k] for k in ("tok", "x1", "x2", "x3", "b", "dhn"))
    x4 = b
    valid, cot = r["valid"], r["cotv"]
    cot_load.wait()
    for i in range(images):
        rows = pl.ds(PAD * i, PAD)
        cot[rows, :] = (cot[rows, :].astype(F32) * valid[i].astype(F32)).astype(BF)
    dhn[...] = jnp.zeros_like(dhn)
    table = r["table"]
    perm = r["perm"]
    win1, wout1, wid1, win2, wout2 = (r[k] for k in ("win1", "wout1", "wid1", "win2", "wout2"))

    def none():
        return None

    def batch(*steps):
        def tick():
            for step in steps:
                step()

        return tick if remote else none

    if remote:
        ga.across(0)
        for d in (1, 2, 3):
            ga.plane(d)
        gb.plane(0)
        for d in (1, 2, 3):
            ga.across(d)
        ga.core(0)
        gb.across(0)
        for d in (1, 2, 3):
            gb.plane(d)
        for d in (1, 2, 3):
            ga.core(d)
        for d in range(4):
            for g in (gu, gv):
                if d:
                    g.send_z(d)
        for d in range(4):
            ga.here(d)
    else:
        loads[0].wait()

    def both(step, d):
        return batch(lambda: getattr(gu, step)(d), lambda: getattr(gv, step)(d))

    decode(w1a, 0, perm[...], (win1, wout1))
    decode_small(w1a, r["gains"], r["router"])
    gains = [r["gains"][pl.ds(k, 1), :] for k in range(4)]
    router = r["router"][...]
    ticks = [
        batch(lambda: gb.across(1), lambda: gb.across(2)),
        batch(lambda: gb.across(3), lambda: gb.core(0), lambda: gb.core(1), both("plane", 0)),
        batch(lambda: gb.core(2), lambda: gb.core(3), both("across", 0)),
        batch(both("plane", 1)),
    ]
    attention_forward(images, x0, x1, gains[0], win1, wout1, r["hn1"], r["qkv1"], r["pb1"], r["o1"], ticks)
    if remote:
        for d in range(4):
            gb.here(d)
    else:
        loads[1].wait()
    decode(w1b, 48, perm[...], (wid1,))
    decode(w1b, 0, perm[...], (win2, wout2))
    ticks = [batch(both("across", 1), both("core", 0)), batch(both("plane", 2))]
    dense_forward(images, x1, x2, gains[1], wid1, w1b, r["hn2"], r["z1"], r["g1"], ticks)
    ticks = [batch(both("across", 2)), batch(both("core", 1)), batch(both("plane", 3)), batch(both("across", 3))]
    attention_forward(images, x2, x3, gains[2], win2, wout2, r["hn3"], r["qkv2"], r["pb2"], r["o2"], ticks)
    router_forward(images, x3, x4, gains[3], router, r["routes"], r["hn4"], table)

    if remote:
        buffers = iter(r["rs"])
        take = lambda: [next(buffers) for _ in range(5)]
        bufs_u, bufs_v = [take(), take()], [take(), take()]
        ru = [Reduce(net, uw, [d], bufs_u[d % 2], r["r4u"]) for d in range(4)]
        rv = [Reduce(net, vw, [d], bufs_v[d % 2], r["r4v"]) for d in range(4)]
        rb = Reduce(net, w1b, [0, 1, 2, 3], take(), r["r4b"])
        ra = Reduce(net, w1a, [0, 1, 2, 3], take(), r["r4a"])
    else:
        loads[2].wait()
        loads[3].wait()

    def reduce_step(step, d):
        return batch(lambda: getattr(ru[d], step)(), lambda: getattr(rv[d], step)())

    def run_expert(d, ticks, late):
        if remote:
            gu.here(d)
            gv.here(d)
        before = batch(lambda: gu.sent(d), lambda: gv.sent(d))
        late = [*late, batch(lambda: ru[d].one())]
        expert_step(
            images, experts[d], x4, cot, dhn, uw, vw, r["hn4"], table, r["ze"], r["ge"], r["dy"], ticks, late, before
        )
        batch(lambda: rv[d].one())()

    run_expert(0, [both("core", 2), both("core", 3)], [])
    run_expert(1, [reduce_step("two", 0), none], [])
    reduce_step("three", 0)()
    run_expert(2, [reduce_step("two", 1), reduce_step("four", 0)], [])
    reduce_step("three", 1)()
    run_expert(3, [reduce_step("two", 2), reduce_step("four", 1)], [])
    reduce_step("three", 2)()
    out_cols = pl.ds(0, D)
    for i in range(images):
        rows = pl.ds(PAD * i, PAD)
        r["ge"][rows, out_cols] = (x4[rows, :] * valid[i].astype(F32)).astype(BF)
    out_store = pltpu.make_async_copy(r["ge"].at[:, out_cols], r["out"], sem.at[5])
    out_store.start()
    gs, dgain, drouter = r["gs"], r["dgain"], r["drouter"]
    gs[...] = jnp.zeros_like(gs)
    router_backward(images, b, cot, x3, gains[3], router, dhn, table, r["hn4"], drouter, dgain)
    gs[pl.ds(4, EXPERTS), :] = drouter[pl.ds(0, EXPERTS), :]
    gs[pl.ds(3, 1), :] = dgain[...]
    dqkv, da = r["ze"], r["dy"]
    ticks = [reduce_step("two", 3), reduce_step("four", 2), reduce_step("three", 3)]
    attention_backward(images, b, x2, gains[2], win2, wout2, r["hn3"], r["qkv2"], r["pb2"], r["o2"], da, dqkv, dgain, win2, wout2, ticks)
    gs[pl.ds(2, 1), :] = dgain[...]
    batch(*(lambda d=d: gb.sent(d) for d in range(4)))()
    encode(w1b, 0, perm[...], (win2, wout2))
    ticks = [reduce_step("four", 3)]
    dense_backward(images, b, x1, gains[1], wid1, w1b, r["hn2"], r["z1"], r["g1"], da, dgain, wid1, ticks)
    gs[pl.ds(1, 1), :] = dgain[...]
    encode(w1b, 48, perm[...], (wid1,))
    if remote:
        rb.one()
    ticks = [batch(lambda: rb.two()), none, batch(lambda: rb.three()), batch(lambda: rb.four())]
    attention_backward(images, b, x0, gains[0], win1, wout1, r["hn1"], r["qkv1"], r["pb1"], r["o1"], da, dqkv, dgain, win1, wout1, ticks)
    gs[pl.ds(0, 1), :] = dgain[...]
    batch(*(lambda d=d: ga.sent(d) for d in range(4)))()
    encode(w1a, 0, perm[...], (win1, wout1))
    encode_small(w1a, gs)
    if remote:
        ra.one()
    r["o1"][...] = b[...].astype(BF)
    delta_store = pltpu.make_async_copy(r["o1"], r["dtok"], sem.at[6])
    delta_store.start()
    if remote:
        stores = finish(net, vw, rv, r["r4v"], x3, 0, r["vw_out"], sem.at[pl.ds(7, 1)])
        stores += finish(net, uw, ru, r["r4u"], x3, 192, r["uw_out"], sem.at[pl.ds(8, 4)])
        ra.two()
        stores += finish(net, w1b, [rb], r["r4b"], x3, 384, r["w1b_out"], sem.at[pl.ds(12, 1)])
        ra.three()
        ra.four()
        stores += finish(net, w1a, [ra], r["r4a"], x3, 528, r["w1a_out"], sem.at[pl.ds(13, 1)])
        for copy in stores:
            copy.wait()
        for job in (*ru, *rv, rb, ra):
            job.sent()
    else:
        stores = [
            pltpu.make_async_copy(buf, r[k + "_out"], sem.at[j])
            for j, (k, buf) in enumerate(zip(("w1a", "w1b", "uw", "vw"), arrays))
        ]
        for copy in stores:
            copy.start()
        for copy in stores:
            copy.wait()
    out_store.wait()
    delta_store.wait()


def run_blocks(remote, tok, cot, valid, routes, w1a, w1b, uw, vw):
    t = tok.shape[0]
    images = t // PAD
    v = pltpu.VMEM
    vmem, smem, hbm = (pl.BlockSpec(memory_space=m) for m in (pltpu.VMEM, pltpu.SMEM, pl.ANY))
    table = permutation()
    pieces = [w.shape[-2:] for w in (w1a, w1b, uw, vw)]
    whole = [(4, 2, 2, 2) + s for s in pieces]
    inputs = dict(
        tok=(tok, vmem), cot=(cot, hbm), valid=(valid, smem), routes=(routes, vmem),
        perm=(jnp.asarray(table, BF), vmem),
        w1a_in=(w1a, hbm), w1b_in=(w1b, hbm), uw_in=(uw, hbm), vw_in=(vw, hbm),
    )
    flat = jax.ShapeDtypeStruct(tok.shape, BF)
    outputs = dict(out=(flat, hbm), dtok=(flat, hbm))
    for name, piece, full in zip(("w1a", "w1b", "uw", "vw"), pieces, whole):
        outputs[name + "_out"] = (jax.ShapeDtypeStruct(piece, F32) if remote else jax.ShapeDtypeStruct(full, BF), hbm)
    scratch = dict(
        w1a=v(whole[0], BF), w1b=v(whole[1], BF), uw=v(whole[2], BF), vw=v(whole[3], BF),
        win1=v((D, 3 * D), BF), wout1=v((D, D), BF), wid1=v((D, FF), BF), win2=v((D, 3 * D), BF), wout2=v((D, D), BF),
        x1=v((t, D), F32), x2=v((t, D), F32), x3=v((t, D), F32), b=v((t, D), F32), dhn=v((t, D), F32),
        hn1=v((t, D), BF), hn2=v((t, D), BF), hn3=v((t, D), BF), hn4=v((t, D), BF),
        qkv1=v((t, 3 * D), BF), qkv2=v((t, 3 * D), BF), o1=v((t, D), BF), o2=v((t, D), BF),
        pb1=v((images * PAIRS, 2 * PAD, PAD), BF), pb2=v((images * PAIRS, 2 * PAD, PAD), BF),
        z1=v((t, FF), BF), g1=v((t, FF), BF), ze=v((t, FF), BF), ge=v((t, FF), BF), dy=v((t, D), BF), cotv=v((t, D), BF),
        table=v((t, LANES), F32),
        drouter=v((LANES, D), F32), dgain=v((1, D), F32), gs=v((16, D), F32), gains=v((8, D), F32), router=v((LANES, D), BF),
        sem=pltpu.SemaphoreType.DMA((14,)),
    )
    if remote:
        scratch["rs"] = [
            spec
            for piece, planes in [(pieces[2], 1)] * 2 + [(pieces[3], 1)] * 2 + [(pieces[1], 4), (pieces[0], 4)]
            for spec in reduce_buffers(*piece, planes)
        ]
        for k, piece in zip("abuv", pieces):
            scratch["r4" + k] = v((3,) + piece, BF)
        scratch["send_sem"] = pltpu.SemaphoreType.DMA((256,))
        scratch["recv_sem"] = pltpu.SemaphoreType.DMA((256,))
    names = (*inputs, *outputs, *scratch)
    params = dict(collective_id=0, has_side_effects=True) if remote else {}
    return pl.pallas_call(
        functools.partial(block_kernel, remote, names),
        out_shape=tuple(o[0] for o in outputs.values()),
        in_specs=[i[1] for i in inputs.values()],
        out_specs=tuple(o[1] for o in outputs.values()),
        scratch_shapes=list(scratch.values()),
        compiler_params=pltpu.CompilerParams(vmem_limit_bytes=63 * 2**20, **params),
    )(*[i[0] for i in inputs.values()])


def chunked(matrices, rows):
    side = jnp.concatenate([m.reshape(rows, -1) for m in matrices], axis=1)
    return side.reshape(rows, -1, D).transpose(1, 0, 2).reshape(-1, D)


def unchunked(piece):
    return piece.reshape(-1, ROWS, D).transpose(1, 0, 2).reshape(ROWS, -1)


def my_pieces(me, norm_gains, in_one, out_one, widen, narrow, router, in_two, out_two, experts_widen, experts_narrow):
    share = norm_gains.shape[0]
    gain_row = lax.dynamic_update_slice(jnp.zeros((1, D), BF), norm_gains[None, :], (0, me % (D // share) * share))
    router_rows = lax.dynamic_update_slice(jnp.zeros((EXPERTS, D), BF), router.reshape(ROWS, EXPERTS).T, (0, me * ROWS))
    rest = jnp.zeros((16 - 1 - EXPERTS, D), BF)
    return (
        jnp.concatenate([chunked((in_one, out_one), ROWS), gain_row, router_rows, rest], axis=0),
        jnp.concatenate([chunked((in_two, out_two), ROWS), chunked((widen,), ROWS), narrow.reshape(-1, D)], axis=0),
        experts_widen.reshape(-1, FF),
        experts_narrow.reshape(-1, D),
    )


def my_deltas(me, w1a, w1b, uw, vw):
    one, two = unchunked(w1a[0:48]), unchunked(w1b[0:48])
    share = 4 * D // SHARDS
    gains = lax.dynamic_slice(w1a[48], (me % (D // share) * share,), (share,))
    router = lax.dynamic_slice(w1a[49:53], (0, me * ROWS), (EXPERTS, ROWS)).T
    parts = (
        gains, one[:, : 3 * D], one[:, 3 * D :], unchunked(w1b[48:96]), w1b[96:144], router, two[:, : 3 * D], two[:, 3 * D :], uw, vw
    )
    return tuple(p.reshape(-1) for p in parts)


def all_pieces(norm_gains, in_one, out_one, widen, narrow, router, in_two, out_two, experts_widen, experts_narrow):
    def cut(*matrices):
        side = jnp.concatenate([m.reshape(D, -1) for m in matrices], axis=1)
        return side.reshape(SHARDS, ROWS, -1, D).transpose(0, 2, 1, 3).reshape(SHARDS, -1, D)

    small = jnp.zeros((SHARDS, 16, D), BF)
    small = small.at[:: SHARDS // 4, 0].set(norm_gains.reshape(4, D))
    small = small.at[0, 1 : 1 + EXPERTS].set(router.reshape(D, EXPERTS).T)
    parts = (
        jnp.concatenate([cut(in_one, out_one), small], axis=1),
        jnp.concatenate([cut(in_two, out_two), cut(widen), narrow.reshape(SHARDS, -1, D)], axis=1),
        experts_widen.reshape(SHARDS, -1, FF),
        experts_narrow.reshape(SHARDS, -1, D),
    )
    return [p.reshape((4, 2, 2, 2) + p.shape[1:]) for p in parts]


def all_deltas(*parts):
    w1a, w1b, uw, vw = (p.astype(F32).reshape((SHARDS,) + p.shape[-2:]) for p in parts)

    def join(part):
        return part.reshape(SHARDS, -1, ROWS, D).transpose(0, 2, 1, 3).reshape(D, -1)

    one, two = join(w1a[:, 0:48]), join(w1b[:, 0:48])
    whole = (
        w1a[:: SHARDS // 4, 48], one[:, : 3 * D], one[:, 3 * D :], join(w1b[:, 48:96]), w1b[:, 96:144], w1a[0, 49:53].T,
        two[:, : 3 * D], two[:, 3 * D :], uw, vw,
    )
    return [p.reshape(-1) for p in whole]


def on_device(shards, tokens, cotangent, image_valid, routes, *weights):
    images = tokens.shape[0] * tokens.shape[1]

    def padded(array):
        return jnp.pad(array.reshape(images, SEQ, D), ((0, 0), (0, PAD - SEQ), (0, 0))).reshape(images * PAD, D)

    def cut(array):
        return array.reshape(images, PAD, D)[:, :SEQ].reshape(tokens.shape)

    named = routes.reshape(images, SEQ, 2).transpose(0, 2, 1)
    named = jnp.pad(named, ((0, 0), (0, 6), (0, 2 * LANES - SEQ)))
    data = (padded(tokens), padded(cotangent), image_valid.reshape(images), named)
    if shards == SHARDS:
        me = lax.axis_index("fsdp")
        out, delta, *sums = run_blocks(True, *data, *my_pieces(me, *weights))
        deltas = my_deltas(me, *sums)
    else:
        whole = [lax.all_gather(w, "fsdp", axis=0, tiled=True) for w in weights]
        out, delta, *sums = run_blocks(False, *data, *all_pieces(*whole))
        deltas = [lax.psum_scatter(d, "fsdp", scatter_dimension=0, tiled=True) for d in all_deltas(*sums)]
    return (cut(out), cut(delta), *deltas)


def solution(mesh):
    split, flat = P(None, "fsdp", None, None), P("fsdp")
    return jax.shard_map(
        functools.partial(on_device, mesh.shape["fsdp"]),
        mesh=mesh,
        in_specs=(split, split, P(None, "fsdp"), split) + (flat,) * 10,
        out_specs=(split, split) + (flat,) * 10,
        check_vma=False,
    )
```

```python
import functools
import math

import jax
import jax.numpy as jnp
import numpy as np
from jax import lax
from jax.experimental import pallas as pl
from jax.experimental.pallas import tpu as pltpu
from jax.sharding import PartitionSpec as P

D = 384
HEADS = 6
HDIM = 64
FF = 1536
EXPERTS = 4
SEQ = 197
PAD = 208
PAIRS = HEADS // 2
SHARDS = 32
ROWS = D // SHARDS
LANES = 128
EPSILON = 1e-06
BF = jnp.bfloat16
F32 = jnp.float32
MESH = pl.DeviceIdType.MESH
C0 = math.sqrt(2.0 / math.pi)
C1 = 0.044715


def dot_nn(a, b):
    return lax.dot_general(a, b, (((1,), (0,)), ((), ())), preferred_element_type=F32)


def dot_nt(a, b):
    return lax.dot_general(a, b, (((1,), (1,)), ((), ())), preferred_element_type=F32)


def dot_tn(a, b):
    return lax.dot_general(a, b, (((0,), (0,)), ((), ())), preferred_element_type=F32)


def normed(x):
    centred = x - jnp.mean(x, axis=-1, keepdims=True)
    rstd = lax.rsqrt(jnp.mean(centred * centred, axis=-1, keepdims=True) + EPSILON)
    return centred * rstd, rstd


def norm_back(x, gain, dhn):
    xhat, rstd = normed(x)
    dxhat = dhn * gain
    mean_d = jnp.mean(dxhat, axis=-1, keepdims=True)
    mean_dx = jnp.mean(dxhat * xhat, axis=-1, keepdims=True)
    return rstd * (dxhat - mean_d - xhat * mean_dx), jnp.sum(dhn * xhat, axis=0, keepdims=True)


def gelu_both(u):
    u2 = u * u
    t = jnp.tanh(u * (C0 + (C0 * C1) * u2))
    h = 0.5 + 0.5 * t
    z = u * h
    return z, h + z * (1.0 - h) * (2.0 * C0 + (6.0 * C0 * C1) * u2)


def rows_of(i, size=PAD):
    return pl.ds(pl.multiple_of(i * size, 16), size)


def loop(count, body, ticks=()):
    def step(i, carry):
        body(i)
        for k, tick in enumerate(ticks):
            pl.when(i == k)(tick)
        return carry

    lax.fori_loop(0, count, step, 0)


def attention_forward(images, x_in, x_out, gain, win, wout, hn_ref, qkv_ref, pb_ref, o_ref, ticks=()):
    low_half = lax.broadcasted_iota(jnp.int32, (PAD, LANES), 1) < HDIM
    real_key = lax.broadcasted_iota(jnp.int32, (2 * PAD, PAD), 1) < SEQ

    def image(i):
        r = rows_of(i)
        x = x_in[r, :].astype(F32)
        xhat, _ = normed(x)
        hn = (xhat * gain).astype(BF)
        hn_ref[r, :] = hn
        for j in range(3):
            cols = pl.ds(D * j, D)
            qkv_ref[r, cols] = dot_nn(hn, win[:, cols]).astype(BF)
        for p in range(PAIRS):
            q2 = qkv_ref[r, pl.ds(LANES * p, LANES)]
            k2 = qkv_ref[r, pl.ds(D + LANES * p, LANES)]
            v2 = qkv_ref[r, pl.ds(2 * D + LANES * p, LANES)]
            zero = jnp.zeros_like(q2)
            qs = jnp.concatenate([jnp.where(low_half, q2, zero), jnp.where(low_half, zero, q2)], axis=0)
            s = dot_nt(qs, k2) * HDIM ** (-0.5)
            s = jnp.where(real_key, s, -1e30)
            w = jnp.exp(s - jnp.max(s, axis=-1, keepdims=True))
            soft = w * (1.0 / jnp.sum(w, axis=-1, keepdims=True))
            pb = soft.astype(BF)
            pb_ref[i * PAIRS + p] = pb
            o2 = dot_nn(pb, v2)
            o_ref[r, pl.ds(LANES * p, LANES)] = jnp.where(low_half, o2[:PAD], o2[PAD:]).astype(BF)
        x_out[r, :] = x + dot_nn(o_ref[r, :], wout[...])

    loop(images, image, ticks)


def attention_backward(
    images, b_ref, x_in, gain, win, wout, hn_ref, qkv_ref, pb_ref, o_ref, da_ref, dqkv_ref, dgain_ref, dwin, dwout, ticks=()
):
    low_half = lax.broadcasted_iota(jnp.int32, (PAD, LANES), 1) < HDIM
    dgain_ref[...] = jnp.zeros_like(dgain_ref)

    def image(i):
        r = rows_of(i)
        b = b_ref[r, :]
        da = b.astype(BF)
        da_ref[r, :] = da
        do = dot_nt(da, wout[...]).astype(BF)
        for p in range(PAIRS):
            cols = [pl.ds(D * j + LANES * p, LANES) for j in range(3)]
            q2, k2, v2 = (qkv_ref[r, c] for c in cols)
            do2 = do[:, LANES * p : LANES * (p + 1)]
            zero = jnp.zeros_like(q2)
            qs = jnp.concatenate([jnp.where(low_half, q2, zero), jnp.where(low_half, zero, q2)], axis=0)
            dos = jnp.concatenate([jnp.where(low_half, do2, zero), jnp.where(low_half, zero, do2)], axis=0)
            pb = pb_ref[i * PAIRS + p]
            soft = pb.astype(F32)
            dp = dot_nt(dos, v2)
            ds = (soft * (dp - jnp.sum(dp * soft, axis=-1, keepdims=True))).astype(BF)
            dq = dot_nn(ds, k2) * HDIM ** (-0.5)
            dqkv_ref[r, cols[0]] = jnp.where(low_half, dq[:PAD], dq[PAD:]).astype(BF)
            dqkv_ref[r, cols[1]] = (dot_tn(ds, qs) * HDIM ** (-0.5)).astype(BF)
            dqkv_ref[r, cols[2]] = dot_tn(pb, dos).astype(BF)
        dhn = dot_nt(dqkv_ref[r, pl.ds(0, 3 * D)], win[...])
        dx, dg = norm_back(x_in[r, :].astype(F32), gain, dhn)
        b_ref[r, :] = b + dx
        dgain_ref[...] += dg

    loop(images, image, ticks)
    dwout[...] = dot_tn(o_ref[...], da_ref[...]).astype(BF)
    hn = hn_ref[...]
    for j in range(3):
        cols = pl.ds(D * j, D)
        dwin[:, cols] = dot_tn(hn, dqkv_ref[:, cols]).astype(BF)


def piece_rows(buf, z, row, cols=None):
    block = buf[z, :, :, :, row : row + 48, :]
    return block.reshape(8 * 48, D)


WIDE = 512
HALF = FF // 2


def narrow_half(w1b, h):
    return w1b[2 * h : 2 * h + 2, :, :, :, 96:144, :].reshape(HALF, D)


def gelu_tiles(hn, wide, z_ref, g_ref, r):
    for j in range(FF // WIDE):
        cols = pl.ds(WIDE * j, WIDE)
        z, g = gelu_both(dot_nn(hn, wide(cols)))
        z_ref[r, cols] = z.astype(BF)
        g_ref[r, cols] = g.astype(BF)


def slope_halves(dy, tall, g_ref, r):
    for h in range(2):
        cols = pl.ds(HALF * h, HALF)
        g_ref[r, cols] = (dot_nt(dy, tall(h)) * g_ref[r, cols].astype(F32)).astype(BF)


def tall_delta(dy_t, z_tile):
    return dot_nn(dy_t, z_tile).astype(BF).T


def row_block(images):
    return 2 * PAD if images % 2 == 0 else PAD


def dense_forward(images, x_in, x_out, gain, wid, w1b, hn_ref, z_ref, g_ref, ticks=()):
    size = row_block(images)

    def block(i):
        r = rows_of(i, size)
        x = x_in[r, :]
        hn = (normed(x)[0] * gain).astype(BF)
        hn_ref[r, :] = hn
        gelu_tiles(hn, lambda cols: wid[:, cols], z_ref, g_ref, r)
        tall = w1b[:, :, :, :, 96:144, :].reshape(FF, D)
        x_out[r, :] = x + dot_nn(z_ref[r, :], tall)

    loop(images * PAD // size, block, ticks)


def dense_backward(images, b_ref, x_in, gain, wid, w1b, hn_ref, z_ref, g_ref, da_ref, dgain_ref, dwid, ticks=()):
    size = row_block(images)
    dgain_ref[...] = jnp.zeros_like(dgain_ref)

    def block(i):
        r = rows_of(i, size)
        b = b_ref[r, :]
        da = b.astype(BF)
        da_ref[r, pl.ds(0, D)] = da
        slope_halves(da, lambda h: narrow_half(w1b, h), g_ref, r)
        dhn = dot_nt(g_ref[r, :], wid[...])
        dx, dg = norm_back(x_in[r, :], gain, dhn)
        b_ref[r, :] = b + dx
        dgain_ref[...] += dg

    loop(images * PAD // size, block, ticks)
    hn_t, da_t = hn_ref[...].T, da_ref[...].T
    for j in range(FF // WIDE):
        cols = pl.ds(WIDE * j, WIDE)
        dwid[:, cols] = dot_nn(hn_t, g_ref[:, cols]).astype(BF)
    for h in range(2):
        delta = tall_delta(da_t, z_ref[:, pl.ds(HALF * h, HALF)])
        w1b[2 * h : 2 * h + 2, :, :, :, 96:144, :] = delta.reshape(2, 2, 2, 2, 48, D)


def router_forward(images, x_in, x_out, gain, router, routes_ref, hn_ref, table_ref):
    lane = lax.broadcasted_iota(jnp.int32, (SEQ, LANES), 1) - EXPERTS
    low_lane = lax.broadcasted_iota(jnp.int32, (PAD, LANES), 1) < EXPERTS

    def image(i):
        r = rows_of(i)
        x = x_in[r, :]
        hn = (normed(x)[0] * gain).astype(BF)
        hn_ref[r, :] = hn
        x_out[r, :] = x
        logits = jnp.where(low_lane, dot_nt(hn, router), -1e30)
        w = jnp.exp(logits - jnp.max(logits, axis=-1, keepdims=True))
        probs = w * (1.0 / jnp.sum(w, axis=-1, keepdims=True))
        table_ref[r, :] = probs
        named = routes_ref[i].T
        hot = (lane == named[:SEQ, 0:1]) | (lane == named[:SEQ, 1:2])
        table_ref[pl.ds(pl.multiple_of(i * PAD, 16), SEQ), :] = jnp.where(hot, 1.0, probs[:SEQ])

    loop(images, image)


def expert_step(
    images, e, x_out, cot_ref, dhn_ref, uw, vw, hn_ref, table_ref, z_ref, g_ref, dy_ref, ticks=(), late=(), before=None
):
    size = row_block(images)
    lane = lax.broadcasted_iota(jnp.int32, (size, LANES), 1)

    def u_tile(cols):
        return uw[e, :, :, :, :, cols].reshape(D, -1)

    def v_half(h):
        return vw[e, h].reshape(HALF, D)

    def block(i):
        r = rows_of(i, size)
        hn = hn_ref[r, :]
        gelu_tiles(hn, u_tile, z_ref, g_ref, r)
        y = dot_nn(z_ref[r, :], vw[e].reshape(FF, D))
        table = table_ref[r, :]
        hot = jnp.sum(jnp.where(lane == e + EXPERTS, table, 0.0), axis=-1, keepdims=True)
        gate = hot * jnp.sum(jnp.where(lane == e, table, 0.0), axis=-1, keepdims=True)
        b = cot_ref[r, :].astype(F32)
        x_out[r, :] += gate * y
        dgate = hot * jnp.sum(b * y, axis=-1, keepdims=True)
        table_ref[r, :] = jnp.where(lane == e + 2 * EXPERTS, dgate, table)
        dy = (gate * b).astype(BF)
        dy_ref[r, :] = dy
        slope_halves(dy, v_half, g_ref, r)
        dhn_ref[r, :] += dot_nt(g_ref[r, :], u_tile(pl.ds(0, FF)))

    loop(images * PAD // size, block, ticks)
    if before is not None:
        before()
    hn_t, dy_t = hn_ref[...].T, dy_ref[...].T
    for j in range(FF // WIDE):
        cols = pl.ds(WIDE * j, WIDE)
        uw[e, :, :, :, :, cols] = dot_nn(hn_t, g_ref[:, cols]).astype(BF).reshape(2, 2, 2, 48, WIDE)
    for tick in late:
        tick()
    for h in range(2):
        vw[e, h] = tall_delta(dy_t, z_ref[:, pl.ds(HALF * h, HALF)]).reshape(2, 2, 192, D)


def router_backward(images, b_ref, cot_ref, x_in, gain, router, dhn_ref, table_ref, hn_ref, drouter_ref, dgain_ref, ticks=()):
    dgain_ref[...] = jnp.zeros_like(dgain_ref)
    drouter_ref[...] = jnp.zeros_like(drouter_ref)
    low_lane = lax.broadcasted_iota(jnp.int32, (PAD, LANES), 1) < EXPERTS

    def image(i):
        r = rows_of(i)
        table = table_ref[r, :]
        probs = jnp.where(low_lane, table, 0.0)
        dprobs = pltpu.roll(table, LANES - 2 * EXPERTS, 1)
        dlogits = (probs * (dprobs - jnp.sum(dprobs * probs, axis=-1, keepdims=True))).astype(BF)
        drouter_ref[...] += dot_tn(dlogits, hn_ref[r, :])[:8]
        dhn = dhn_ref[r, :] + dot_nn(dlogits, router)
        dx, dg = norm_back(x_in[r, :], gain, dhn)
        b_ref[r, :] = cot_ref[r, :].astype(F32) + dx
        dgain_ref[...] += dg

    loop(images, image, ticks)


def chunk_spots(matrices):
    return [(m, c) for m in matrices for c in range(m.shape[1] // D)]


def decode(buf, row, matrices):
    spots, perm = chunk_spots(matrices), permutation()

    def group(g):
        full = dot_tn(perm, piece_rows(buf, g, row)).astype(BF)
        r = rows_of(g, 96)
        for k, (m, c) in enumerate(spots):
            m[r, pl.ds(D * c, D)] = full[96 * k : 96 * (k + 1)]

    loop(4, group)


def encode(buf, row, matrices):
    spots, perm = chunk_spots(matrices), permutation()

    def group(g):
        r = rows_of(g, 96)
        parts = jnp.concatenate([m[r, pl.ds(D * c, D)] for m, c in spots], axis=0)
        buf[g, :, :, :, row : row + 48, :] = dot_nn(perm, parts).astype(BF).reshape(2, 2, 2, 48, D)

    loop(4, group)


def decode_small(w1a, gains_ref, router_ref):
    block = w1a[:, :, :, :, 48:64, :].reshape(-1, D)
    spot = lax.broadcasted_iota(jnp.int32, (8, block.shape[0]), 1)
    row = lax.broadcasted_iota(jnp.int32, (8, block.shape[0]), 0)
    pick = (spot % 16 == 0) & (spot // 128 == row)
    gains_ref[...] = dot_nn(jnp.where(pick, 1.0, 0.0).astype(BF), block)
    spot = lax.broadcasted_iota(jnp.int32, (LANES, block.shape[0]), 1)
    row = lax.broadcasted_iota(jnp.int32, (LANES, block.shape[0]), 0)
    pick = (spot % 16 == row + 1) & (row < EXPERTS)
    router_ref[...] = dot_nn(jnp.where(pick, 1.0, 0.0).astype(BF), block).astype(BF)


def encode_small(w1a, gs_ref):
    rest = jnp.zeros((16 - 1 - EXPERTS, D), F32)
    for g in range(4):
        block = jnp.concatenate([gs_ref[pl.ds(g, 1), :], gs_ref[pl.ds(4, EXPERTS), :], rest], axis=0).astype(BF)
        for d in range(8):
            w1a[g, d // 4, d // 2 % 2, d % 2, 48:64, :] = block


def spot_grid(shape):
    return lax.broadcasted_iota(jnp.int32, shape, 0), lax.broadcasted_iota(jnp.int32, shape, 1)


def picked(rows, flat, spot):
    row, col = spot_grid((rows, flat.shape[0]))
    parts = [dot_nn(jnp.where(col == spot(row, k), 1.0, 0.0).astype(BF), flat) for k in range(D // LANES)]
    return jnp.concatenate(parts, axis=1)


def chunk_rows(flat, first, chunks, rows=4 * ROWS):
    wide = chunks * D // LANES

    def spot(row, k):
        c = row // ROWS - first
        inside = (c >= 0) & (c < chunks)
        return jnp.where(inside, wide * (row % ROWS) + D // LANES * c + k, -1)

    return picked(rows, flat, spot)


def assemble_attention(own, row, flat_in, flat_out):
    both = chunk_rows(flat_in[...], 0, 3) + chunk_rows(flat_out[...], 3, 1)
    own[row : row + 4 * ROWS, :] = both.astype(BF)


def small_places(me):
    i, j = spot_grid((LANES, D))
    share = 4 * D // SHARDS
    place = [(i < share) & (j == me % (D // share) * share + i)]
    for e in range(EXPERTS):
        place.append((i >= share) & (i < 2 * share) & (i % EXPERTS == e) & (j == me * ROWS + (i - share) // EXPERTS))
    return [jnp.where(p, 1.0, 0.0) for p in place]


def assemble_small(own, places, flat):
    row, _ = spot_grid((16, D))
    total = jnp.zeros((16, D), F32)
    for q, place in enumerate(places):
        total += jnp.where(row == q, dot_nn(flat, place.astype(BF))[0:1], 0.0)
    own[48:64, :] = total.astype(BF)


def scatter_chunks(stage, row, cols, total, first, chunks):
    wide = chunks * D // LANES
    for c in range(chunks):
        for k in range(D // LANES):
            spots = pl.ds(row + D // LANES * c + k, ROWS, stride=wide)
            stage[spots, cols] = total[ROWS * (first + c) : ROWS * (first + c + 1), LANES * k : LANES * (k + 1)]


def scatter_rows(stage, row, cols, total):
    wide = total.shape[1] // LANES
    for k in range(wide):
        stage[pl.ds(row + k, total.shape[0], stride=wide), cols] = total[:, LANES * k : LANES * (k + 1)]


def permutation():
    k = lax.broadcasted_iota(jnp.int32, (1, D), 1)
    spot = k // ROWS % 8 * (4 * ROWS) + k // (8 * ROWS) * ROWS + k % ROWS
    return jnp.where(lax.broadcasted_iota(jnp.int32, (D, D), 0) == spot, 1.0, 0.0).astype(BF)


class Copy:
    def __init__(self, net, k, ends, mask):
        self.net, self.k, self.ends, self.mask = net, k, ends, mask

    def make(self):
        src, dst = self.ends()
        return pltpu.make_async_remote_copy(
            src_ref=src, dst_ref=dst, send_sem=self.net.send_sem.at[self.k], recv_sem=self.net.recv_sem.at[self.k],
            device_id=(self.net.partner(self.mask),), device_id_type=MESH)

    def start(self):
        self.make().start()

    def wait_recv(self):
        self.make().wait_recv()

    def wait_send(self):
        self.make().wait_send()


class Net:
    masks = (1, 2, 4, 8, 16, 24)

    def __init__(self, send_sem, recv_sem):
        self.send_sem, self.recv_sem, self.count = send_sem, recv_sem, 0
        me = self.me = lax.axis_index("fsdp")
        self.c, self.x, self.y, self.z = me % 2, me // 2 % 2, me // 4 % 2, me // 8
        self.zs = [self.flip_z(d) for d in range(4)]
        self.partners = {m: self.partner_of(m) for m in self.masks}

    def partner(self, mask):
        return self.partners[mask]

    def partner_of(self, mask):
        c = 1 - self.c if mask & 1 else self.c
        x = 1 - self.x if mask & 2 else self.x
        y = 1 - self.y if mask & 4 else self.y
        return self.zs[mask >> 3] * 8 + y * 4 + x * 2 + c

    def flip_z(self, d):
        lo, hi = self.z % 2, self.z // 2
        lo = 1 - lo if d & 1 else lo
        hi = 1 - hi if d & 2 else hi
        return hi * 2 + lo

    def barrier(self):
        sem = pltpu.get_barrier_semaphore()
        for m in self.masks:
            pl.semaphore_signal(sem, inc=1, device_id=(self.partner(m),), device_id_type=MESH)
        pl.semaphore_wait(sem, len(self.masks))

    def copy(self, ends, mask):
        k = self.count
        self.count += 1
        return Copy(self, k, ends, mask)


def halves(rows, w):
    if w == D:
        cut = (rows // 32 + 1) * 16 if rows % 32 else rows // 2
        return (pl.ds(0, cut), pl.ds(0, w)), (pl.ds(cut, rows - cut), pl.ds(0, w))
    return (pl.ds(0, rows), pl.ds(0, w // 2)), (pl.ds(0, rows), pl.ds(w // 2, w // 2))


class Gather:
    def __init__(self, net, buf):
        x, y, c = net.x, net.y, net.c
        a, b = halves(*buf.shape[-2:])

        def copy(d, yy, xx, half, mask):
            def ends():
                ref = buf.at[net.zs[d], yy, xx, c]
                ref = ref if half is None else ref.at[half[0], half[1]]
                return ref, ref

            return net.copy(ends, mask)

        def pair(d):
            def ends():
                ref = buf.at[net.zs[d], :, :, c]
                return ref, ref

            return net.copy(ends, 1)

        slots = range(4)
        self.along_z = [None] + [copy(0, y, x, None, d << 3) for d in (1, 2, 3)]
        self.to_y = [copy(d, y, x, a, 4) for d in slots]
        self.to_x = [copy(d, y, x, b, 2) for d in slots]
        self.own_x = [copy(d, y, x, a, 2) for d in slots]
        self.own_y = [copy(d, y, x, b, 4) for d in slots]
        self.far_x = [copy(d, 1 - y, x, a, 2) for d in slots]
        self.far_y = [copy(d, y, 1 - x, b, 4) for d in slots]
        self.pair = [pair(d) for d in slots]

    def send_z(self, d):
        self.along_z[d].start()

    def plane(self, d):
        if d:
            self.along_z[d].wait_recv()
        self.to_y[d].start()
        self.to_x[d].start()
        self.own_x[d].start()
        self.own_y[d].start()

    def across(self, d):
        self.to_y[d].wait_recv()
        self.far_x[d].start()
        self.to_x[d].wait_recv()
        self.far_y[d].start()

    def core(self, d):
        for copy in (self.own_x, self.own_y, self.far_x, self.far_y):
            copy[d].wait_recv()
        self.pair[d].start()

    def here(self, d):
        self.pair[d].wait_recv()

    def sent(self, d):
        for copy in (self.to_y, self.to_x, self.own_x, self.own_y, self.far_x, self.far_y, self.pair):
            copy[d].wait_send()
        if d == 0:
            for k in (1, 2, 3):
                self.along_z[k].wait_send()


class Reduce:
    def __init__(self, net, part, slots, bufs, r4):
        self.net, self.part, self.slots, self.r4 = net, part, slots, r4
        self.recv1, self.r2a, self.r2b, self.r3a, self.r3b = bufs
        x, y, c = net.x, net.y, net.c
        self.a, self.b = halves(*part.shape[-2:])
        planes = pl.ds(0, 4) if len(slots) == 4 else pl.ds(net.zs[slots[0]], 1)
        self.planes = range(4) if len(slots) == 4 else [net.zs[slots[0]]]
        a, b = self.a, self.b

        def one(yy, xx):
            return net.copy(lambda: (part.at[planes, yy, xx, 1 - c], self.recv1.at[:, yy, xx]), 1)

        self.s1 = {(fy, fx): one(1 - y if fy else y, 1 - x if fx else x) for fx in (1, 0) for fy in (1, 0)}

        def two_a(yy):
            return net.copy(lambda: (part.at[planes, yy, 1 - x, c, a[0], a[1]], self.r2a.at[:, yy]), 2)

        def two_b(xx):
            return net.copy(lambda: (part.at[planes, 1 - y, xx, c, b[0], b[1]], self.r2b.at[:, xx]), 4)

        self.s2a = [two_a(1 - y), two_a(y)]
        self.s2b = [two_b(1 - x), two_b(x)]
        self.s3a = net.copy(lambda: (part.at[planes, 1 - y, x, c, a[0], a[1]], self.r3a), 4)
        self.s3b = net.copy(lambda: (part.at[planes, y, 1 - x, c, b[0], b[1]], self.r3b), 2)

        def four(d):
            return net.copy(lambda: (part.at[net.zs[d], y, x, c], r4.at[d - 1]), d << 3)

        self.s4 = {d: four(d) for d in slots if d}

    def add(self, ref, other):
        ref[...] = (ref[...].astype(F32) + other[...].astype(F32)).astype(BF)

    def one(self):
        for copy in self.s1.values():
            copy.start()

    def two(self):
        net = self.net
        x, y, c = net.x, net.y, net.c

        def add_all(fy, fx):
            self.s1[fy, fx].wait_recv()
            yy, xx = (1 - y if fy else y), (1 - x if fx else x)
            for k, z in enumerate(self.planes):
                self.add(self.part.at[z, yy, xx, c], self.recv1.at[k, yy, xx])

        add_all(1, 1)
        self.s2a[0].start()
        self.s2b[0].start()
        add_all(0, 1)
        self.s2a[1].start()
        add_all(1, 0)
        self.s2b[1].start()
        add_all(0, 0)

    def three(self):
        net = self.net
        x, y, c = net.x, net.y, net.c
        a, b = self.a, self.b

        def add_half(yy, xx, half, buf, spot):
            for k, z in enumerate(self.planes):
                self.add(self.part.at[z, yy, xx, c, half[0], half[1]], buf.at[k, spot])

        self.s2a[0].wait_recv()
        add_half(1 - y, x, a, self.r2a, 1 - y)
        self.s3a.start()
        self.s2b[0].wait_recv()
        add_half(y, 1 - x, b, self.r2b, 1 - x)
        self.s3b.start()
        self.s2a[1].wait_recv()
        add_half(y, x, a, self.r2a, y)
        self.s2b[1].wait_recv()
        add_half(y, x, b, self.r2b, x)

    def four(self):
        net = self.net
        x, y, c = net.x, net.y, net.c
        for copy, half, buf in ((self.s3a, self.a, self.r3a), (self.s3b, self.b, self.r3b)):
            copy.wait_recv()
            for k, z in enumerate(self.planes):
                self.add(self.part.at[z, y, x, c, half[0], half[1]], buf.at[k])
        for copy in self.s4.values():
            copy.start()

    def sent(self):
        for copy in [*self.s1.values(), *self.s2a, *self.s2b, self.s3a, self.s3b, *self.s4.values()]:
            copy.wait_send()


def summed(net, part, reduces, r4):
    total = part[net.z, net.y, net.x, net.c].astype(F32)
    for job in reduces:
        for d, copy in job.s4.items():
            copy.wait_recv()
            total += r4[d - 1].astype(F32)
    return total


def reduce_buffers(rows, w, planes):
    a, b = halves(rows, w)
    sa, sb = (a[0].size, a[1].size), (b[0].size, b[1].size)
    shapes = [(planes, 2, 2, rows, w), (planes, 2) + sa, (planes, 2) + sb, (planes,) + sa, (planes,) + sb]
    return [pltpu.VMEM(s, BF) for s in shapes]


def block_kernel(remote, names, *refs):
    r = dict(zip(names, refs))
    images = r["tok"].shape[0] // PAD
    w1a, w1b, uw, vw = arrays = [r[k] for k in ("w1a", "w1b", "uw", "vw")]
    sem = r["sem"]
    cot_load = pltpu.make_async_copy(r["cot"], r["cotv"], sem.at[4])
    cot_load.start()
    x0 = r["hn4"]
    tok_load = pltpu.make_async_copy(r["tok"], x0, sem.at[6])
    tok_load.start()

    if remote:
        net = Net(r["send_sem"], r["recv_sem"])
        own = [buf.at[net.z, net.y, net.x, net.c] for buf in arrays]
        tall = [r["ge"].at[pl.ds(0, r[name].shape[0]), pl.ds(LANES * k, LANES)] for k, name in enumerate(FLAT[-2:])]
        loads = [pltpu.make_async_copy(r[name], ref, sem.at[k]) for k, (name, ref) in enumerate(zip(FLAT[-2:], tall))]
        for copy in loads:
            copy.start()
        places = small_places(net.me)
        assemble_attention(own[0], 0, r["in_one"], r["out_one"])
        assemble_small(own[0], places, r["small"][...])
        net.barrier()
        ga, gb, gu, gv = [Gather(net, buf) for buf in arrays]
        experts = [net.zs[d] for d in range(4)]
        for d in (1, 2, 3):
            ga.send_z(d)
        ga.plane(0)
        assemble_attention(own[1], 0, r["in_two"], r["out_two"])
        own[1][48:96, :] = chunk_rows(r["widen"][...], 0, 4).astype(BF)
        own[1][96:144, :] = picked(48, r["narrow"][...], lambda row, k: 3 * row + k).astype(BF)
    else:
        loads = [
            pltpu.make_async_copy(r[k + "_in"], buf, sem.at[j])
            for j, (k, buf) in enumerate(zip(("w1a", "w1b", "uw", "vw"), arrays))
        ]
        for copy in loads:
            copy.start()
        experts = range(4)
    x1, x2, x3, b, dhn = (r[k] for k in ("x1", "x2", "x3", "b", "dhn"))
    x4 = b
    valid, cot = r["valid"], r["cotv"]
    cot_load.wait()
    tok_load.wait()
    for i in range(images):
        rows = pl.ds(PAD * i, PAD)
        cot[rows, :] = (cot[rows, :].astype(F32) * valid[i].astype(F32)).astype(BF)
    dhn[...] = jnp.zeros_like(dhn)
    table = r["table"]
    win1, wout1, wid1, win2, wout2 = (r[k] for k in ("win1", "wout1", "wid1", "win2", "wout2"))

    def none():
        return None

    def batch(*steps):
        def tick():
            for step in steps:
                step()

        return tick if remote else none

    def both(step, d):
        return batch(lambda: getattr(gu, step)(d), lambda: getattr(gv, step)(d))

    if remote:
        ga.across(0)
        for d in (1, 2, 3):
            ga.plane(d)
        for d in (1, 2, 3):
            gb.send_z(d)
        for copy in loads:
            copy.wait()
        for j in range(FF // D):
            own[2][:, pl.ds(D * j, D)] = picked(48, tall[0][...], lambda row, k: 12 * row + 3 * j + k).astype(BF)
        own[3][...] = picked(192, tall[1][...], lambda row, k: 3 * row + k).astype(BF)
        gb.plane(0)
        for d in (1, 2, 3):
            ga.across(d)
        gu.send_z(1)
        gv.send_z(1)
        ga.core(0)
        gb.across(0)
        for d in (1, 2, 3):
            gb.plane(d)
        for d in (1, 2, 3):
            ga.core(d)
        both("send_z", 2)()
        for d in range(4):
            ga.here(d)
    else:
        loads[0].wait()

    decode(w1a, 0, (win1, wout1))
    decode_small(w1a, r["gains"], r["router"])
    gains = [r["gains"][pl.ds(k, 1), :] for k in range(4)]
    router = r["router"][...]
    ticks = [
        batch(lambda: gb.across(1), lambda: gb.across(2), lambda: gb.across(3), both("plane", 0)),
        batch(lambda: gb.core(0), lambda: gb.core(1), lambda: gb.core(2)),
        batch(lambda: gb.core(3), both("send_z", 3)),
        batch(both("across", 0)),
    ]
    attention_forward(images, x0, x1, gains[0], win1, wout1, r["hn1"], r["qkv1"], r["pb1"], r["o1"], ticks)
    if remote:
        for d in range(4):
            gb.here(d)
    else:
        loads[1].wait()
    decode(w1b, 48, (wid1,))
    decode(w1b, 0, (win2, wout2))
    ticks = [both("plane", 1), both("core", 0)]
    dense_forward(images, x1, x2, gains[1], wid1, w1b, r["hn2"], r["z1"], r["g1"], ticks)
    ticks = [none, both("across", 1), none, both("plane", 2)]
    attention_forward(images, x2, x3, gains[2], win2, wout2, r["hn3"], r["qkv2"], r["pb2"], r["o2"], ticks)
    router_forward(images, x3, x4, gains[3], router, r["routes"], r["hn4"], table)

    if remote:
        buffers = iter(r["rs"])
        take = lambda: [next(buffers) for _ in range(5)]
        bufs_u, bufs_v = [take(), take()], [take(), take()]
        ru = [Reduce(net, uw, [d], bufs_u[d % 2], r["r4u"]) for d in range(4)]
        rv = [Reduce(net, vw, [d], bufs_v[d % 2], r["r4v"]) for d in range(4)]
        rb = Reduce(net, w1b, [0, 1, 2, 3], take(), r["r4b"])
        ra = Reduce(net, w1a, [0, 1, 2, 3], take(), r["r4a"])
    else:
        loads[2].wait()
        loads[3].wait()

    def reduce_step(step, d):
        return batch(lambda: getattr(ru[d], step)(), lambda: getattr(rv[d], step)())

    def run_expert(d, ticks, late):
        if remote:
            gu.here(d)
            gv.here(d)
        before = batch(lambda: gu.sent(d), lambda: gv.sent(d))
        late = [*late, batch(lambda: ru[d].one())]
        expert_step(
            images, experts[d], x4, cot, dhn, uw, vw, r["hn4"], table, r["ze"], r["ge"], r["dy"], ticks, late, before
        )
        batch(lambda: rv[d].one())()

    both("core", 1)()
    run_expert(0, [both("across", 2), both("plane", 3)], [both("core", 2)])
    both("across", 3)()
    run_expert(1, [reduce_step("two", 0), both("core", 3)], [])
    reduce_step("three", 0)()
    run_expert(2, [reduce_step("two", 1), reduce_step("four", 0)], [])
    reduce_step("three", 1)()
    run_expert(3, [reduce_step("two", 2), reduce_step("four", 1)], [])
    reduce_step("three", 2)()
    out_cols = pl.ds(0, D)
    for i in range(images):
        rows = pl.ds(PAD * i, PAD)
        r["ge"][rows, out_cols] = (x4[rows, :] * valid[i].astype(F32)).astype(BF)
    out_store = pltpu.make_async_copy(r["ge"].at[:, out_cols], r["out"], sem.at[5])
    out_store.start()
    gs, dgain, drouter = r["gs"], r["dgain"], r["drouter"]
    gs[...] = jnp.zeros_like(gs)
    router_backward(images, b, cot, x3, gains[3], router, dhn, table, r["hn4"], drouter, dgain)
    tok_load.start()
    gs[pl.ds(4, EXPERTS), :] = drouter[pl.ds(0, EXPERTS), :]
    gs[pl.ds(3, 1), :] = dgain[...]
    dqkv, da = r["ze"], r["dy"]
    ticks = [reduce_step("two", 3), reduce_step("four", 2), reduce_step("three", 3)]
    attention_backward(images, b, x2, gains[2], win2, wout2, r["hn3"], r["qkv2"], r["pb2"], r["o2"], da, dqkv, dgain, win2, wout2, ticks)
    gs[pl.ds(2, 1), :] = dgain[...]
    batch(*(lambda d=d: gb.sent(d) for d in range(4)))()
    encode(w1b, 0, (win2, wout2))
    ticks = [reduce_step("four", 3)]
    dense_backward(images, b, x1, gains[1], wid1, w1b, r["hn2"], r["z1"], r["g1"], da, dgain, wid1, ticks)
    gs[pl.ds(1, 1), :] = dgain[...]
    encode(w1b, 48, (wid1,))
    if remote:
        rb.one()
    lanes = pl.ds(0, LANES)

    def leave(name, row, k):
        flat = r[name + "_out"]
        return pltpu.make_async_copy(table.at[pl.ds(row, flat.shape[0]), :], flat, sem.at[k])

    def tall_sum():
        scatter_rows(table, 0, lanes, summed(net, vw, rv, r["r4v"]))
        leave("tall_v", 0, 7).start()

    tok_load.wait()
    ticks = [batch(lambda: rb.two()), none, batch(lambda: rb.three()), batch(tall_sum, lambda: rb.four())]
    attention_backward(images, b, x0, gains[0], win1, wout1, r["hn1"], r["qkv1"], r["pb1"], r["o1"], da, dqkv, dgain, win1, wout1, ticks)
    gs[pl.ds(0, 1), :] = dgain[...]
    batch(*(lambda d=d: ga.sent(d) for d in range(4)))()
    encode(w1a, 0, (win1, wout1))
    encode_small(w1a, gs)
    if remote:
        ra.one()
    r["o1"][...] = b[...].astype(BF)
    delta_store = pltpu.make_async_copy(r["o1"], r["dtok"], sem.at[6])
    delta_store.start()
    if remote:
        leave("tall_v", 0, 7).wait()
        scatter_rows(table, 0, lanes, summed(net, uw, ru, r["r4u"]))
        leave("tall_u", 0, 8).start()
        ra.two()
        total = summed(net, w1b, [rb], r["r4b"])
        scatter_chunks(r["in_two_out"], 0, lanes, total, 0, 3)
        scatter_chunks(r["out_two_out"], 0, lanes, total, 3, 1)
        scatter_chunks(table, 576, lanes, total, 4, 4)
        leave("widen", 576, 9).start()
        scatter_rows(r["narrow_out"], 0, lanes, total[96:144])
        ra.three()
        ra.four()
        total = summed(net, w1a, [ra], r["r4a"])
        scatter_chunks(r["in_one_out"], 0, lanes, total, 0, 3)
        scatter_chunks(r["out_one_out"], 0, lanes, total, 3, 1)
        exact = dict(precision=lax.Precision.HIGHEST, preferred_element_type=F32)
        small = jnp.zeros((8, LANES), F32)
        for q, place in enumerate(places):
            line = jnp.broadcast_to(total[48 + q : 49 + q], (8, D))
            small += lax.dot_general(line, place, (((1,), (1,)), ((), ())), **exact)
        r["small_out"][...] = small
        leave("tall_u", 0, 8).wait()
        leave("widen", 576, 9).wait()
        for job in (*ru, *rv, rb, ra):
            job.sent()
    else:
        stores = [
            pltpu.make_async_copy(buf, r[k + "_out"], sem.at[j])
            for j, (k, buf) in enumerate(zip(("w1a", "w1b", "uw", "vw"), arrays))
        ]
        for copy in stores:
            copy.start()
        for copy in stores:
            copy.wait()
    out_store.wait()
    delta_store.wait()


PIECES = ((64, D), (144, D), (48, FF), (192, D))
AWAY = ("widen", "tall_u", "tall_v")
FLAT = ("in_one", "out_one", "widen", "narrow", "in_two", "out_two", "tall_u", "tall_v")


def run_blocks(remote, tok, cot, valid, routes, *weights):
    t = tok.shape[0]
    images = t // PAD
    v = pltpu.VMEM
    vmem, smem, hbm = (pl.BlockSpec(memory_space=m) for m in (pltpu.VMEM, pltpu.SMEM, pl.ANY))
    whole = [(4, 2, 2, 2) + s for s in PIECES]
    inputs = dict(
        tok=(tok, hbm), cot=(cot, hbm), valid=(valid, smem), routes=(routes, vmem),
    )
    if remote:
        inputs.update({name: (w, hbm if name in FLAT[-2:] else vmem) for name, w in zip((*FLAT, "small"), weights)})
    else:
        inputs.update({name + "_in": (w, hbm) for name, w in zip(("w1a", "w1b", "uw", "vw"), weights)})
    flat = jax.ShapeDtypeStruct(tok.shape, BF)
    outputs = dict(out=(flat, hbm), dtok=(flat, hbm))
    if remote:
        for name, w in zip(FLAT, weights):
            outputs[name + "_out"] = (jax.ShapeDtypeStruct(w.shape, F32), hbm if name in AWAY else vmem)
        outputs["small_out"] = (jax.ShapeDtypeStruct((8, LANES), F32), vmem)
    else:
        for name, full in zip(("w1a", "w1b", "uw", "vw"), whole):
            outputs[name + "_out"] = (jax.ShapeDtypeStruct(full, BF), hbm)
    scratch = dict(
        w1a=v(whole[0], BF), w1b=v(whole[1], BF), uw=v(whole[2], BF), vw=v(whole[3], BF),
        win1=v((D, 3 * D), BF), wout1=v((D, D), BF), wid1=v((D, FF), BF), win2=v((D, 3 * D), BF), wout2=v((D, D), BF),
        x1=v((t, D), F32), x2=v((t, D), F32), x3=v((t, D), F32), b=v((t, D), F32), dhn=v((t, D), F32),
        hn1=v((t, D), BF), hn2=v((t, D), BF), hn3=v((t, D), BF), hn4=v((t, D), BF),
        qkv1=v((t, 3 * D), BF), qkv2=v((t, 3 * D), BF), o1=v((t, D), BF), o2=v((t, D), BF),
        pb1=v((images * PAIRS, 2 * PAD, PAD), BF), pb2=v((images * PAIRS, 2 * PAD, PAD), BF),
        z1=v((t, FF), BF), g1=v((t, FF), BF), ze=v((t, FF), BF), ge=v((t, FF), BF), dy=v((t, D), BF), cotv=v((t, D), BF),
        table=v((t, LANES), F32),
        drouter=v((8, D), F32), dgain=v((1, D), F32), gs=v((16, D), F32), gains=v((8, D), F32), router=v((LANES, D), BF),
        sem=pltpu.SemaphoreType.DMA((16,)),
    )
    if remote:
        scratch["rs"] = [
            spec
            for piece, planes in [(PIECES[2], 1)] * 2 + [(PIECES[3], 1)] * 2 + [(PIECES[1], 4), (PIECES[0], 4)]
            for spec in reduce_buffers(*piece, planes)
        ]
        for k, piece in zip("abuv", PIECES):
            scratch["r4" + k] = v((3,) + piece, BF)
        scratch["send_sem"] = pltpu.SemaphoreType.DMA((256,))
        scratch["recv_sem"] = pltpu.SemaphoreType.DMA((256,))
    names = (*inputs, *outputs, *scratch)
    params = dict(collective_id=0, has_side_effects=True) if remote else {}
    return pl.pallas_call(
        functools.partial(block_kernel, remote, names),
        out_shape=tuple(o[0] for o in outputs.values()),
        in_specs=[i[1] for i in inputs.values()],
        out_specs=tuple(o[1] for o in outputs.values()),
        scratch_shapes=list(scratch.values()),
        compiler_params=pltpu.CompilerParams(vmem_limit_bytes=127 * 2**19, **params),
    )(*[i[0] for i in inputs.values()])


def all_pieces(norm_gains, in_one, out_one, widen, narrow, router, in_two, out_two, experts_widen, experts_narrow):
    def cut(*matrices):
        side = jnp.concatenate([m.reshape(D, -1) for m in matrices], axis=1)
        return side.reshape(SHARDS, ROWS, -1, D).transpose(0, 2, 1, 3).reshape(SHARDS, -1, D)

    small = jnp.zeros((SHARDS, 16, D), BF)
    small = small.at[:: SHARDS // 4, 0].set(norm_gains.reshape(4, D))
    small = small.at[0, 1 : 1 + EXPERTS].set(router.reshape(D, EXPERTS).T)
    parts = (
        jnp.concatenate([cut(in_one, out_one), small], axis=1),
        jnp.concatenate([cut(in_two, out_two), cut(widen), narrow.reshape(SHARDS, -1, D)], axis=1),
        experts_widen.reshape(SHARDS, -1, FF),
        experts_narrow.reshape(SHARDS, -1, D),
    )
    return [p.reshape((4, 2, 2, 2) + p.shape[1:]) for p in parts]


def all_deltas(*parts):
    w1a, w1b, uw, vw = (p.astype(F32).reshape((SHARDS,) + p.shape[-2:]) for p in parts)

    def join(part):
        return part.reshape(SHARDS, -1, ROWS, D).transpose(0, 2, 1, 3).reshape(D, -1)

    one, two = join(w1a[:, 0:48]), join(w1b[:, 0:48])
    whole = (
        w1a[:: SHARDS // 4, 48], one[:, : 3 * D], one[:, 3 * D :], join(w1b[:, 48:96]), w1b[:, 96:144], w1a[0, 49:53].T,
        two[:, : 3 * D], two[:, 3 * D :], uw, vw,
    )
    return [p.reshape(-1) for p in whole]


def on_device(shards, tokens, cotangent, image_valid, routes, *weights):
    images = tokens.shape[0] * tokens.shape[1]

    def padded(array):
        return jnp.pad(array.reshape(images, SEQ, D), ((0, 0), (0, PAD - SEQ), (0, 0))).reshape(images * PAD, D)

    def cut(array):
        return array.reshape(images, PAD, D)[:, :SEQ].reshape(tokens.shape)

    named = routes.reshape(images, SEQ, 2).transpose(0, 2, 1)
    named = jnp.pad(named, ((0, 0), (0, 6), (0, 2 * LANES - SEQ)))
    data = (padded(tokens), padded(cotangent), image_valid.reshape(images), named)
    if shards == SHARDS:
        gains, in_one, out_one, widen, narrow, router, in_two, out_two, tall_u, tall_v = weights
        flat = [w.reshape(-1, LANES) for w in (in_one, out_one, widen, narrow, in_two, out_two, tall_u, tall_v)]
        small = jnp.pad(jnp.concatenate([gains, router]), (0, LANES - 2 * gains.shape[0]))
        small = jnp.broadcast_to(small[None], (16, LANES))
        out, delta, *sums, small = run_blocks(True, *data, *flat, small)
        sums = [d.reshape(-1) for d in sums]
        share = gains.shape[0]
        deltas = [small[0, :share], *sums[:4], small[0, share : 2 * share], *sums[4:]]
    else:
        whole = [lax.all_gather(w, "fsdp", axis=0, tiled=True) for w in weights]
        out, delta, *sums = run_blocks(False, *data, *all_pieces(*whole))
        deltas = [lax.psum_scatter(d, "fsdp", scatter_dimension=0, tiled=True) for d in all_deltas(*sums)]
    return (cut(out), cut(delta), *deltas)


def solution(mesh):
    split, flat = P(None, "fsdp", None, None), P("fsdp")
    return jax.shard_map(
        functools.partial(on_device, mesh.shape["fsdp"]),
        mesh=mesh,
        in_specs=(split, split, P(None, "fsdp"), split) + (flat,) * 10,
        out_specs=(split, split) + (flat,) * 10,
        check_vma=False,
    )
```

```python
import functools
import math

import jax
import jax.numpy as jnp
import numpy as np
from jax import lax
from jax.experimental import pallas as pl
from jax.experimental.pallas import tpu as pltpu
from jax.sharding import PartitionSpec as P

D = 384
HEADS = 6
HDIM = 64
FF = 1536
EXPERTS = 4
SEQ = 197
PAD = 208
PAIRS = HEADS // 2
SHARDS = 32
ROWS = D // SHARDS
LANES = 128
EPSILON = 1e-06
BF = jnp.bfloat16
F32 = jnp.float32
MESH = pl.DeviceIdType.MESH
C0 = math.sqrt(2.0 / math.pi)
C1 = 0.044715


def dot_nn(a, b):
    return lax.dot_general(a, b, (((1,), (0,)), ((), ())), preferred_element_type=F32)


def dot_nt(a, b):
    return lax.dot_general(a, b, (((1,), (1,)), ((), ())), preferred_element_type=F32)


def dot_tn(a, b):
    return lax.dot_general(a, b, (((0,), (0,)), ((), ())), preferred_element_type=F32)


def normed(x):
    centred = x - jnp.mean(x, axis=-1, keepdims=True)
    rstd = lax.rsqrt(jnp.mean(centred * centred, axis=-1, keepdims=True) + EPSILON)
    return centred * rstd, rstd


def norm_back(x, gain, dhn):
    xhat, rstd = normed(x)
    dxhat = dhn * gain
    mean_d = jnp.mean(dxhat, axis=-1, keepdims=True)
    mean_dx = jnp.mean(dxhat * xhat, axis=-1, keepdims=True)
    return rstd * (dxhat - mean_d - xhat * mean_dx), jnp.sum(dhn * xhat, axis=0, keepdims=True)


def gelu_both(u):
    u2 = u * u
    t = jnp.tanh(u * (C0 + (C0 * C1) * u2))
    h = 0.5 + 0.5 * t
    z = u * h
    return z, h + z * (1.0 - h) * (2.0 * C0 + (6.0 * C0 * C1) * u2)


def rows_of(i, size=PAD):
    return pl.ds(pl.multiple_of(i * size, 16), size)


def loop(count, body, ticks=()):
    def step(i, carry):
        body(i)
        for k, tick in enumerate(ticks):
            pl.when(i == k)(tick)
        return carry

    lax.fori_loop(0, count, step, 0)


def attention_forward(images, x_in, x_out, gain, win, wout, hn_ref, qkv_ref, pb_ref, o_ref, ticks=()):
    low_half = lax.broadcasted_iota(jnp.int32, (PAD, LANES), 1) < HDIM
    real_key = lax.broadcasted_iota(jnp.int32, (2 * PAD, PAD), 1) < SEQ

    def image(i):
        r = rows_of(i)
        x = x_in[r, :].astype(F32)
        xhat, _ = normed(x)
        hn = (xhat * gain).astype(BF)
        hn_ref[r, :] = hn
        for j in range(3):
            cols = pl.ds(D * j, D)
            qkv_ref[r, cols] = dot_nn(hn, win[:, cols]).astype(BF)
        for p in range(PAIRS):
            q2 = qkv_ref[r, pl.ds(LANES * p, LANES)] * jnp.asarray(HDIM ** (-0.5), BF)
            k2 = qkv_ref[r, pl.ds(D + LANES * p, LANES)]
            v2 = qkv_ref[r, pl.ds(2 * D + LANES * p, LANES)]
            zero = jnp.zeros_like(q2)
            qs = jnp.concatenate([jnp.where(low_half, q2, zero), jnp.where(low_half, zero, q2)], axis=0)
            s = dot_nt(qs, k2)
            s = jnp.where(real_key, s, -1e30)
            w = jnp.exp(s - jnp.max(s, axis=-1, keepdims=True))
            soft = w * (1.0 / jnp.sum(w, axis=-1, keepdims=True))
            pb = soft.astype(BF)
            pb_ref[i * PAIRS + p] = pb
            o2 = dot_nn(pb, v2)
            o_ref[r, pl.ds(LANES * p, LANES)] = jnp.where(low_half, o2[:PAD], o2[PAD:]).astype(BF)
        x_out[r, :] = x + dot_nn(o_ref[r, :], wout[...])

    loop(images, image, ticks)


def attention_backward(
    images, b_ref, x_in, gain, win, wout, hn_ref, qkv_ref, pb_ref, o_ref, da_ref, dqkv_ref, dgain_ref, dwin, dwout, ticks=()
):
    low_half = lax.broadcasted_iota(jnp.int32, (PAD, LANES), 1) < HDIM
    dgain_ref[...] = jnp.zeros_like(dgain_ref)

    def image(i):
        r = rows_of(i)
        b = b_ref[r, :]
        da = b.astype(BF)
        da_ref[r, :] = da
        do = dot_nt(da, wout[...]).astype(BF)
        for p in range(PAIRS):
            cols = [pl.ds(D * j + LANES * p, LANES) for j in range(3)]
            q2, k2, v2 = (qkv_ref[r, c] for c in cols)
            do2 = do[:, LANES * p : LANES * (p + 1)]
            zero = jnp.zeros_like(q2)
            qs = jnp.concatenate([jnp.where(low_half, q2, zero), jnp.where(low_half, zero, q2)], axis=0)
            dos = jnp.concatenate([jnp.where(low_half, do2, zero), jnp.where(low_half, zero, do2)], axis=0)
            pb = pb_ref[i * PAIRS + p]
            soft = pb.astype(F32)
            dp = dot_nt(dos, v2)
            ds = (soft * (dp - jnp.sum(dp * soft, axis=-1, keepdims=True))).astype(BF)
            dq = dot_nn(ds, k2) * HDIM ** (-0.5)
            dqkv_ref[r, cols[0]] = jnp.where(low_half, dq[:PAD], dq[PAD:]).astype(BF)
            dqkv_ref[r, cols[1]] = (dot_tn(ds, qs) * HDIM ** (-0.5)).astype(BF)
            dqkv_ref[r, cols[2]] = dot_tn(pb, dos).astype(BF)
        dhn = dot_nt(dqkv_ref[r, pl.ds(0, 3 * D)], win[...])
        dx, dg = norm_back(x_in[r, :].astype(F32), gain, dhn)
        b_ref[r, :] = b + dx
        dgain_ref[...] += dg

    loop(images, image, ticks)
    dwout[...] = dot_tn(o_ref[...], da_ref[...]).astype(BF)
    hn = hn_ref[...]
    for j in range(3):
        cols = pl.ds(D * j, D)
        dwin[:, cols] = dot_tn(hn, dqkv_ref[:, cols]).astype(BF)


def piece_rows(buf, z, row, cols=None):
    block = buf[z, :, :, :, row : row + 48, :]
    return block.reshape(8 * 48, D)


WIDE = 512
HALF = FF // 2


def narrow_half(w1b, h):
    return w1b[2 * h : 2 * h + 2, :, :, :, 96:144, :].reshape(HALF, D)


def gelu_tiles(hn, wide, z_ref, g_ref, r):
    for j in range(FF // WIDE):
        cols = pl.ds(WIDE * j, WIDE)
        z, g = gelu_both(dot_nn(hn, wide(cols)))
        z_ref[r, cols] = z.astype(BF)
        g_ref[r, cols] = g.astype(BF)


def slope_halves(dy, tall, g_ref, r):
    for h in range(2):
        cols = pl.ds(HALF * h, HALF)
        g_ref[r, cols] = (dot_nt(dy, tall(h)) * g_ref[r, cols].astype(F32)).astype(BF)


def tall_delta(dy_t, z_tile):
    return dot_nn(dy_t, z_tile).astype(BF).T


def row_block(images):
    return 2 * PAD if images % 2 == 0 else PAD


def dense_forward(images, x_in, x_out, gain, wid, w1b, hn_ref, z_ref, g_ref, ticks=()):
    size = row_block(images)

    def block(i):
        r = rows_of(i, size)
        x = x_in[r, :]
        hn = (normed(x)[0] * gain).astype(BF)
        hn_ref[r, :] = hn
        gelu_tiles(hn, lambda cols: wid[:, cols], z_ref, g_ref, r)
        tall = w1b[:, :, :, :, 96:144, :].reshape(FF, D)
        x_out[r, :] = x + dot_nn(z_ref[r, :], tall)

    loop(images * PAD // size, block, ticks)


def dense_backward(images, b_ref, x_in, gain, wid, w1b, hn_ref, z_ref, g_ref, da_ref, dgain_ref, dwid, ticks=()):
    size = row_block(images)
    dgain_ref[...] = jnp.zeros_like(dgain_ref)

    def block(i):
        r = rows_of(i, size)
        b = b_ref[r, :]
        da = b.astype(BF)
        da_ref[r, pl.ds(0, D)] = da
        slope_halves(da, lambda h: narrow_half(w1b, h), g_ref, r)
        dhn = dot_nt(g_ref[r, :], wid[...])
        dx, dg = norm_back(x_in[r, :], gain, dhn)
        b_ref[r, :] = b + dx
        dgain_ref[...] += dg

    loop(images * PAD // size, block, ticks)
    hn_t, da_t = hn_ref[...].T, da_ref[...].T
    for j in range(FF // WIDE):
        cols = pl.ds(WIDE * j, WIDE)
        dwid[:, cols] = dot_nn(hn_t, g_ref[:, cols]).astype(BF)
    for h in range(2):
        delta = tall_delta(da_t, z_ref[:, pl.ds(HALF * h, HALF)])
        w1b[2 * h : 2 * h + 2, :, :, :, 96:144, :] = delta.reshape(2, 2, 2, 2, 48, D)


def router_forward(images, x_in, x_out, gain, router, routes_ref, hn_ref, table_ref):
    lane = lax.broadcasted_iota(jnp.int32, (SEQ, LANES), 1) - EXPERTS
    low_lane = lax.broadcasted_iota(jnp.int32, (PAD, LANES), 1) < EXPERTS

    def image(i):
        r = rows_of(i)
        x = x_in[r, :]
        hn = (normed(x)[0] * gain).astype(BF)
        hn_ref[r, :] = hn
        x_out[r, :] = x
        logits = jnp.where(low_lane, dot_nt(hn, router), -1e30)
        w = jnp.exp(logits - jnp.max(logits, axis=-1, keepdims=True))
        probs = w * (1.0 / jnp.sum(w, axis=-1, keepdims=True))
        table_ref[r, :] = probs
        named = routes_ref[i].T
        hot = (lane == named[:SEQ, 0:1]) | (lane == named[:SEQ, 1:2])
        table_ref[pl.ds(pl.multiple_of(i * PAD, 16), SEQ), :] = jnp.where(hot, 1.0, probs[:SEQ])

    loop(images, image)


def expert_step(
    images, e, x_out, cot_ref, dhn_ref, uw, vw, hn_ref, table_ref, z_ref, g_ref, dy_ref, ticks=(), late=(), before=None
):
    size = row_block(images)
    lane = lax.broadcasted_iota(jnp.int32, (size, LANES), 1)

    def u_tile(cols):
        return uw[e, :, :, :, :, cols].reshape(D, -1)

    def v_half(h):
        return vw[e, h].reshape(HALF, D)

    def block(i):
        r = rows_of(i, size)
        hn = hn_ref[r, :]
        gelu_tiles(hn, u_tile, z_ref, g_ref, r)
        y = dot_nn(z_ref[r, :], vw[e].reshape(FF, D))
        table = table_ref[r, :]
        hot = jnp.sum(jnp.where(lane == e + EXPERTS, table, 0.0), axis=-1, keepdims=True)
        gate = hot * jnp.sum(jnp.where(lane == e, table, 0.0), axis=-1, keepdims=True)
        b = cot_ref[r, :].astype(F32)
        x_out[r, :] += gate * y
        dgate = hot * jnp.sum(b * y, axis=-1, keepdims=True)
        table_ref[r, :] = jnp.where(lane == e + 2 * EXPERTS, dgate, table)
        dy = (gate * b).astype(BF)
        dy_ref[r, :] = dy
        slope_halves(dy, v_half, g_ref, r)
        dhn_ref[r, :] += dot_nt(g_ref[r, :], u_tile(pl.ds(0, FF)))

    loop(images * PAD // size, block, ticks)
    if before is not None:
        before()
    hn_t, dy_t = hn_ref[...].T, dy_ref[...].T
    for j in range(FF // WIDE):
        cols = pl.ds(WIDE * j, WIDE)
        uw[e, :, :, :, :, cols] = dot_nn(hn_t, g_ref[:, cols]).astype(BF).reshape(2, 2, 2, 48, WIDE)
    for tick in late:
        tick()
    for h in range(2):
        vw[e, h] = tall_delta(dy_t, z_ref[:, pl.ds(HALF * h, HALF)]).reshape(2, 2, 192, D)


def router_backward(images, b_ref, cot_ref, x_in, gain, router, dhn_ref, table_ref, hn_ref, drouter_ref, dgain_ref, ticks=()):
    dgain_ref[...] = jnp.zeros_like(dgain_ref)
    drouter_ref[...] = jnp.zeros_like(drouter_ref)
    low_lane = lax.broadcasted_iota(jnp.int32, (PAD, LANES), 1) < EXPERTS

    def image(i):
        r = rows_of(i)
        table = table_ref[r, :]
        probs = jnp.where(low_lane, table, 0.0)
        dprobs = pltpu.roll(table, LANES - 2 * EXPERTS, 1)
        dlogits = (probs * (dprobs - jnp.sum(dprobs * probs, axis=-1, keepdims=True))).astype(BF)
        drouter_ref[...] += dot_tn(dlogits, hn_ref[r, :])[:8]
        dhn = dhn_ref[r, :] + dot_nn(dlogits, router)
        dx, dg = norm_back(x_in[r, :], gain, dhn)
        b_ref[r, :] = cot_ref[r, :].astype(F32) + dx
        dgain_ref[...] += dg

    loop(images, image, ticks)


def chunk_spots(matrices):
    return [(m, c) for m in matrices for c in range(m.shape[1] // D)]


def decode(buf, row, matrices):
    spots, perm = chunk_spots(matrices), permutation()

    def group(g):
        full = dot_tn(perm, piece_rows(buf, g, row)).astype(BF)
        r = rows_of(g, 96)
        for k, (m, c) in enumerate(spots):
            m[r, pl.ds(D * c, D)] = full[96 * k : 96 * (k + 1)]

    loop(4, group)


def encode(buf, row, matrices):
    spots, perm = chunk_spots(matrices), permutation()

    def group(g):
        r = rows_of(g, 96)
        parts = jnp.concatenate([m[r, pl.ds(D * c, D)] for m, c in spots], axis=0)
        buf[g, :, :, :, row : row + 48, :] = dot_nn(perm, parts).astype(BF).reshape(2, 2, 2, 48, D)

    loop(4, group)


def decode_small(w1a, gains_ref, router_ref):
    block = w1a[:, :, :, :, 48:64, :].reshape(-1, D)
    spot = lax.broadcasted_iota(jnp.int32, (8, block.shape[0]), 1)
    row = lax.broadcasted_iota(jnp.int32, (8, block.shape[0]), 0)
    pick = (spot % 16 == 0) & (spot // 128 == row)
    gains_ref[...] = dot_nn(jnp.where(pick, 1.0, 0.0).astype(BF), block)
    spot = lax.broadcasted_iota(jnp.int32, (LANES, block.shape[0]), 1)
    row = lax.broadcasted_iota(jnp.int32, (LANES, block.shape[0]), 0)
    pick = (spot % 16 == row + 1) & (row < EXPERTS)
    router_ref[...] = dot_nn(jnp.where(pick, 1.0, 0.0).astype(BF), block).astype(BF)


def encode_small(w1a, gs_ref):
    rest = jnp.zeros((16 - 1 - EXPERTS, D), F32)
    for g in range(4):
        block = jnp.concatenate([gs_ref[pl.ds(g, 1), :], gs_ref[pl.ds(4, EXPERTS), :], rest], axis=0).astype(BF)
        for d in range(8):
            w1a[g, d // 4, d // 2 % 2, d % 2, 48:64, :] = block


def spot_grid(shape):
    return lax.broadcasted_iota(jnp.int32, shape, 0), lax.broadcasted_iota(jnp.int32, shape, 1)


def picked(rows, flat, spot):
    row, col = spot_grid((rows, flat.shape[0]))
    parts = [dot_nn(jnp.where(col == spot(row, k), 1.0, 0.0).astype(BF), flat) for k in range(D // LANES)]
    return jnp.concatenate(parts, axis=1)


def chunk_rows(flat, first, chunks, rows=4 * ROWS):
    wide = chunks * D // LANES

    def spot(row, k):
        c = row // ROWS - first
        inside = (c >= 0) & (c < chunks)
        return jnp.where(inside, wide * (row % ROWS) + D // LANES * c + k, -1)

    return picked(rows, flat, spot)


def assemble_attention(own, row, flat_in, flat_out):
    both = chunk_rows(flat_in[...], 0, 3) + chunk_rows(flat_out[...], 3, 1)
    own[row : row + 4 * ROWS, :] = both.astype(BF)


def small_places(me):
    i, j = spot_grid((LANES, D))
    share = 4 * D // SHARDS
    place = [(i < share) & (j == me % (D // share) * share + i)]
    for e in range(EXPERTS):
        place.append((i >= share) & (i < 2 * share) & (i % EXPERTS == e) & (j == me * ROWS + (i - share) // EXPERTS))
    return [jnp.where(p, 1.0, 0.0) for p in place]


def assemble_small(own, places, flat):
    row, _ = spot_grid((16, D))
    total = jnp.zeros((16, D), F32)
    for q, place in enumerate(places):
        total += jnp.where(row == q, dot_nn(flat, place.astype(BF))[0:1], 0.0)
    own[48:64, :] = total.astype(BF)


def scatter_chunks(stage, row, cols, total, first, chunks):
    wide = chunks * D // LANES
    for c in range(chunks):
        for k in range(D // LANES):
            spots = pl.ds(row + D // LANES * c + k, ROWS, stride=wide)
            stage[spots, cols] = total[ROWS * (first + c) : ROWS * (first + c + 1), LANES * k : LANES * (k + 1)]


def scatter_rows(stage, row, cols, total):
    wide = total.shape[1] // LANES
    for k in range(wide):
        stage[pl.ds(row + k, total.shape[0], stride=wide), cols] = total[:, LANES * k : LANES * (k + 1)]


def permutation():
    k = lax.broadcasted_iota(jnp.int32, (1, D), 1)
    spot = k // ROWS % 8 * (4 * ROWS) + k // (8 * ROWS) * ROWS + k % ROWS
    return jnp.where(lax.broadcasted_iota(jnp.int32, (D, D), 0) == spot, 1.0, 0.0).astype(BF)


class Copy:
    def __init__(self, net, k, ends, mask):
        self.net, self.k, self.ends, self.mask = net, k, ends, mask

    def make(self):
        src, dst = self.ends()
        return pltpu.make_async_remote_copy(
            src_ref=src, dst_ref=dst, send_sem=self.net.send_sem.at[self.k], recv_sem=self.net.recv_sem.at[self.k],
            device_id=(self.net.partner(self.mask),), device_id_type=MESH)

    def start(self):
        self.make().start()

    def wait_recv(self):
        self.make().wait_recv()

    def wait_send(self):
        self.make().wait_send()


class Net:
    masks = (1, 2, 4, 8, 16, 24)

    def __init__(self, send_sem, recv_sem):
        self.send_sem, self.recv_sem, self.count = send_sem, recv_sem, 0
        me = self.me = lax.axis_index("fsdp")
        self.c, self.x, self.y, self.z = me % 2, me // 2 % 2, me // 4 % 2, me // 8
        self.zs = [self.flip_z(d) for d in range(4)]
        self.partners = {m: self.partner_of(m) for m in self.masks}

    def partner(self, mask):
        return self.partners[mask]

    def partner_of(self, mask):
        c = 1 - self.c if mask & 1 else self.c
        x = 1 - self.x if mask & 2 else self.x
        y = 1 - self.y if mask & 4 else self.y
        return self.zs[mask >> 3] * 8 + y * 4 + x * 2 + c

    def flip_z(self, d):
        lo, hi = self.z % 2, self.z // 2
        lo = 1 - lo if d & 1 else lo
        hi = 1 - hi if d & 2 else hi
        return hi * 2 + lo

    def barrier(self):
        sem = pltpu.get_barrier_semaphore()
        for m in self.masks:
            pl.semaphore_signal(sem, inc=1, device_id=(self.partner(m),), device_id_type=MESH)
        pl.semaphore_wait(sem, len(self.masks))

    def copy(self, ends, mask):
        k = self.count
        self.count += 1
        return Copy(self, k, ends, mask)


def halves(rows, w):
    if w == D:
        cut = (rows // 32 + 1) * 16 if rows % 32 else rows // 2
        return (pl.ds(0, cut), pl.ds(0, w)), (pl.ds(cut, rows - cut), pl.ds(0, w))
    return (pl.ds(0, rows), pl.ds(0, w // 2)), (pl.ds(0, rows), pl.ds(w // 2, w // 2))


class Gather:
    def __init__(self, net, buf):
        x, y, c = net.x, net.y, net.c
        a, b = halves(*buf.shape[-2:])

        def copy(d, yy, xx, half, mask):
            def ends():
                ref = buf.at[net.zs[d], yy, xx, c]
                ref = ref if half is None else ref.at[half[0], half[1]]
                return ref, ref

            return net.copy(ends, mask)

        def pair(d):
            def ends():
                ref = buf.at[net.zs[d], :, :, c]
                return ref, ref

            return net.copy(ends, 1)

        slots = range(4)
        self.along_z = [None] + [copy(0, y, x, None, d << 3) for d in (1, 2, 3)]
        self.to_y = [copy(d, y, x, a, 4) for d in slots]
        self.to_x = [copy(d, y, x, b, 2) for d in slots]
        self.own_x = [copy(d, y, x, a, 2) for d in slots]
        self.own_y = [copy(d, y, x, b, 4) for d in slots]
        self.far_x = [copy(d, 1 - y, x, a, 2) for d in slots]
        self.far_y = [copy(d, y, 1 - x, b, 4) for d in slots]
        self.pair = [pair(d) for d in slots]

    def send_z(self, d):
        self.along_z[d].start()

    def plane(self, d):
        if d:
            self.along_z[d].wait_recv()
        self.to_y[d].start()
        self.to_x[d].start()
        self.own_x[d].start()
        self.own_y[d].start()

    def across(self, d):
        self.to_y[d].wait_recv()
        self.far_x[d].start()
        self.to_x[d].wait_recv()
        self.far_y[d].start()

    def core(self, d):
        for copy in (self.own_x, self.own_y, self.far_x, self.far_y):
            copy[d].wait_recv()
        self.pair[d].start()

    def here(self, d):
        self.pair[d].wait_recv()

    def sent(self, d):
        for copy in (self.to_y, self.to_x, self.own_x, self.own_y, self.far_x, self.far_y, self.pair):
            copy[d].wait_send()
        if d == 0:
            for k in (1, 2, 3):
                self.along_z[k].wait_send()


class Reduce:
    def __init__(self, net, part, slots, bufs, r4):
        self.net, self.part, self.slots, self.r4 = net, part, slots, r4
        self.recv1, self.r2a, self.r2b, self.r3a, self.r3b = bufs
        x, y, c = net.x, net.y, net.c
        self.a, self.b = halves(*part.shape[-2:])
        planes = pl.ds(0, 4) if len(slots) == 4 else pl.ds(net.zs[slots[0]], 1)
        self.planes = range(4) if len(slots) == 4 else [net.zs[slots[0]]]
        a, b = self.a, self.b

        def one(yy, xx):
            return net.copy(lambda: (part.at[planes, yy, xx, 1 - c], self.recv1.at[:, yy, xx]), 1)

        self.s1 = {(fy, fx): one(1 - y if fy else y, 1 - x if fx else x) for fx in (1, 0) for fy in (1, 0)}

        def two_a(yy):
            return net.copy(lambda: (part.at[planes, yy, 1 - x, c, a[0], a[1]], self.r2a.at[:, yy]), 2)

        def two_b(xx):
            return net.copy(lambda: (part.at[planes, 1 - y, xx, c, b[0], b[1]], self.r2b.at[:, xx]), 4)

        self.s2a = [two_a(1 - y), two_a(y)]
        self.s2b = [two_b(1 - x), two_b(x)]
        self.s3a = net.copy(lambda: (part.at[planes, 1 - y, x, c, a[0], a[1]], self.r3a), 4)
        self.s3b = net.copy(lambda: (part.at[planes, y, 1 - x, c, b[0], b[1]], self.r3b), 2)

        def four(d):
            return net.copy(lambda: (part.at[net.zs[d], y, x, c], r4.at[d - 1]), d << 3)

        self.s4 = {d: four(d) for d in slots if d}

    def add(self, ref, other):
        ref[...] = (ref[...].astype(F32) + other[...].astype(F32)).astype(BF)

    def one(self):
        for copy in self.s1.values():
            copy.start()

    def two(self):
        net = self.net
        x, y, c = net.x, net.y, net.c

        def add_all(fy, fx):
            self.s1[fy, fx].wait_recv()
            yy, xx = (1 - y if fy else y), (1 - x if fx else x)
            for k, z in enumerate(self.planes):
                self.add(self.part.at[z, yy, xx, c], self.recv1.at[k, yy, xx])

        add_all(1, 1)
        self.s2a[0].start()
        self.s2b[0].start()
        add_all(0, 1)
        self.s2a[1].start()
        add_all(1, 0)
        self.s2b[1].start()
        add_all(0, 0)

    def three(self):
        net = self.net
        x, y, c = net.x, net.y, net.c
        a, b = self.a, self.b

        def add_half(yy, xx, half, buf, spot):
            for k, z in enumerate(self.planes):
                self.add(self.part.at[z, yy, xx, c, half[0], half[1]], buf.at[k, spot])

        self.s2a[0].wait_recv()
        add_half(1 - y, x, a, self.r2a, 1 - y)
        self.s3a.start()
        self.s2b[0].wait_recv()
        add_half(y, 1 - x, b, self.r2b, 1 - x)
        self.s3b.start()
        self.s2a[1].wait_recv()
        add_half(y, x, a, self.r2a, y)
        self.s2b[1].wait_recv()
        add_half(y, x, b, self.r2b, x)

    def four(self):
        net = self.net
        x, y, c = net.x, net.y, net.c
        for copy, half, buf in ((self.s3a, self.a, self.r3a), (self.s3b, self.b, self.r3b)):
            copy.wait_recv()
            for k, z in enumerate(self.planes):
                self.add(self.part.at[z, y, x, c, half[0], half[1]], buf.at[k])
        for copy in self.s4.values():
            copy.start()

    def sent(self):
        for copy in [*self.s1.values(), *self.s2a, *self.s2b, self.s3a, self.s3b, *self.s4.values()]:
            copy.wait_send()


def summed(net, part, reduces, r4):
    total = part[net.z, net.y, net.x, net.c].astype(F32)
    for job in reduces:
        for d, copy in job.s4.items():
            copy.wait_recv()
            total += r4[d - 1].astype(F32)
    return total


def reduce_buffers(rows, w, planes):
    a, b = halves(rows, w)
    sa, sb = (a[0].size, a[1].size), (b[0].size, b[1].size)
    shapes = [(planes, 2, 2, rows, w), (planes, 2) + sa, (planes, 2) + sb, (planes,) + sa, (planes,) + sb]
    return [pltpu.VMEM(s, BF) for s in shapes]


def block_kernel(remote, names, *refs):
    r = dict(zip(names, refs))
    images = r["tok"].shape[0] // PAD
    w1a, w1b, uw, vw = arrays = [r[k] for k in ("w1a", "w1b", "uw", "vw")]
    sem = r["sem"]
    cot_load = pltpu.make_async_copy(r["cot"], r["cotv"], sem.at[4])
    cot_load.start()
    x0 = r["hn4"]
    tok_load = pltpu.make_async_copy(r["tok"], x0, sem.at[6])
    tok_load.start()

    if remote:
        net = Net(r["send_sem"], r["recv_sem"])
        own = [buf.at[net.z, net.y, net.x, net.c] for buf in arrays]
        tall = [r["ge"].at[pl.ds(0, r[name].shape[0]), pl.ds(LANES * k, LANES)] for k, name in enumerate(FLAT[-2:])]
        loads = [pltpu.make_async_copy(r[name], ref, sem.at[k]) for k, (name, ref) in enumerate(zip(FLAT[-2:], tall))]
        for copy in loads:
            copy.start()
        places = small_places(net.me)
        assemble_attention(own[0], 0, r["in_one"], r["out_one"])
        assemble_small(own[0], places, r["small"][...])
        net.barrier()
        ga, gb, gu, gv = [Gather(net, buf) for buf in arrays]
        experts = [net.zs[d] for d in range(4)]
        for d in (1, 2, 3):
            ga.send_z(d)
        ga.plane(0)
        assemble_attention(own[1], 0, r["in_two"], r["out_two"])
        own[1][48:96, :] = chunk_rows(r["widen"][...], 0, 4).astype(BF)
        own[1][96:144, :] = picked(48, r["narrow"][...], lambda row, k: 3 * row + k).astype(BF)
    else:
        loads = [
            pltpu.make_async_copy(r[k + "_in"], buf, sem.at[j])
            for j, (k, buf) in enumerate(zip(("w1a", "w1b", "uw", "vw"), arrays))
        ]
        for copy in loads:
            copy.start()
        experts = range(4)
    x1, x2, x3, b, dhn = (r[k] for k in ("x1", "x2", "x3", "b", "dhn"))
    x4 = b
    valid, cot = r["valid"], r["cotv"]
    cot_load.wait()
    tok_load.wait()
    for i in range(images):
        rows = pl.ds(PAD * i, PAD)
        cot[rows, :] = (cot[rows, :].astype(F32) * valid[i].astype(F32)).astype(BF)
    dhn[...] = jnp.zeros_like(dhn)
    table = r["table"]
    win1, wout1, wid1, win2, wout2 = (r[k] for k in ("win1", "wout1", "wid1", "win2", "wout2"))

    def none():
        return None

    def batch(*steps):
        def tick():
            for step in steps:
                step()

        return tick if remote else none

    def both(step, d):
        return batch(lambda: getattr(gu, step)(d), lambda: getattr(gv, step)(d))

    if remote:
        ga.across(0)
        for d in (1, 2, 3):
            ga.plane(d)
        for d in (1, 2, 3):
            gb.send_z(d)
        gb.plane(0)
        for d in (1, 2, 3):
            ga.across(d)
        for d in range(4):
            ga.core(d)
        gb.across(0)
        gb.plane(1)
        for copy in loads:
            copy.wait()
        for j in range(FF // D):
            own[2][:, pl.ds(D * j, D)] = picked(48, tall[0][...], lambda row, k: 12 * row + 3 * j + k).astype(BF)
        own[3][...] = picked(192, tall[1][...], lambda row, k: 3 * row + k).astype(BF)
        both("send_z", 1)()
        both("send_z", 2)()
        for d in range(4):
            ga.here(d)
        gb.plane(2)
        gb.plane(3)
    else:
        loads[0].wait()

    decode(w1a, 0, (win1, wout1))
    decode_small(w1a, r["gains"], r["router"])
    gains = [r["gains"][pl.ds(k, 1), :] for k in range(4)]
    router = r["router"][...]
    ticks = [
        batch(lambda: gb.across(1), lambda: gb.across(2), lambda: gb.across(3), both("plane", 0)),
        batch(lambda: gb.core(0), lambda: gb.core(1), lambda: gb.core(2)),
        batch(lambda: gb.core(3), both("send_z", 3)),
        batch(both("across", 0)),
    ]
    attention_forward(images, x0, x1, gains[0], win1, wout1, r["hn1"], r["qkv1"], r["pb1"], r["o1"], ticks)
    if remote:
        for d in range(4):
            gb.here(d)
    else:
        loads[1].wait()
    decode(w1b, 48, (wid1,))
    decode(w1b, 0, (win2, wout2))
    ticks = [both("plane", 1), both("core", 0)]
    dense_forward(images, x1, x2, gains[1], wid1, w1b, r["hn2"], r["z1"], r["g1"], ticks)
    ticks = [none, both("across", 1), none, both("plane", 2)]
    attention_forward(images, x2, x3, gains[2], win2, wout2, r["hn3"], r["qkv2"], r["pb2"], r["o2"], ticks)
    router_forward(images, x3, x4, gains[3], router, r["routes"], r["hn4"], table)

    if remote:
        buffers = iter(r["rs"])
        take = lambda: [next(buffers) for _ in range(5)]
        bufs_u, bufs_v = [take(), take()], [take(), take()]
        ru = [Reduce(net, uw, [d], bufs_u[d % 2], r["r4u"]) for d in range(4)]
        rv = [Reduce(net, vw, [d], bufs_v[d % 2], r["r4v"]) for d in range(4)]
        rb = Reduce(net, w1b, [0, 1, 2, 3], take(), r["r4b"])
        ra = Reduce(net, w1a, [0, 1, 2, 3], take(), r["r4a"])
    else:
        loads[2].wait()
        loads[3].wait()

    def reduce_step(step, d):
        return batch(lambda: getattr(ru[d], step)(), lambda: getattr(rv[d], step)())

    def run_expert(d, ticks, late):
        if remote:
            gu.here(d)
            gv.here(d)
        before = batch(lambda: gu.sent(d), lambda: gv.sent(d))
        late = [*late, batch(lambda: ru[d].one())]
        expert_step(
            images, experts[d], x4, cot, dhn, uw, vw, r["hn4"], table, r["ze"], r["ge"], r["dy"], ticks, late, before
        )
        batch(lambda: rv[d].one())()

    both("core", 1)()
    run_expert(0, [both("across", 2), both("plane", 3)], [both("core", 2)])
    both("across", 3)()
    run_expert(1, [reduce_step("two", 0), both("core", 3)], [])
    reduce_step("three", 0)()
    run_expert(2, [reduce_step("two", 1), reduce_step("four", 0)], [])
    reduce_step("three", 1)()
    run_expert(3, [reduce_step("two", 2), reduce_step("four", 1)], [])
    reduce_step("three", 2)()
    out_cols = pl.ds(0, D)
    for i in range(images):
        rows = pl.ds(PAD * i, PAD)
        r["ge"][rows, out_cols] = (x4[rows, :] * valid[i].astype(F32)).astype(BF)
    out_store = pltpu.make_async_copy(r["ge"].at[:, out_cols], r["out"], sem.at[5])
    out_store.start()
    gs, dgain, drouter = r["gs"], r["dgain"], r["drouter"]
    gs[...] = jnp.zeros_like(gs)
    router_backward(images, b, cot, x3, gains[3], router, dhn, table, r["hn4"], drouter, dgain)
    tok_load.start()
    gs[pl.ds(4, EXPERTS), :] = drouter[pl.ds(0, EXPERTS), :]
    gs[pl.ds(3, 1), :] = dgain[...]
    dqkv, da = r["ze"], r["dy"]
    ticks = [reduce_step("two", 3), reduce_step("four", 2), reduce_step("three", 3)]
    attention_backward(images, b, x2, gains[2], win2, wout2, r["hn3"], r["qkv2"], r["pb2"], r["o2"], da, dqkv, dgain, win2, wout2, ticks)
    gs[pl.ds(2, 1), :] = dgain[...]
    batch(*(lambda d=d: gb.sent(d) for d in range(4)))()
    encode(w1b, 0, (win2, wout2))
    ticks = [reduce_step("four", 3)]
    dense_backward(images, b, x1, gains[1], wid1, w1b, r["hn2"], r["z1"], r["g1"], da, dgain, wid1, ticks)
    gs[pl.ds(1, 1), :] = dgain[...]
    encode(w1b, 48, (wid1,))
    if remote:
        rb.one()
    lanes = pl.ds(0, LANES)

    def leave(name, row, k):
        flat = r[name + "_out"]
        return pltpu.make_async_copy(table.at[pl.ds(row, flat.shape[0]), :], flat, sem.at[k])

    def tall_sum():
        scatter_rows(table, 0, lanes, summed(net, vw, rv, r["r4v"]))
        leave("tall_v", 0, 7).start()

    tok_load.wait()
    ticks = [batch(lambda: rb.two()), none, batch(lambda: rb.three()), batch(tall_sum, lambda: rb.four())]
    attention_backward(images, b, x0, gains[0], win1, wout1, r["hn1"], r["qkv1"], r["pb1"], r["o1"], da, dqkv, dgain, win1, wout1, ticks)
    gs[pl.ds(0, 1), :] = dgain[...]
    batch(*(lambda d=d: ga.sent(d) for d in range(4)))()
    encode(w1a, 0, (win1, wout1))
    encode_small(w1a, gs)
    if remote:
        ra.one()
    r["o1"][...] = b[...].astype(BF)
    delta_store = pltpu.make_async_copy(r["o1"], r["dtok"], sem.at[6])
    delta_store.start()
    if remote:
        leave("tall_v", 0, 7).wait()
        scatter_rows(table, 0, lanes, summed(net, uw, ru, r["r4u"]))
        leave("tall_u", 0, 8).start()
        ra.two()
        total = summed(net, w1b, [rb], r["r4b"])
        scatter_chunks(r["in_two_out"], 0, lanes, total, 0, 3)
        scatter_chunks(r["out_two_out"], 0, lanes, total, 3, 1)
        scatter_chunks(table, 576, lanes, total, 4, 4)
        leave("widen", 576, 9).start()
        scatter_rows(r["narrow_out"], 0, lanes, total[96:144])
        ra.three()
        ra.four()
        total = summed(net, w1a, [ra], r["r4a"])
        scatter_chunks(r["in_one_out"], 0, lanes, total, 0, 3)
        scatter_chunks(r["out_one_out"], 0, lanes, total, 3, 1)
        exact = dict(precision=lax.Precision.HIGHEST, preferred_element_type=F32)
        small = jnp.zeros((8, LANES), F32)
        for q, place in enumerate(places):
            line = jnp.broadcast_to(total[48 + q : 49 + q], (8, D))
            small += lax.dot_general(line, place, (((1,), (1,)), ((), ())), **exact)
        r["small_out"][...] = small
        leave("tall_u", 0, 8).wait()
        leave("widen", 576, 9).wait()
        for job in (*ru, *rv, rb, ra):
            job.sent()
    else:
        stores = [
            pltpu.make_async_copy(buf, r[k + "_out"], sem.at[j])
            for j, (k, buf) in enumerate(zip(("w1a", "w1b", "uw", "vw"), arrays))
        ]
        for copy in stores:
            copy.start()
        for copy in stores:
            copy.wait()
    out_store.wait()
    delta_store.wait()


PIECES = ((64, D), (144, D), (48, FF), (192, D))
AWAY = ("widen", "tall_u", "tall_v")
FLAT = ("in_one", "out_one", "widen", "narrow", "in_two", "out_two", "tall_u", "tall_v")


def run_blocks(remote, tok, cot, valid, routes, *weights):
    t = tok.shape[0]
    images = t // PAD
    v = pltpu.VMEM
    vmem, smem, hbm = (pl.BlockSpec(memory_space=m) for m in (pltpu.VMEM, pltpu.SMEM, pl.ANY))
    whole = [(4, 2, 2, 2) + s for s in PIECES]
    inputs = dict(
        tok=(tok, hbm), cot=(cot, hbm), valid=(valid, smem), routes=(routes, vmem),
    )
    if remote:
        inputs.update({name: (w, hbm if name in FLAT[-2:] else vmem) for name, w in zip((*FLAT, "small"), weights)})
    else:
        inputs.update({name + "_in": (w, hbm) for name, w in zip(("w1a", "w1b", "uw", "vw"), weights)})
    flat = jax.ShapeDtypeStruct(tok.shape, BF)
    outputs = dict(out=(flat, hbm), dtok=(flat, hbm))
    if remote:
        for name, w in zip(FLAT, weights):
            outputs[name + "_out"] = (jax.ShapeDtypeStruct(w.shape, F32), hbm if name in AWAY else vmem)
        outputs["small_out"] = (jax.ShapeDtypeStruct((8, LANES), F32), vmem)
    else:
        for name, full in zip(("w1a", "w1b", "uw", "vw"), whole):
            outputs[name + "_out"] = (jax.ShapeDtypeStruct(full, BF), hbm)
    scratch = dict(
        w1a=v(whole[0], BF), w1b=v(whole[1], BF), uw=v(whole[2], BF), vw=v(whole[3], BF),
        win1=v((D, 3 * D), BF), wout1=v((D, D), BF), wid1=v((D, FF), BF), win2=v((D, 3 * D), BF), wout2=v((D, D), BF),
        x1=v((t, D), F32), x2=v((t, D), F32), x3=v((t, D), F32), b=v((t, D), F32), dhn=v((t, D), F32),
        hn1=v((t, D), BF), hn2=v((t, D), BF), hn3=v((t, D), BF), hn4=v((t, D), BF),
        qkv1=v((t, 3 * D), BF), qkv2=v((t, 3 * D), BF), o1=v((t, D), BF), o2=v((t, D), BF),
        pb1=v((images * PAIRS, 2 * PAD, PAD), BF), pb2=v((images * PAIRS, 2 * PAD, PAD), BF),
        z1=v((t, FF), BF), g1=v((t, FF), BF), ze=v((t, FF), BF), ge=v((t, FF), BF), dy=v((t, D), BF), cotv=v((t, D), BF),
        table=v((t, LANES), F32),
        drouter=v((8, D), F32), dgain=v((1, D), F32), gs=v((16, D), F32), gains=v((8, D), F32), router=v((LANES, D), BF),
        sem=pltpu.SemaphoreType.DMA((16,)),
    )
    if remote:
        scratch["rs"] = [
            spec
            for piece, planes in [(PIECES[2], 1)] * 2 + [(PIECES[3], 1)] * 2 + [(PIECES[1], 4), (PIECES[0], 4)]
            for spec in reduce_buffers(*piece, planes)
        ]
        for k, piece in zip("abuv", PIECES):
            scratch["r4" + k] = v((3,) + piece, BF)
        scratch["send_sem"] = pltpu.SemaphoreType.DMA((256,))
        scratch["recv_sem"] = pltpu.SemaphoreType.DMA((256,))
    names = (*inputs, *outputs, *scratch)
    params = dict(collective_id=0, has_side_effects=True) if remote else {}
    return pl.pallas_call(
        functools.partial(block_kernel, remote, names),
        out_shape=tuple(o[0] for o in outputs.values()),
        in_specs=[i[1] for i in inputs.values()],
        out_specs=tuple(o[1] for o in outputs.values()),
        scratch_shapes=list(scratch.values()),
        compiler_params=pltpu.CompilerParams(vmem_limit_bytes=127 * 2**19, **params),
    )(*[i[0] for i in inputs.values()])


def all_pieces(norm_gains, in_one, out_one, widen, narrow, router, in_two, out_two, experts_widen, experts_narrow):
    def cut(*matrices):
        side = jnp.concatenate([m.reshape(D, -1) for m in matrices], axis=1)
        return side.reshape(SHARDS, ROWS, -1, D).transpose(0, 2, 1, 3).reshape(SHARDS, -1, D)

    small = jnp.zeros((SHARDS, 16, D), BF)
    small = small.at[:: SHARDS // 4, 0].set(norm_gains.reshape(4, D))
    small = small.at[0, 1 : 1 + EXPERTS].set(router.reshape(D, EXPERTS).T)
    parts = (
        jnp.concatenate([cut(in_one, out_one), small], axis=1),
        jnp.concatenate([cut(in_two, out_two), cut(widen), narrow.reshape(SHARDS, -1, D)], axis=1),
        experts_widen.reshape(SHARDS, -1, FF),
        experts_narrow.reshape(SHARDS, -1, D),
    )
    return [p.reshape((4, 2, 2, 2) + p.shape[1:]) for p in parts]


def all_deltas(*parts):
    w1a, w1b, uw, vw = (p.astype(F32).reshape((SHARDS,) + p.shape[-2:]) for p in parts)

    def join(part):
        return part.reshape(SHARDS, -1, ROWS, D).transpose(0, 2, 1, 3).reshape(D, -1)

    one, two = join(w1a[:, 0:48]), join(w1b[:, 0:48])
    whole = (
        w1a[:: SHARDS // 4, 48], one[:, : 3 * D], one[:, 3 * D :], join(w1b[:, 48:96]), w1b[:, 96:144], w1a[0, 49:53].T,
        two[:, : 3 * D], two[:, 3 * D :], uw, vw,
    )
    return [p.reshape(-1) for p in whole]


def on_device(shards, tokens, cotangent, image_valid, routes, *weights):
    images = tokens.shape[0] * tokens.shape[1]

    def padded(array):
        return jnp.pad(array, ((0, 0), (0, 0), (0, PAD - SEQ), (0, 0))).reshape(images * PAD, D)

    def cut(array):
        return array.reshape(tokens.shape[:2] + (PAD, D))[:, :, :SEQ]

    named = routes.reshape(images, SEQ, 2).transpose(0, 2, 1)
    named = jnp.pad(named, ((0, 0), (0, 6), (0, 2 * LANES - SEQ)))
    data = (padded(tokens), padded(cotangent), image_valid.reshape(images), named)
    if shards == SHARDS:
        gains, in_one, out_one, widen, narrow, router, in_two, out_two, tall_u, tall_v = weights
        flat = [w.reshape(-1, LANES) for w in (in_one, out_one, widen, narrow, in_two, out_two, tall_u, tall_v)]
        small = jnp.pad(jnp.concatenate([gains, router]), (0, LANES - 2 * gains.shape[0]))
        small = jnp.broadcast_to(small[None], (16, LANES))
        out, delta, *sums, small = run_blocks(True, *data, *flat, small)
        sums = [d.reshape(-1) for d in sums]
        share = gains.shape[0]
        deltas = [small[0, :share], *sums[:4], small[0, share : 2 * share], *sums[4:]]
    else:
        whole = [lax.all_gather(w, "fsdp", axis=0, tiled=True) for w in weights]
        out, delta, *sums = run_blocks(False, *data, *all_pieces(*whole))
        deltas = [lax.psum_scatter(d, "fsdp", scatter_dimension=0, tiled=True) for d in all_deltas(*sums)]
    return (cut(out), cut(delta), *deltas)


def solution(mesh):
    split, flat = P(None, "fsdp", None, None), P("fsdp")
    return jax.shard_map(
        functools.partial(on_device, mesh.shape["fsdp"]),
        mesh=mesh,
        in_specs=(split, split, P(None, "fsdp"), split) + (flat,) * 10,
        out_specs=(split, split) + (flat,) * 10,
        check_vma=False,
    )
```

```python
import functools
import math

import jax
import jax.numpy as jnp
import numpy as np
from jax import lax
from jax.experimental import pallas as pl
from jax.experimental.pallas import tpu as pltpu
from jax.sharding import PartitionSpec as P

D = 384
HEADS = 6
HDIM = 64
FF = 1536
EXPERTS = 4
SEQ = 197
PAD = 208
PAIRS = HEADS // 2
SHARDS = 32
ROWS = D // SHARDS
LANES = 128
EPSILON = 1e-06
BF = jnp.bfloat16
F32 = jnp.float32
MESH = pl.DeviceIdType.MESH
C0 = math.sqrt(2.0 / math.pi)
C1 = 0.044715


def dot_nn(a, b):
    return lax.dot_general(a, b, (((1,), (0,)), ((), ())), preferred_element_type=F32)


def dot_nt(a, b):
    return lax.dot_general(a, b, (((1,), (1,)), ((), ())), preferred_element_type=F32)


def dot_tn(a, b):
    return lax.dot_general(a, b, (((0,), (0,)), ((), ())), preferred_element_type=F32)


def normed(x):
    centred = x - jnp.mean(x, axis=-1, keepdims=True)
    rstd = lax.rsqrt(jnp.mean(centred * centred, axis=-1, keepdims=True) + EPSILON)
    return centred * rstd, rstd


def norm_back(x, gain, dhn):
    xhat, rstd = normed(x)
    dxhat = dhn * gain
    mean_d = jnp.mean(dxhat, axis=-1, keepdims=True)
    mean_dx = jnp.mean(dxhat * xhat, axis=-1, keepdims=True)
    return rstd * (dxhat - mean_d - xhat * mean_dx), jnp.sum(dhn * xhat, axis=0, keepdims=True)


def gelu_both(u):
    u2 = u * u
    t = jnp.tanh(u * (C0 + (C0 * C1) * u2))
    h = 0.5 + 0.5 * t
    z = u * h
    return z, h + z * (1.0 - h) * (2.0 * C0 + (6.0 * C0 * C1) * u2)


def rows_of(i, size=PAD):
    return pl.ds(pl.multiple_of(i * size, 16), size)


def loop(count, body, ticks=()):
    def step(i, carry):
        body(i)
        for k, tick in enumerate(ticks):
            pl.when(i == k)(tick)
        return carry

    lax.fori_loop(0, count, step, 0)


def attention_forward(images, x_in, x_out, gain, win, wout, hn_ref, qkv_ref, pb_ref, o_ref, ticks=()):
    low_half = lax.broadcasted_iota(jnp.int32, (PAD, LANES), 1) < HDIM
    real_key = lax.broadcasted_iota(jnp.int32, (2 * PAD, PAD), 1) < SEQ

    def image(i):
        r = rows_of(i)
        x = x_in[r, :].astype(F32)
        xhat, _ = normed(x)
        hn = (xhat * gain).astype(BF)
        hn_ref[r, :] = hn
        for j in range(3):
            cols = pl.ds(D * j, D)
            qkv_ref[r, cols] = dot_nn(hn, win[:, cols]).astype(BF)
        for p in range(PAIRS):
            q2 = qkv_ref[r, pl.ds(LANES * p, LANES)] * jnp.asarray(HDIM ** (-0.5), BF)
            k2 = qkv_ref[r, pl.ds(D + LANES * p, LANES)]
            v2 = qkv_ref[r, pl.ds(2 * D + LANES * p, LANES)]
            zero = jnp.zeros_like(q2)
            qs = jnp.concatenate([jnp.where(low_half, q2, zero), jnp.where(low_half, zero, q2)], axis=0)
            s = dot_nt(qs, k2)
            s = jnp.where(real_key, s, -1e30)
            w = jnp.exp(s - jnp.max(s, axis=-1, keepdims=True))
            soft = w * (1.0 / jnp.sum(w, axis=-1, keepdims=True))
            pb = soft.astype(BF)
            pb_ref[i * PAIRS + p] = pb
            o2 = dot_nn(pb, v2)
            o_ref[r, pl.ds(LANES * p, LANES)] = jnp.where(low_half, o2[:PAD], o2[PAD:]).astype(BF)
        x_out[r, :] = x + dot_nn(o_ref[r, :], wout[...])

    loop(images, image, ticks)


def attention_backward(
    images, b_ref, x_in, gain, win, wout, hn_ref, qkv_ref, pb_ref, o_ref, da_ref, dqkv_ref, dgain_ref, dwin, dwout, ticks=()
):
    low_half = lax.broadcasted_iota(jnp.int32, (PAD, LANES), 1) < HDIM
    dgain_ref[...] = jnp.zeros_like(dgain_ref)

    def image(i):
        r = rows_of(i)
        b = b_ref[r, :]
        da = b.astype(BF)
        da_ref[r, :] = da
        do = dot_nt(da, wout[...]).astype(BF)
        for p in range(PAIRS):
            cols = [pl.ds(D * j + LANES * p, LANES) for j in range(3)]
            q2, k2, v2 = (qkv_ref[r, c] for c in cols)
            do2 = do[:, LANES * p : LANES * (p + 1)]
            zero = jnp.zeros_like(q2)
            qs = jnp.concatenate([jnp.where(low_half, q2, zero), jnp.where(low_half, zero, q2)], axis=0)
            dos = jnp.concatenate([jnp.where(low_half, do2, zero), jnp.where(low_half, zero, do2)], axis=0)
            pb = pb_ref[i * PAIRS + p]
            soft = pb.astype(F32)
            dp = dot_nt(dos, v2)
            ds = (soft * (dp - jnp.sum(dp * soft, axis=-1, keepdims=True))).astype(BF)
            dq = dot_nn(ds, k2) * HDIM ** (-0.5)
            dqkv_ref[r, cols[0]] = jnp.where(low_half, dq[:PAD], dq[PAD:]).astype(BF)
            dqkv_ref[r, cols[1]] = (dot_tn(ds, qs) * HDIM ** (-0.5)).astype(BF)
            dqkv_ref[r, cols[2]] = dot_tn(pb, dos).astype(BF)
        dhn = dot_nt(dqkv_ref[r, pl.ds(0, 3 * D)], win[...])
        dx, dg = norm_back(x_in[r, :].astype(F32), gain, dhn)
        b_ref[r, :] = b + dx
        dgain_ref[...] += dg

    loop(images, image, ticks)
    dwout[...] = dot_tn(o_ref[...], da_ref[...]).astype(BF)
    hn = hn_ref[...]
    for j in range(3):
        cols = pl.ds(D * j, D)
        dwin[:, cols] = dot_tn(hn, dqkv_ref[:, cols]).astype(BF)


def piece_rows(buf, z, row, cols=None):
    block = buf[z, :, :, :, row : row + 48, :]
    return block.reshape(8 * 48, D)


WIDE = 512
HALF = FF // 2


def narrow_half(w1b, h):
    return w1b[2 * h : 2 * h + 2, :, :, :, 96:144, :].reshape(HALF, D)


def gelu_tiles(hn, wide, z_ref, g_ref, r):
    for j in range(FF // WIDE):
        cols = pl.ds(WIDE * j, WIDE)
        z, g = gelu_both(dot_nn(hn, wide(cols)))
        z_ref[r, cols] = z.astype(BF)
        g_ref[r, cols] = g.astype(BF)


def slope_halves(dy, tall, g_ref, r):
    for h in range(2):
        cols = pl.ds(HALF * h, HALF)
        g_ref[r, cols] = (dot_nt(dy, tall(h)) * g_ref[r, cols].astype(F32)).astype(BF)


def tall_delta(dy_t, z_tile):
    return dot_nn(dy_t, z_tile).astype(BF).T


def row_block(images):
    return 2 * PAD if images % 2 == 0 else PAD


def dense_forward(images, x_in, x_out, gain, wid, w1b, hn_ref, z_ref, g_ref, ticks=()):
    size = row_block(images)

    def block(i):
        r = rows_of(i, size)
        x = x_in[r, :]
        hn = (normed(x)[0] * gain).astype(BF)
        hn_ref[r, :] = hn
        gelu_tiles(hn, lambda cols: wid[:, cols], z_ref, g_ref, r)
        tall = w1b[:, :, :, :, 96:144, :].reshape(FF, D)
        x_out[r, :] = x + dot_nn(z_ref[r, :], tall)

    loop(images * PAD // size, block, ticks)


def dense_backward(images, b_ref, x_in, gain, wid, w1b, hn_ref, z_ref, g_ref, da_ref, dgain_ref, dwid, ticks=()):
    size = row_block(images)
    dgain_ref[...] = jnp.zeros_like(dgain_ref)

    def block(i):
        r = rows_of(i, size)
        b = b_ref[r, :]
        da = b.astype(BF)
        da_ref[r, pl.ds(0, D)] = da
        slope_halves(da, lambda h: narrow_half(w1b, h), g_ref, r)
        dhn = dot_nt(g_ref[r, :], wid[...])
        dx, dg = norm_back(x_in[r, :], gain, dhn)
        b_ref[r, :] = b + dx
        dgain_ref[...] += dg

    loop(images * PAD // size, block, ticks)
    hn_t, da_t = hn_ref[...].T, da_ref[...].T
    for j in range(FF // WIDE):
        cols = pl.ds(WIDE * j, WIDE)
        dwid[:, cols] = dot_nn(hn_t, g_ref[:, cols]).astype(BF)
    for h in range(2):
        delta = tall_delta(da_t, z_ref[:, pl.ds(HALF * h, HALF)])
        w1b[2 * h : 2 * h + 2, :, :, :, 96:144, :] = delta.reshape(2, 2, 2, 2, 48, D)


def router_forward(images, x_in, x_out, gain, router, routes_ref, hn_ref, table_ref):
    lane = lax.broadcasted_iota(jnp.int32, (SEQ, LANES), 1) - EXPERTS
    low_lane = lax.broadcasted_iota(jnp.int32, (PAD, LANES), 1) < EXPERTS

    def image(i):
        r = rows_of(i)
        x = x_in[r, :]
        hn = (normed(x)[0] * gain).astype(BF)
        hn_ref[r, :] = hn
        x_out[r, :] = x
        logits = jnp.where(low_lane, dot_nt(hn, router), -1e30)
        w = jnp.exp(logits - jnp.max(logits, axis=-1, keepdims=True))
        probs = w * (1.0 / jnp.sum(w, axis=-1, keepdims=True))
        table_ref[r, :] = probs
        named = routes_ref[i].T
        hot = (lane == named[:SEQ, 0:1]) | (lane == named[:SEQ, 1:2])
        table_ref[pl.ds(pl.multiple_of(i * PAD, 16), SEQ), :] = jnp.where(hot, 1.0, probs[:SEQ])

    loop(images, image)


def expert_step(
    images, e, x_out, cot_ref, dhn_ref, uw, vw, hn_ref, table_ref, z_ref, g_ref, dy_ref, ticks=(), late=(), before=None
):
    size = row_block(images)
    lane = lax.broadcasted_iota(jnp.int32, (size, LANES), 1)

    def u_tile(cols):
        return uw[e, :, :, :, :, cols].reshape(D, -1)

    def v_half(h):
        return vw[e, h].reshape(HALF, D)

    def block(i):
        r = rows_of(i, size)
        hn = hn_ref[r, :]
        gelu_tiles(hn, u_tile, z_ref, g_ref, r)
        y = dot_nn(z_ref[r, :], vw[e].reshape(FF, D))
        table = table_ref[r, :]
        hot = jnp.sum(jnp.where(lane == e + EXPERTS, table, 0.0), axis=-1, keepdims=True)
        gate = hot * jnp.sum(jnp.where(lane == e, table, 0.0), axis=-1, keepdims=True)
        b = cot_ref[r, :].astype(F32)
        x_out[r, :] += gate * y
        dgate = hot * jnp.sum(b * y, axis=-1, keepdims=True)
        table_ref[r, :] = jnp.where(lane == e + 2 * EXPERTS, dgate, table)
        dy = (gate * b).astype(BF)
        dy_ref[r, :] = dy
        slope_halves(dy, v_half, g_ref, r)
        dhn_ref[r, :] += dot_nt(g_ref[r, :], u_tile(pl.ds(0, FF)))

    loop(images * PAD // size, block, ticks)
    if before is not None:
        before()
    hn_t, dy_t = hn_ref[...].T, dy_ref[...].T
    for j in range(FF // WIDE):
        cols = pl.ds(WIDE * j, WIDE)
        uw[e, :, :, :, :, cols] = dot_nn(hn_t, g_ref[:, cols]).astype(BF).reshape(2, 2, 2, 48, WIDE)
    for tick in late:
        tick()
    for h in range(2):
        vw[e, h] = tall_delta(dy_t, z_ref[:, pl.ds(HALF * h, HALF)]).reshape(2, 2, 192, D)


def router_backward(images, b_ref, cot_ref, x_in, gain, router, dhn_ref, table_ref, hn_ref, drouter_ref, dgain_ref, ticks=()):
    dgain_ref[...] = jnp.zeros_like(dgain_ref)
    drouter_ref[...] = jnp.zeros_like(drouter_ref)
    low_lane = lax.broadcasted_iota(jnp.int32, (PAD, LANES), 1) < EXPERTS

    def image(i):
        r = rows_of(i)
        table = table_ref[r, :]
        probs = jnp.where(low_lane, table, 0.0)
        dprobs = pltpu.roll(table, LANES - 2 * EXPERTS, 1)
        dlogits = (probs * (dprobs - jnp.sum(dprobs * probs, axis=-1, keepdims=True))).astype(BF)
        drouter_ref[...] += dot_tn(dlogits, hn_ref[r, :])[:8]
        dhn = dhn_ref[r, :] + dot_nn(dlogits, router)
        dx, dg = norm_back(x_in[r, :], gain, dhn)
        b_ref[r, :] = cot_ref[r, :].astype(F32) + dx
        dgain_ref[...] += dg

    loop(images, image, ticks)


def chunk_spots(matrices):
    return [(m, c) for m in matrices for c in range(m.shape[1] // D)]


def decode(buf, row, matrices):
    spots, perm = chunk_spots(matrices), permutation()

    def group(g):
        full = dot_tn(perm, piece_rows(buf, g, row)).astype(BF)
        r = rows_of(g, 96)
        for k, (m, c) in enumerate(spots):
            m[r, pl.ds(D * c, D)] = full[96 * k : 96 * (k + 1)]

    loop(4, group)


def encode(buf, row, matrices):
    spots, perm = chunk_spots(matrices), permutation()

    def group(g):
        r = rows_of(g, 96)
        parts = jnp.concatenate([m[r, pl.ds(D * c, D)] for m, c in spots], axis=0)
        buf[g, :, :, :, row : row + 48, :] = dot_nn(perm, parts).astype(BF).reshape(2, 2, 2, 48, D)

    loop(4, group)


def decode_small(w1a, gains_ref, router_ref):
    block = w1a[:, :, :, :, 48:64, :].reshape(-1, D)
    spot = lax.broadcasted_iota(jnp.int32, (8, block.shape[0]), 1)
    row = lax.broadcasted_iota(jnp.int32, (8, block.shape[0]), 0)
    pick = (spot % 16 == 0) & (spot // 128 == row)
    gains_ref[...] = dot_nn(jnp.where(pick, 1.0, 0.0).astype(BF), block)
    spot = lax.broadcasted_iota(jnp.int32, (LANES, block.shape[0]), 1)
    row = lax.broadcasted_iota(jnp.int32, (LANES, block.shape[0]), 0)
    pick = (spot % 16 == row + 1) & (row < EXPERTS)
    router_ref[...] = dot_nn(jnp.where(pick, 1.0, 0.0).astype(BF), block).astype(BF)


def encode_small(w1a, gs_ref):
    rest = jnp.zeros((16 - 1 - EXPERTS, D), F32)
    for g in range(4):
        block = jnp.concatenate([gs_ref[pl.ds(g, 1), :], gs_ref[pl.ds(4, EXPERTS), :], rest], axis=0).astype(BF)
        for d in range(8):
            w1a[g, d // 4, d // 2 % 2, d % 2, 48:64, :] = block


def spot_grid(shape):
    return lax.broadcasted_iota(jnp.int32, shape, 0), lax.broadcasted_iota(jnp.int32, shape, 1)


def picked(rows, flat, spot):
    row, col = spot_grid((rows, flat.shape[0]))
    parts = [dot_nn(jnp.where(col == spot(row, k), 1.0, 0.0).astype(BF), flat) for k in range(D // LANES)]
    return jnp.concatenate(parts, axis=1)


def chunk_rows(flat, first, chunks, rows=4 * ROWS):
    wide = chunks * D // LANES

    def spot(row, k):
        c = row // ROWS - first
        inside = (c >= 0) & (c < chunks)
        return jnp.where(inside, wide * (row % ROWS) + D // LANES * c + k, -1)

    return picked(rows, flat, spot)


def assemble_attention(own, row, flat_in, flat_out):
    both = chunk_rows(flat_in[...], 0, 3) + chunk_rows(flat_out[...], 3, 1)
    own[row : row + 4 * ROWS, :] = both.astype(BF)


def small_places(me):
    i, j = spot_grid((LANES, D))
    share = 4 * D // SHARDS
    place = [(i < share) & (j == me % (D // share) * share + i)]
    for e in range(EXPERTS):
        place.append((i >= share) & (i < 2 * share) & (i % EXPERTS == e) & (j == me * ROWS + (i - share) // EXPERTS))
    return [jnp.where(p, 1.0, 0.0) for p in place]


def assemble_small(own, places, flat):
    row, _ = spot_grid((16, D))
    total = jnp.zeros((16, D), F32)
    for q, place in enumerate(places):
        total += jnp.where(row == q, dot_nn(flat, place.astype(BF))[0:1], 0.0)
    own[48:64, :] = total.astype(BF)


def scatter_chunks(stage, row, cols, total, first, chunks):
    wide = chunks * D // LANES
    for c in range(chunks):
        for k in range(D // LANES):
            spots = pl.ds(row + D // LANES * c + k, ROWS, stride=wide)
            stage[spots, cols] = total[ROWS * (first + c) : ROWS * (first + c + 1), LANES * k : LANES * (k + 1)]


def scatter_rows(stage, row, cols, total):
    wide = total.shape[1] // LANES
    for k in range(wide):
        stage[pl.ds(row + k, total.shape[0], stride=wide), cols] = total[:, LANES * k : LANES * (k + 1)]


def permutation():
    k = lax.broadcasted_iota(jnp.int32, (1, D), 1)
    spot = k // ROWS % 8 * (4 * ROWS) + k // (8 * ROWS) * ROWS + k % ROWS
    return jnp.where(lax.broadcasted_iota(jnp.int32, (D, D), 0) == spot, 1.0, 0.0).astype(BF)


class Copy:
    def __init__(self, net, k, ends, mask):
        self.net, self.k, self.ends, self.mask = net, k, ends, mask

    def make(self):
        src, dst = self.ends()
        return pltpu.make_async_remote_copy(
            src_ref=src, dst_ref=dst, send_sem=self.net.send_sem.at[self.k], recv_sem=self.net.recv_sem.at[self.k],
            device_id=(self.net.partner(self.mask),), device_id_type=MESH)

    def start(self):
        self.make().start()

    def wait_recv(self):
        self.make().wait_recv()

    def wait_send(self):
        self.make().wait_send()


class Net:
    masks = (1, 2, 4, 8, 16, 24)

    def __init__(self, send_sem, recv_sem):
        self.send_sem, self.recv_sem, self.count = send_sem, recv_sem, 0
        me = self.me = lax.axis_index("fsdp")
        self.c, self.x, self.y, self.z = me % 2, me // 2 % 2, me // 4 % 2, me // 8
        self.zs = [self.flip_z(d) for d in range(4)]
        self.partners = {m: self.partner_of(m) for m in self.masks}

    def partner(self, mask):
        return self.partners[mask]

    def partner_of(self, mask):
        c = 1 - self.c if mask & 1 else self.c
        x = 1 - self.x if mask & 2 else self.x
        y = 1 - self.y if mask & 4 else self.y
        return self.zs[mask >> 3] * 8 + y * 4 + x * 2 + c

    def flip_z(self, d):
        lo, hi = self.z % 2, self.z // 2
        lo = 1 - lo if d & 1 else lo
        hi = 1 - hi if d & 2 else hi
        return hi * 2 + lo

    def barrier(self):
        sem = pltpu.get_barrier_semaphore()
        for m in self.masks:
            pl.semaphore_signal(sem, inc=1, device_id=(self.partner(m),), device_id_type=MESH)
        pl.semaphore_wait(sem, len(self.masks))

    def copy(self, ends, mask):
        k = self.count
        self.count += 1
        return Copy(self, k, ends, mask)


def halves(rows, w):
    if w == D:
        cut = (rows // 32 + 1) * 16 if rows % 32 else rows // 2
        return (pl.ds(0, cut), pl.ds(0, w)), (pl.ds(cut, rows - cut), pl.ds(0, w))
    return (pl.ds(0, rows), pl.ds(0, w // 2)), (pl.ds(0, rows), pl.ds(w // 2, w // 2))


class Gather:
    def __init__(self, net, buf):
        x, y, c = net.x, net.y, net.c
        a, b = halves(*buf.shape[-2:])

        def copy(d, yy, xx, half, mask):
            def ends():
                ref = buf.at[net.zs[d], yy, xx, c]
                ref = ref if half is None else ref.at[half[0], half[1]]
                return ref, ref

            return net.copy(ends, mask)

        def pair(d):
            def ends():
                ref = buf.at[net.zs[d], :, :, c]
                return ref, ref

            return net.copy(ends, 1)

        slots = range(4)
        self.along_z = [None] + [copy(0, y, x, None, d << 3) for d in (1, 2, 3)]
        self.to_y = [copy(d, y, x, a, 4) for d in slots]
        self.to_x = [copy(d, y, x, b, 2) for d in slots]
        self.own_x = [copy(d, y, x, a, 2) for d in slots]
        self.own_y = [copy(d, y, x, b, 4) for d in slots]
        self.far_x = [copy(d, 1 - y, x, a, 2) for d in slots]
        self.far_y = [copy(d, y, 1 - x, b, 4) for d in slots]
        self.pair = [pair(d) for d in slots]

    def send_z(self, d):
        self.along_z[d].start()

    def plane(self, d):
        if d:
            self.along_z[d].wait_recv()
        self.to_y[d].start()
        self.to_x[d].start()
        self.own_x[d].start()
        self.own_y[d].start()

    def across(self, d):
        self.to_y[d].wait_recv()
        self.far_x[d].start()
        self.to_x[d].wait_recv()
        self.far_y[d].start()

    def core(self, d):
        for copy in (self.own_x, self.own_y, self.far_x, self.far_y):
            copy[d].wait_recv()
        self.pair[d].start()

    def here(self, d):
        self.pair[d].wait_recv()

    def sent(self, d):
        for copy in (self.to_y, self.to_x, self.own_x, self.own_y, self.far_x, self.far_y, self.pair):
            copy[d].wait_send()
        if d == 0:
            for k in (1, 2, 3):
                self.along_z[k].wait_send()


class Reduce:
    def __init__(self, net, part, slots, bufs, r4):
        self.net, self.part, self.slots, self.r4 = net, part, slots, r4
        self.recv1, self.r2a, self.r2b, self.r3a, self.r3b = bufs
        x, y, c = net.x, net.y, net.c
        self.a, self.b = halves(*part.shape[-2:])
        planes = pl.ds(0, 4) if len(slots) == 4 else pl.ds(net.zs[slots[0]], 1)
        self.planes = range(4) if len(slots) == 4 else [net.zs[slots[0]]]
        a, b = self.a, self.b

        def one(yy, xx):
            return net.copy(lambda: (part.at[planes, yy, xx, 1 - c], self.recv1.at[:, yy, xx]), 1)

        self.s1 = {(fy, fx): one(1 - y if fy else y, 1 - x if fx else x) for fx in (1, 0) for fy in (1, 0)}

        def two_a(yy):
            return net.copy(lambda: (part.at[planes, yy, 1 - x, c, a[0], a[1]], self.r2a.at[:, yy]), 2)

        def two_b(xx):
            return net.copy(lambda: (part.at[planes, 1 - y, xx, c, b[0], b[1]], self.r2b.at[:, xx]), 4)

        self.s2a = [two_a(1 - y), two_a(y)]
        self.s2b = [two_b(1 - x), two_b(x)]
        self.s3a = net.copy(lambda: (part.at[planes, 1 - y, x, c, a[0], a[1]], self.r3a), 4)
        self.s3b = net.copy(lambda: (part.at[planes, y, 1 - x, c, b[0], b[1]], self.r3b), 2)

        def four(d):
            return net.copy(lambda: (part.at[net.zs[d], y, x, c], r4.at[d - 1]), d << 3)

        self.s4 = {d: four(d) for d in slots if d}

    def add(self, ref, other):
        ref[...] = (ref[...].astype(F32) + other[...].astype(F32)).astype(BF)

    def one(self):
        for copy in self.s1.values():
            copy.start()

    def two(self):
        net = self.net
        x, y, c = net.x, net.y, net.c

        def add_all(fy, fx):
            self.s1[fy, fx].wait_recv()
            yy, xx = (1 - y if fy else y), (1 - x if fx else x)
            for k, z in enumerate(self.planes):
                self.add(self.part.at[z, yy, xx, c], self.recv1.at[k, yy, xx])

        add_all(1, 1)
        self.s2a[0].start()
        self.s2b[0].start()
        add_all(0, 1)
        self.s2a[1].start()
        add_all(1, 0)
        self.s2b[1].start()
        add_all(0, 0)

    def three(self):
        net = self.net
        x, y, c = net.x, net.y, net.c
        a, b = self.a, self.b

        def add_half(yy, xx, half, buf, spot):
            for k, z in enumerate(self.planes):
                self.add(self.part.at[z, yy, xx, c, half[0], half[1]], buf.at[k, spot])

        self.s2a[0].wait_recv()
        add_half(1 - y, x, a, self.r2a, 1 - y)
        self.s3a.start()
        self.s2b[0].wait_recv()
        add_half(y, 1 - x, b, self.r2b, 1 - x)
        self.s3b.start()
        self.s2a[1].wait_recv()
        add_half(y, x, a, self.r2a, y)
        self.s2b[1].wait_recv()
        add_half(y, x, b, self.r2b, x)

    def four(self):
        net = self.net
        x, y, c = net.x, net.y, net.c
        for copy, half, buf in ((self.s3a, self.a, self.r3a), (self.s3b, self.b, self.r3b)):
            copy.wait_recv()
            for k, z in enumerate(self.planes):
                self.add(self.part.at[z, y, x, c, half[0], half[1]], buf.at[k])
        for copy in self.s4.values():
            copy.start()

    def sent(self):
        for copy in [*self.s1.values(), *self.s2a, *self.s2b, self.s3a, self.s3b, *self.s4.values()]:
            copy.wait_send()


def summed(net, part, reduces, r4):
    total = part[net.z, net.y, net.x, net.c].astype(F32)
    for job in reduces:
        for d, copy in job.s4.items():
            copy.wait_recv()
            total += r4[d - 1].astype(F32)
    return total


def reduce_buffers(rows, w, planes):
    a, b = halves(rows, w)
    sa, sb = (a[0].size, a[1].size), (b[0].size, b[1].size)
    shapes = [(planes, 2, 2, rows, w), (planes, 2) + sa, (planes, 2) + sb, (planes,) + sa, (planes,) + sb]
    return [pltpu.VMEM(s, BF) for s in shapes]


def block_kernel(remote, names, *refs):
    r = dict(zip(names, refs))
    images = r["tok"].shape[0] // PAD
    w1a, w1b, uw, vw = arrays = [r[k] for k in ("w1a", "w1b", "uw", "vw")]
    sem = r["sem"]
    cot_load = pltpu.make_async_copy(r["cot"], r["cotv"], sem.at[4])
    cot_load.start()
    x0 = r["hn4"]
    tok_load = pltpu.make_async_copy(r["tok"], x0, sem.at[6])
    tok_load.start()

    if remote:
        net = Net(r["send_sem"], r["recv_sem"])
        own = [buf.at[net.z, net.y, net.x, net.c] for buf in arrays]
        tall = [r["ge"].at[pl.ds(0, r[name].shape[0]), pl.ds(LANES * k, LANES)] for k, name in enumerate(FLAT[-2:])]
        loads = [pltpu.make_async_copy(r[name], ref, sem.at[k]) for k, (name, ref) in enumerate(zip(FLAT[-2:], tall))]
        for copy in loads:
            copy.start()
        places = small_places(net.me)
        assemble_attention(own[0], 0, r["in_one"], r["out_one"])
        assemble_small(own[0], places, r["small"][...])
        net.barrier()
        ga, gb, gu, gv = [Gather(net, buf) for buf in arrays]
        experts = [net.zs[d] for d in range(4)]
        for d in (1, 2, 3):
            ga.send_z(d)
        ga.plane(0)
        assemble_attention(own[1], 0, r["in_two"], r["out_two"])
        own[1][48:96, :] = chunk_rows(r["widen"][...], 0, 4).astype(BF)
        own[1][96:144, :] = picked(48, r["narrow"][...], lambda row, k: 3 * row + k).astype(BF)
    else:
        loads = [
            pltpu.make_async_copy(r[k + "_in"], buf, sem.at[j])
            for j, (k, buf) in enumerate(zip(("w1a", "w1b", "uw", "vw"), arrays))
        ]
        for copy in loads:
            copy.start()
        experts = range(4)
    x1, x2, x3, b, dhn = (r[k] for k in ("x1", "x2", "x3", "b", "dhn"))
    x4 = b
    valid, cot = r["valid"], r["cotv"]
    cot_load.wait()
    tok_load.wait()
    for i in range(images):
        rows = pl.ds(PAD * i, PAD)
        cot[rows, :] = (cot[rows, :].astype(F32) * valid[i].astype(F32)).astype(BF)
    dhn[...] = jnp.zeros_like(dhn)
    table = r["table"]
    win1, wout1, wid1, win2, wout2 = (r[k] for k in ("win1", "wout1", "wid1", "win2", "wout2"))

    def none():
        return None

    def batch(*steps):
        def tick():
            for step in steps:
                step()

        return tick if remote else none

    def both(step, d):
        return batch(lambda: getattr(gu, step)(d), lambda: getattr(gv, step)(d))

    if remote:
        ga.across(0)
        for d in (1, 2, 3):
            ga.plane(d)
        for d in (1, 2, 3):
            gb.send_z(d)
        gb.plane(0)
        for d in (1, 2, 3):
            ga.across(d)
        for d in range(4):
            ga.core(d)
        gb.across(0)
        gb.plane(1)
        for copy in loads:
            copy.wait()
        for j in range(FF // D):
            own[2][:, pl.ds(D * j, D)] = picked(48, tall[0][...], lambda row, k: 12 * row + 3 * j + k).astype(BF)
        own[3][...] = picked(192, tall[1][...], lambda row, k: 3 * row + k).astype(BF)
        both("send_z", 1)()
        both("send_z", 2)()
        for d in range(4):
            ga.here(d)
        gb.plane(2)
        gb.plane(3)
    else:
        loads[0].wait()

    decode(w1a, 0, (win1, wout1))
    decode_small(w1a, r["gains"], r["router"])
    gains = [r["gains"][pl.ds(k, 1), :] for k in range(4)]
    router = r["router"][...]
    ticks = [
        batch(lambda: gb.across(1), lambda: gb.across(2), lambda: gb.across(3), both("plane", 0)),
        batch(lambda: gb.core(0), lambda: gb.core(1), lambda: gb.core(2)),
        batch(lambda: gb.core(3), both("send_z", 3)),
        batch(both("across", 0)),
    ]
    attention_forward(images, x0, x1, gains[0], win1, wout1, r["hn1"], r["qkv1"], r["pb1"], r["o1"], ticks)
    if remote:
        for d in range(4):
            gb.here(d)
    else:
        loads[1].wait()
    decode(w1b, 48, (wid1,))
    decode(w1b, 0, (win2, wout2))
    ticks = [both("plane", 1), both("core", 0)]
    dense_forward(images, x1, x2, gains[1], wid1, w1b, r["hn2"], r["z1"], r["g1"], ticks)
    ticks = [none, both("across", 1), none, both("plane", 2)]
    attention_forward(images, x2, x3, gains[2], win2, wout2, r["hn3"], r["qkv2"], r["pb2"], r["o2"], ticks)
    router_forward(images, x3, x4, gains[3], router, r["routes"], r["hn4"], table)

    if remote:
        buffers = iter(r["rs"])
        take = lambda: [next(buffers) for _ in range(5)]
        bufs_u, bufs_v = [take(), take()], [take(), take()]
        ru = [Reduce(net, uw, [d], bufs_u[d % 2], r["r4u"]) for d in range(4)]
        rv = [Reduce(net, vw, [d], bufs_v[d % 2], r["r4v"]) for d in range(4)]
        rb = Reduce(net, w1b, [0, 1, 2, 3], take(), r["r4b"])
        ra = Reduce(net, w1a, [0, 1, 2, 3], take(), r["r4a"])
    else:
        loads[2].wait()
        loads[3].wait()

    def reduce_step(step, d):
        return batch(lambda: getattr(ru[d], step)(), lambda: getattr(rv[d], step)())

    def run_expert(d, ticks, late):
        if remote:
            gu.here(d)
            gv.here(d)
        before = batch(lambda: gu.sent(d), lambda: gv.sent(d))
        late = [*late, batch(lambda: ru[d].one())]
        expert_step(
            images, experts[d], x4, cot, dhn, uw, vw, r["hn4"], table, r["ze"], r["ge"], r["dy"], ticks, late, before
        )
        batch(lambda: rv[d].one())()

    both("core", 1)()
    run_expert(0, [both("across", 2), both("plane", 3)], [both("core", 2)])
    both("across", 3)()
    run_expert(1, [reduce_step("two", 0), both("core", 3)], [])
    reduce_step("three", 0)()
    run_expert(2, [reduce_step("two", 1), reduce_step("four", 0)], [])
    reduce_step("three", 1)()
    run_expert(3, [reduce_step("two", 2), reduce_step("four", 1)], [])
    reduce_step("three", 2)()
    out_cols = pl.ds(0, D)
    for i in range(images):
        rows = pl.ds(PAD * i, PAD)
        r["ge"][rows, out_cols] = (x4[rows, :] * valid[i].astype(F32)).astype(BF)
    out_store = pltpu.make_async_copy(r["ge"].at[:, out_cols], r["out"], sem.at[5])
    out_store.start()
    gs, dgain, drouter = r["gs"], r["dgain"], r["drouter"]
    gs[...] = jnp.zeros_like(gs)
    router_backward(images, b, cot, x3, gains[3], router, dhn, table, r["hn4"], drouter, dgain)
    tok_load.start()
    gs[pl.ds(4, EXPERTS), :] = drouter[pl.ds(0, EXPERTS), :]
    gs[pl.ds(3, 1), :] = dgain[...]
    dqkv, da = r["ze"], r["dy"]
    ticks = [reduce_step("two", 3), reduce_step("four", 2), reduce_step("three", 3)]
    attention_backward(images, b, x2, gains[2], win2, wout2, r["hn3"], r["qkv2"], r["pb2"], r["o2"], da, dqkv, dgain, win2, wout2, ticks)
    gs[pl.ds(2, 1), :] = dgain[...]
    batch(*(lambda d=d: gb.sent(d) for d in range(4)))()
    encode(w1b, 0, (win2, wout2))
    ticks = [reduce_step("four", 3)]
    dense_backward(images, b, x1, gains[1], wid1, w1b, r["hn2"], r["z1"], r["g1"], da, dgain, wid1, ticks)
    gs[pl.ds(1, 1), :] = dgain[...]
    encode(w1b, 48, (wid1,))
    if remote:
        rb.one()
    lanes = pl.ds(0, LANES)

    def leave(name, row, k):
        flat = r[name + "_out"]
        return pltpu.make_async_copy(table.at[pl.ds(row, flat.shape[0]), :], flat, sem.at[k])

    def tall_sum():
        scatter_rows(table, 0, lanes, summed(net, vw, rv, r["r4v"]))
        leave("tall_v", 0, 7).start()

    tok_load.wait()
    ticks = [batch(lambda: rb.two()), none, batch(lambda: rb.three()), batch(tall_sum, lambda: rb.four())]
    attention_backward(images, b, x0, gains[0], win1, wout1, r["hn1"], r["qkv1"], r["pb1"], r["o1"], da, dqkv, dgain, win1, wout1, ticks)
    gs[pl.ds(0, 1), :] = dgain[...]
    batch(*(lambda d=d: ga.sent(d) for d in range(4)))()
    encode(w1a, 0, (win1, wout1))
    encode_small(w1a, gs)
    if remote:
        ra.one()
    r["o1"][...] = b[...].astype(BF)
    delta_store = pltpu.make_async_copy(r["o1"], r["dtok"], sem.at[6])
    delta_store.start()
    if remote:
        leave("tall_v", 0, 7).wait()
        scatter_rows(table, 0, lanes, summed(net, uw, ru, r["r4u"]))
        leave("tall_u", 0, 8).start()
        ra.two()
        total = summed(net, w1b, [rb], r["r4b"])
        scatter_chunks(r["in_two_out"], 0, lanes, total, 0, 3)
        scatter_chunks(r["out_two_out"], 0, lanes, total, 3, 1)
        scatter_chunks(table, 576, lanes, total, 4, 4)
        leave("widen", 576, 9).start()
        scatter_rows(r["narrow_out"], 0, lanes, total[96:144])
        ra.three()
        ra.four()
        total = summed(net, w1a, [ra], r["r4a"])
        scatter_chunks(r["in_one_out"], 0, lanes, total, 0, 3)
        scatter_chunks(r["out_one_out"], 0, lanes, total, 3, 1)
        exact = dict(precision=lax.Precision.HIGHEST, preferred_element_type=F32)
        small = jnp.zeros((8, LANES), F32)
        for q, place in enumerate(places):
            line = jnp.broadcast_to(total[48 + q : 49 + q], (8, D))
            small += lax.dot_general(line, place, (((1,), (1,)), ((), ())), **exact)
        r["small_out"][...] = small
        leave("tall_u", 0, 8).wait()
        leave("widen", 576, 9).wait()
        for job in (*ru, *rv, rb, ra):
            job.sent()
    else:
        stores = [
            pltpu.make_async_copy(buf, r[k + "_out"], sem.at[j])
            for j, (k, buf) in enumerate(zip(("w1a", "w1b", "uw", "vw"), arrays))
        ]
        for copy in stores:
            copy.start()
        for copy in stores:
            copy.wait()
    out_store.wait()
    delta_store.wait()


PIECES = ((64, D), (144, D), (48, FF), (192, D))
AWAY = ("widen", "tall_u", "tall_v")
FLAT = ("in_one", "out_one", "widen", "narrow", "in_two", "out_two", "tall_u", "tall_v")


def run_blocks(remote, tok, cot, valid, routes, *weights):
    t = tok.shape[0]
    images = t // PAD
    v = pltpu.VMEM
    vmem, smem, hbm = (pl.BlockSpec(memory_space=m) for m in (pltpu.VMEM, pltpu.SMEM, pl.ANY))
    whole = [(4, 2, 2, 2) + s for s in PIECES]
    inputs = dict(
        tok=(tok, hbm), cot=(cot, hbm), valid=(valid, smem), routes=(routes, vmem),
    )
    if remote:
        inputs.update({name: (w, hbm if name in FLAT[-2:] else vmem) for name, w in zip((*FLAT, "small"), weights)})
    else:
        inputs.update({name + "_in": (w, hbm) for name, w in zip(("w1a", "w1b", "uw", "vw"), weights)})
    flat = jax.ShapeDtypeStruct(tok.shape, BF)
    outputs = dict(out=(flat, hbm), dtok=(flat, hbm))
    if remote:
        for name, w in zip(FLAT, weights):
            outputs[name + "_out"] = (jax.ShapeDtypeStruct(w.shape, F32), hbm if name in AWAY else vmem)
        outputs["small_out"] = (jax.ShapeDtypeStruct((8, LANES), F32), vmem)
    else:
        for name, full in zip(("w1a", "w1b", "uw", "vw"), whole):
            outputs[name + "_out"] = (jax.ShapeDtypeStruct(full, BF), hbm)
    scratch = dict(
        w1a=v(whole[0], BF), w1b=v(whole[1], BF), uw=v(whole[2], BF), vw=v(whole[3], BF),
        win1=v((D, 3 * D), BF), wout1=v((D, D), BF), wid1=v((D, FF), BF), win2=v((D, 3 * D), BF), wout2=v((D, D), BF),
        x1=v((t, D), F32), x2=v((t, D), F32), x3=v((t, D), F32), b=v((t, D), F32), dhn=v((t, D), F32),
        hn1=v((t, D), BF), hn2=v((t, D), BF), hn3=v((t, D), BF), hn4=v((t, D), BF),
        qkv1=v((t, 3 * D), BF), qkv2=v((t, 3 * D), BF), o1=v((t, D), BF), o2=v((t, D), BF),
        pb1=v((images * PAIRS, 2 * PAD, PAD), BF), pb2=v((images * PAIRS, 2 * PAD, PAD), BF),
        z1=v((t, FF), BF), g1=v((t, FF), BF), ze=v((t, FF), BF), ge=v((t, FF), BF), dy=v((t, D), BF), cotv=v((t, D), BF),
        table=v((t, LANES), F32),
        drouter=v((8, D), F32), dgain=v((1, D), F32), gs=v((16, D), F32), gains=v((8, D), F32), router=v((LANES, D), BF),
        sem=pltpu.SemaphoreType.DMA((16,)),
    )
    if remote:
        scratch["rs"] = [
            spec
            for piece, planes in [(PIECES[2], 1)] * 2 + [(PIECES[3], 1)] * 2 + [(PIECES[1], 4), (PIECES[0], 4)]
            for spec in reduce_buffers(*piece, planes)
        ]
        for k, piece in zip("abuv", PIECES):
            scratch["r4" + k] = v((3,) + piece, BF)
        scratch["send_sem"] = pltpu.SemaphoreType.DMA((256,))
        scratch["recv_sem"] = pltpu.SemaphoreType.DMA((256,))
    names = (*inputs, *outputs, *scratch)
    params = dict(collective_id=0, has_side_effects=True) if remote else {}
    return pl.pallas_call(
        functools.partial(block_kernel, remote, names),
        out_shape=tuple(o[0] for o in outputs.values()),
        in_specs=[i[1] for i in inputs.values()],
        out_specs=tuple(o[1] for o in outputs.values()),
        scratch_shapes=list(scratch.values()),
        compiler_params=pltpu.CompilerParams(vmem_limit_bytes=127 * 2**19, **params),
    )(*[i[0] for i in inputs.values()])


def hand_over(*arrays):
    count = len(arrays)

    def kernel(*refs):
        sem = refs[-1]
        copies = [pltpu.make_async_copy(refs[k], refs[count + k], sem.at[k]) for k in range(count)]
        for copy in copies:
            copy.start()
        for copy in copies:
            copy.wait()

    hbm = pl.BlockSpec(memory_space=pl.ANY)
    return pl.pallas_call(
        kernel,
        out_shape=[jax.ShapeDtypeStruct(a.shape, a.dtype) for a in arrays],
        in_specs=[hbm] * count,
        out_specs=[hbm] * count,
        scratch_shapes=[pltpu.SemaphoreType.DMA((count,))],
    )(*arrays)


def all_pieces(norm_gains, in_one, out_one, widen, narrow, router, in_two, out_two, experts_widen, experts_narrow):
    def cut(*matrices):
        side = jnp.concatenate([m.reshape(D, -1) for m in matrices], axis=1)
        return side.reshape(SHARDS, ROWS, -1, D).transpose(0, 2, 1, 3).reshape(SHARDS, -1, D)

    small = jnp.zeros((SHARDS, 16, D), BF)
    small = small.at[:: SHARDS // 4, 0].set(norm_gains.reshape(4, D))
    small = small.at[0, 1 : 1 + EXPERTS].set(router.reshape(D, EXPERTS).T)
    parts = (
        jnp.concatenate([cut(in_one, out_one), small], axis=1),
        jnp.concatenate([cut(in_two, out_two), cut(widen), narrow.reshape(SHARDS, -1, D)], axis=1),
        experts_widen.reshape(SHARDS, -1, FF),
        experts_narrow.reshape(SHARDS, -1, D),
    )
    return [p.reshape((4, 2, 2, 2) + p.shape[1:]) for p in parts]


def all_deltas(*parts):
    w1a, w1b, uw, vw = (p.astype(F32).reshape((SHARDS,) + p.shape[-2:]) for p in parts)

    def join(part):
        return part.reshape(SHARDS, -1, ROWS, D).transpose(0, 2, 1, 3).reshape(D, -1)

    one, two = join(w1a[:, 0:48]), join(w1b[:, 0:48])
    whole = (
        w1a[:: SHARDS // 4, 48], one[:, : 3 * D], one[:, 3 * D :], join(w1b[:, 48:96]), w1b[:, 96:144], w1a[0, 49:53].T,
        two[:, : 3 * D], two[:, 3 * D :], uw, vw,
    )
    return [p.reshape(-1) for p in whole]


def on_device(shards, tokens, cotangent, image_valid, routes, *weights):
    images = tokens.shape[0] * tokens.shape[1]

    def padded(array):
        return jnp.pad(array, ((0, 0), (0, 0), (0, PAD - SEQ), (0, 0))).reshape(images * PAD, D)

    def cut(array):
        return array.reshape(tokens.shape[:2] + (PAD, D))[:, :, :SEQ]

    named = routes.reshape(images, SEQ, 2).transpose(0, 2, 1)
    named = jnp.pad(named, ((0, 0), (0, 6), (0, 2 * LANES - SEQ)))
    data = (padded(tokens), padded(cotangent), image_valid.reshape(images), named)
    if shards == SHARDS:
        gains, in_one, out_one, widen, narrow, router, in_two, out_two, tall_u, tall_v = weights
        flat = [w.reshape(-1, LANES) for w in (in_one, out_one, widen, narrow, in_two, out_two, tall_u, tall_v)]
        small = jnp.pad(jnp.concatenate([gains, router]), (0, LANES - 2 * gains.shape[0]))
        small = jnp.broadcast_to(small[None], (16, LANES))
        out, delta, *sums, small = run_blocks(True, *data, *flat, small)
        sums = [d.reshape(-1) for d in hand_over(*sums)]
        share = gains.shape[0]
        deltas = [small[0, :share], *sums[:4], small[0, share : 2 * share], *sums[4:]]
    else:
        whole = [lax.all_gather(w, "fsdp", axis=0, tiled=True) for w in weights]
        out, delta, *sums = run_blocks(False, *data, *all_pieces(*whole))
        deltas = [lax.psum_scatter(d, "fsdp", scatter_dimension=0, tiled=True) for d in all_deltas(*sums)]
    return (cut(out), cut(delta), *deltas)


def solution(mesh):
    split, flat = P(None, "fsdp", None, None), P("fsdp")
    return jax.shard_map(
        functools.partial(on_device, mesh.shape["fsdp"]),
        mesh=mesh,
        in_specs=(split, split, P(None, "fsdp"), split) + (flat,) * 10,
        out_specs=(split, split) + (flat,) * 10,
        check_vma=False,
    )
```

```python
import functools
import math

import jax
import jax.numpy as jnp
import numpy as np
from jax import lax
from jax.experimental import pallas as pl
from jax.experimental.pallas import tpu as pltpu
from jax.sharding import PartitionSpec as P

D = 384
HEADS = 6
HDIM = 64
FF = 1536
EXPERTS = 4
SEQ = 197
PAD = 208
PAIRS = HEADS // 2
SHARDS = 32
ROWS = D // SHARDS
LANES = 128
EPSILON = 1e-06
BF = jnp.bfloat16
F32 = jnp.float32
MESH = pl.DeviceIdType.MESH
C0 = math.sqrt(2.0 / math.pi)
C1 = 0.044715


def dot_nn(a, b):
    return lax.dot_general(a, b, (((1,), (0,)), ((), ())), preferred_element_type=F32)


def dot_nt(a, b):
    return lax.dot_general(a, b, (((1,), (1,)), ((), ())), preferred_element_type=F32)


def dot_tn(a, b):
    return lax.dot_general(a, b, (((0,), (0,)), ((), ())), preferred_element_type=F32)


def normed(x):
    centred = x - jnp.mean(x, axis=-1, keepdims=True)
    rstd = lax.rsqrt(jnp.mean(centred * centred, axis=-1, keepdims=True) + EPSILON)
    return centred * rstd, rstd


def norm_back(x, gain, dhn):
    xhat, rstd = normed(x)
    dxhat = dhn * gain
    mean_d = jnp.mean(dxhat, axis=-1, keepdims=True)
    mean_dx = jnp.mean(dxhat * xhat, axis=-1, keepdims=True)
    return rstd * (dxhat - mean_d - xhat * mean_dx), jnp.sum(dhn * xhat, axis=0, keepdims=True)


def gelu_both(u):
    u2 = u * u
    t = jnp.tanh(u * (C0 + (C0 * C1) * u2))
    h = 0.5 + 0.5 * t
    z = u * h
    return z, h + z * (1.0 - h) * (2.0 * C0 + (6.0 * C0 * C1) * u2)


def rows_of(i, size=PAD):
    return pl.ds(pl.multiple_of(i * size, 16), size)


def loop(count, body, ticks=()):
    def step(i, carry):
        body(i)
        for k, tick in enumerate(ticks):
            pl.when(i == k)(tick)
        return carry

    lax.fori_loop(0, count, step, 0)


def attention_forward(images, x_in, x_out, gain, win, wout, hn_ref, qkv_ref, pb_ref, o_ref, ticks=()):
    low_half = lax.broadcasted_iota(jnp.int32, (PAD, LANES), 1) < HDIM
    real_key = lax.broadcasted_iota(jnp.int32, (2 * PAD, PAD), 1) < SEQ

    def image(i):
        r = rows_of(i)
        x = x_in[r, :].astype(F32)
        xhat, _ = normed(x)
        hn = (xhat * gain).astype(BF)
        hn_ref[r, :] = hn
        for j in range(3):
            cols = pl.ds(D * j, D)
            qkv_ref[r, cols] = dot_nn(hn, win[:, cols]).astype(BF)
        for p in range(PAIRS):
            q2 = qkv_ref[r, pl.ds(LANES * p, LANES)] * jnp.asarray(HDIM ** (-0.5), BF)
            k2 = qkv_ref[r, pl.ds(D + LANES * p, LANES)]
            v2 = qkv_ref[r, pl.ds(2 * D + LANES * p, LANES)]
            zero = jnp.zeros_like(q2)
            qs = jnp.concatenate([jnp.where(low_half, q2, zero), jnp.where(low_half, zero, q2)], axis=0)
            s = dot_nt(qs, k2)
            s = jnp.where(real_key, s, -1e30)
            w = jnp.exp(s - jnp.max(s, axis=-1, keepdims=True))
            soft = w * (1.0 / jnp.sum(w, axis=-1, keepdims=True))
            pb = soft.astype(BF)
            pb_ref[i * PAIRS + p] = pb
            o2 = dot_nn(pb, v2)
            o_ref[r, pl.ds(LANES * p, LANES)] = jnp.where(low_half, o2[:PAD], o2[PAD:]).astype(BF)
        x_out[r, :] = x + dot_nn(o_ref[r, :], wout[...])

    loop(images, image, ticks)


def attention_backward(
    images, b_ref, x_in, gain, win, wout, hn_ref, qkv_ref, pb_ref, o_ref, da_ref, dqkv_ref, dgain_ref, dwin, dwout, ticks=()
):
    low_half = lax.broadcasted_iota(jnp.int32, (PAD, LANES), 1) < HDIM
    dgain_ref[...] = jnp.zeros_like(dgain_ref)

    def image(i):
        r = rows_of(i)
        b = b_ref[r, :]
        da = b.astype(BF)
        da_ref[r, :] = da
        do = dot_nt(da, wout[...]).astype(BF)
        for p in range(PAIRS):
            cols = [pl.ds(D * j + LANES * p, LANES) for j in range(3)]
            q2, k2, v2 = (qkv_ref[r, c] for c in cols)
            do2 = do[:, LANES * p : LANES * (p + 1)]
            zero = jnp.zeros_like(q2)
            qs = jnp.concatenate([jnp.where(low_half, q2, zero), jnp.where(low_half, zero, q2)], axis=0)
            dos = jnp.concatenate([jnp.where(low_half, do2, zero), jnp.where(low_half, zero, do2)], axis=0)
            pb = pb_ref[i * PAIRS + p]
            soft = pb.astype(F32)
            dp = dot_nt(dos, v2)
            ds = (soft * (dp - jnp.sum(dp * soft, axis=-1, keepdims=True))).astype(BF)
            dq = dot_nn(ds, k2) * HDIM ** (-0.5)
            dqkv_ref[r, cols[0]] = jnp.where(low_half, dq[:PAD], dq[PAD:]).astype(BF)
            dqkv_ref[r, cols[1]] = (dot_tn(ds, qs) * HDIM ** (-0.5)).astype(BF)
            dqkv_ref[r, cols[2]] = dot_tn(pb, dos).astype(BF)
        dhn = dot_nt(dqkv_ref[r, pl.ds(0, 3 * D)], win[...])
        dx, dg = norm_back(x_in[r, :].astype(F32), gain, dhn)
        b_ref[r, :] = b + dx
        dgain_ref[...] += dg

    loop(images, image, ticks)
    dwout[...] = dot_tn(o_ref[...], da_ref[...]).astype(BF)
    hn = hn_ref[...]
    for j in range(3):
        cols = pl.ds(D * j, D)
        dwin[:, cols] = dot_tn(hn, dqkv_ref[:, cols]).astype(BF)


def piece_rows(buf, z, row, cols=None):
    block = buf[z, :, :, :, row : row + 48, :]
    return block.reshape(8 * 48, D)


WIDE = 512
HALF = FF // 2


def narrow_half(w1b, h):
    return w1b[2 * h : 2 * h + 2, :, :, :, 96:144, :].reshape(HALF, D)


def gelu_tiles(hn, wide, z_ref, g_ref, r):
    for j in range(FF // WIDE):
        cols = pl.ds(WIDE * j, WIDE)
        z, g = gelu_both(dot_nn(hn, wide(cols)))
        z_ref[r, cols] = z.astype(BF)
        g_ref[r, cols] = g.astype(BF)


def slope_halves(dy, tall, g_ref, r):
    for h in range(2):
        cols = pl.ds(HALF * h, HALF)
        g_ref[r, cols] = (dot_nt(dy, tall(h)) * g_ref[r, cols].astype(F32)).astype(BF)


def tall_delta(dy_t, z_tile):
    return dot_nn(dy_t, z_tile).astype(BF).T


def row_block(images):
    return 2 * PAD if images % 2 == 0 else PAD


def dense_forward(images, x_in, x_out, gain, wid, w1b, hn_ref, z_ref, g_ref, ticks=()):
    size = row_block(images)

    def block(i):
        r = rows_of(i, size)
        x = x_in[r, :]
        hn = (normed(x)[0] * gain).astype(BF)
        hn_ref[r, :] = hn
        gelu_tiles(hn, lambda cols: wid[:, cols], z_ref, g_ref, r)
        tall = w1b[:, :, :, :, 96:144, :].reshape(FF, D)
        x_out[r, :] = x + dot_nn(z_ref[r, :], tall)

    loop(images * PAD // size, block, ticks)


def dense_backward(images, b_ref, x_in, gain, wid, w1b, hn_ref, z_ref, g_ref, da_ref, dgain_ref, dwid, ticks=()):
    size = row_block(images)
    dgain_ref[...] = jnp.zeros_like(dgain_ref)

    def block(i):
        r = rows_of(i, size)
        b = b_ref[r, :]
        da = b.astype(BF)
        da_ref[r, pl.ds(0, D)] = da
        slope_halves(da, lambda h: narrow_half(w1b, h), g_ref, r)
        dhn = dot_nt(g_ref[r, :], wid[...])
        dx, dg = norm_back(x_in[r, :], gain, dhn)
        b_ref[r, :] = b + dx
        dgain_ref[...] += dg

    loop(images * PAD // size, block, ticks)
    hn_t, da_t = hn_ref[...].T, da_ref[...].T
    for j in range(FF // WIDE):
        cols = pl.ds(WIDE * j, WIDE)
        dwid[:, cols] = dot_nn(hn_t, g_ref[:, cols]).astype(BF)
    for h in range(2):
        delta = tall_delta(da_t, z_ref[:, pl.ds(HALF * h, HALF)])
        w1b[2 * h : 2 * h + 2, :, :, :, 96:144, :] = delta.reshape(2, 2, 2, 2, 48, D)


def router_forward(images, x_in, x_out, gain, router, routes_ref, hn_ref, table_ref):
    lane = lax.broadcasted_iota(jnp.int32, (SEQ, LANES), 1) - EXPERTS
    low_lane = lax.broadcasted_iota(jnp.int32, (PAD, LANES), 1) < EXPERTS

    def image(i):
        r = rows_of(i)
        x = x_in[r, :]
        hn = (normed(x)[0] * gain).astype(BF)
        hn_ref[r, :] = hn
        x_out[r, :] = x
        logits = jnp.where(low_lane, dot_nt(hn, router), -1e30)
        w = jnp.exp(logits - jnp.max(logits, axis=-1, keepdims=True))
        probs = w * (1.0 / jnp.sum(w, axis=-1, keepdims=True))
        table_ref[r, :] = probs
        named = routes_ref[i].T
        hot = (lane == named[:SEQ, 0:1]) | (lane == named[:SEQ, 1:2])
        table_ref[pl.ds(pl.multiple_of(i * PAD, 16), SEQ), :] = jnp.where(hot, 1.0, probs[:SEQ])

    loop(images, image)


def expert_step(
    images, e, x_out, cot_ref, dhn_ref, uw, vw, hn_ref, table_ref, z_ref, g_ref, dy_ref, ticks=(), late=(), before=None
):
    size = row_block(images)
    lane = lax.broadcasted_iota(jnp.int32, (size, LANES), 1)

    def u_tile(cols):
        return uw[e, :, :, :, :, cols].reshape(D, -1)

    def v_half(h):
        return vw[e, h].reshape(HALF, D)

    def block(i):
        r = rows_of(i, size)
        hn = hn_ref[r, :]
        gelu_tiles(hn, u_tile, z_ref, g_ref, r)
        y = dot_nn(z_ref[r, :], vw[e].reshape(FF, D))
        table = table_ref[r, :]
        hot = jnp.sum(jnp.where(lane == e + EXPERTS, table, 0.0), axis=-1, keepdims=True)
        gate = hot * jnp.sum(jnp.where(lane == e, table, 0.0), axis=-1, keepdims=True)
        b = cot_ref[r, :].astype(F32)
        x_out[r, :] += gate * y
        dgate = hot * jnp.sum(b * y, axis=-1, keepdims=True)
        table_ref[r, :] = jnp.where(lane == e + 2 * EXPERTS, dgate, table)
        dy = (gate * b).astype(BF)
        dy_ref[r, :] = dy
        slope_halves(dy, v_half, g_ref, r)
        dhn_ref[r, :] += dot_nt(g_ref[r, :], u_tile(pl.ds(0, FF)))

    loop(images * PAD // size, block, ticks)
    if before is not None:
        before()
    hn_t, dy_t = hn_ref[...].T, dy_ref[...].T
    for j in range(FF // WIDE):
        cols = pl.ds(WIDE * j, WIDE)
        uw[e, :, :, :, :, cols] = dot_nn(hn_t, g_ref[:, cols]).astype(BF).reshape(2, 2, 2, 48, WIDE)
    for tick in late:
        tick()
    for h in range(2):
        vw[e, h] = tall_delta(dy_t, z_ref[:, pl.ds(HALF * h, HALF)]).reshape(2, 2, 192, D)


def router_backward(images, b_ref, cot_ref, x_in, gain, router, dhn_ref, table_ref, hn_ref, drouter_ref, dgain_ref, ticks=()):
    dgain_ref[...] = jnp.zeros_like(dgain_ref)
    drouter_ref[...] = jnp.zeros_like(drouter_ref)
    low_lane = lax.broadcasted_iota(jnp.int32, (PAD, LANES), 1) < EXPERTS

    def image(i):
        r = rows_of(i)
        table = table_ref[r, :]
        probs = jnp.where(low_lane, table, 0.0)
        dprobs = pltpu.roll(table, LANES - 2 * EXPERTS, 1)
        dlogits = (probs * (dprobs - jnp.sum(dprobs * probs, axis=-1, keepdims=True))).astype(BF)
        drouter_ref[...] += dot_tn(dlogits, hn_ref[r, :])[:8]
        dhn = dhn_ref[r, :] + dot_nn(dlogits, router)
        dx, dg = norm_back(x_in[r, :], gain, dhn)
        b_ref[r, :] = cot_ref[r, :].astype(F32) + dx
        dgain_ref[...] += dg

    loop(images, image, ticks)


def chunk_spots(matrices):
    return [(m, c) for m in matrices for c in range(m.shape[1] // D)]


def decode(buf, row, matrices):
    spots, perm = chunk_spots(matrices), permutation()

    def group(g):
        full = dot_tn(perm, piece_rows(buf, g, row)).astype(BF)
        r = rows_of(g, 96)
        for k, (m, c) in enumerate(spots):
            m[r, pl.ds(D * c, D)] = full[96 * k : 96 * (k + 1)]

    loop(4, group)


def encode(buf, row, matrices):
    spots, perm = chunk_spots(matrices), permutation()

    def group(g):
        r = rows_of(g, 96)
        parts = jnp.concatenate([m[r, pl.ds(D * c, D)] for m, c in spots], axis=0)
        buf[g, :, :, :, row : row + 48, :] = dot_nn(perm, parts).astype(BF).reshape(2, 2, 2, 48, D)

    loop(4, group)


def decode_small(w1a, gains_ref, router_ref):
    block = w1a[:, :, :, :, 48:64, :].reshape(-1, D)
    spot = lax.broadcasted_iota(jnp.int32, (8, block.shape[0]), 1)
    row = lax.broadcasted_iota(jnp.int32, (8, block.shape[0]), 0)
    pick = (spot % 16 == 0) & (spot // 128 == row)
    gains_ref[...] = dot_nn(jnp.where(pick, 1.0, 0.0).astype(BF), block)
    spot = lax.broadcasted_iota(jnp.int32, (LANES, block.shape[0]), 1)
    row = lax.broadcasted_iota(jnp.int32, (LANES, block.shape[0]), 0)
    pick = (spot % 16 == row + 1) & (row < EXPERTS)
    router_ref[...] = dot_nn(jnp.where(pick, 1.0, 0.0).astype(BF), block).astype(BF)


def encode_small(w1a, gs_ref):
    rest = jnp.zeros((16 - 1 - EXPERTS, D), F32)
    for g in range(4):
        block = jnp.concatenate([gs_ref[pl.ds(g, 1), :], gs_ref[pl.ds(4, EXPERTS), :], rest], axis=0).astype(BF)
        for d in range(8):
            w1a[g, d // 4, d // 2 % 2, d % 2, 48:64, :] = block


def spot_grid(shape):
    return lax.broadcasted_iota(jnp.int32, shape, 0), lax.broadcasted_iota(jnp.int32, shape, 1)


def picked(rows, flat, spot):
    row, col = spot_grid((rows, flat.shape[0]))
    parts = [dot_nn(jnp.where(col == spot(row, k), 1.0, 0.0).astype(BF), flat) for k in range(D // LANES)]
    return jnp.concatenate(parts, axis=1)


def chunk_rows(flat, first, chunks, rows=4 * ROWS):
    wide = chunks * D // LANES

    def spot(row, k):
        c = row // ROWS - first
        inside = (c >= 0) & (c < chunks)
        return jnp.where(inside, wide * (row % ROWS) + D // LANES * c + k, -1)

    return picked(rows, flat, spot)


def assemble_attention(own, row, flat_in, flat_out):
    both = chunk_rows(flat_in[...], 0, 3) + chunk_rows(flat_out[...], 3, 1)
    own[row : row + 4 * ROWS, :] = both.astype(BF)


def small_places(me):
    i, j = spot_grid((LANES, D))
    share = 4 * D // SHARDS
    place = [(i < share) & (j == me % (D // share) * share + i)]
    for e in range(EXPERTS):
        place.append((i >= share) & (i < 2 * share) & (i % EXPERTS == e) & (j == me * ROWS + (i - share) // EXPERTS))
    return [jnp.where(p, 1.0, 0.0) for p in place]


def assemble_small(own, places, flat):
    row, _ = spot_grid((16, D))
    total = jnp.zeros((16, D), F32)
    for q, place in enumerate(places):
        total += jnp.where(row == q, dot_nn(flat, place.astype(BF))[0:1], 0.0)
    own[48:64, :] = total.astype(BF)


def scatter_chunks(stage, row, cols, total, first, chunks):
    wide = chunks * D // LANES
    for c in range(chunks):
        for k in range(D // LANES):
            spots = pl.ds(row + D // LANES * c + k, ROWS, stride=wide)
            stage[spots, cols] = total[ROWS * (first + c) : ROWS * (first + c + 1), LANES * k : LANES * (k + 1)]


def scatter_rows(stage, row, cols, total):
    wide = total.shape[1] // LANES
    for k in range(wide):
        stage[pl.ds(row + k, total.shape[0], stride=wide), cols] = total[:, LANES * k : LANES * (k + 1)]


def permutation():
    k = lax.broadcasted_iota(jnp.int32, (1, D), 1)
    spot = k // ROWS % 8 * (4 * ROWS) + k // (8 * ROWS) * ROWS + k % ROWS
    return jnp.where(lax.broadcasted_iota(jnp.int32, (D, D), 0) == spot, 1.0, 0.0).astype(BF)


class Copy:
    def __init__(self, net, k, ends, mask):
        self.net, self.k, self.ends, self.mask = net, k, ends, mask

    def make(self):
        src, dst = self.ends()
        return pltpu.make_async_remote_copy(
            src_ref=src, dst_ref=dst, send_sem=self.net.send_sem.at[self.k], recv_sem=self.net.recv_sem.at[self.k],
            device_id=(self.net.partner(self.mask),), device_id_type=MESH)

    def start(self):
        self.make().start()

    def wait_recv(self):
        self.make().wait_recv()

    def wait_send(self):
        self.make().wait_send()


class Net:
    masks = (1, 2, 4, 8, 16, 24)

    def __init__(self, send_sem, recv_sem):
        self.send_sem, self.recv_sem, self.count = send_sem, recv_sem, 0
        me = self.me = lax.axis_index("fsdp")
        self.c, self.x, self.y, self.z = me % 2, me // 2 % 2, me // 4 % 2, me // 8
        self.zs = [self.flip_z(d) for d in range(4)]
        self.partners = {m: self.partner_of(m) for m in self.masks}

    def partner(self, mask):
        return self.partners[mask]

    def partner_of(self, mask):
        c = 1 - self.c if mask & 1 else self.c
        x = 1 - self.x if mask & 2 else self.x
        y = 1 - self.y if mask & 4 else self.y
        return self.zs[mask >> 3] * 8 + y * 4 + x * 2 + c

    def flip_z(self, d):
        lo, hi = self.z % 2, self.z // 2
        lo = 1 - lo if d & 1 else lo
        hi = 1 - hi if d & 2 else hi
        return hi * 2 + lo

    def barrier(self):
        sem = pltpu.get_barrier_semaphore()
        for m in self.masks:
            pl.semaphore_signal(sem, inc=1, device_id=(self.partner(m),), device_id_type=MESH)
        pl.semaphore_wait(sem, len(self.masks))

    def copy(self, ends, mask):
        k = self.count
        self.count += 1
        return Copy(self, k, ends, mask)


def halves(rows, w):
    if w == D:
        cut = (rows // 32 + 1) * 16 if rows % 32 else rows // 2
        return (pl.ds(0, cut), pl.ds(0, w)), (pl.ds(cut, rows - cut), pl.ds(0, w))
    return (pl.ds(0, rows), pl.ds(0, w // 2)), (pl.ds(0, rows), pl.ds(w // 2, w // 2))


class Gather:
    def __init__(self, net, buf):
        x, y, c = net.x, net.y, net.c
        a, b = halves(*buf.shape[-2:])

        def copy(d, yy, xx, half, mask):
            def ends():
                ref = buf.at[net.zs[d], yy, xx, c]
                ref = ref if half is None else ref.at[half[0], half[1]]
                return ref, ref

            return net.copy(ends, mask)

        def pair(d):
            def ends():
                ref = buf.at[net.zs[d], :, :, c]
                return ref, ref

            return net.copy(ends, 1)

        slots = range(4)
        self.along_z = [None] + [copy(0, y, x, None, d << 3) for d in (1, 2, 3)]
        self.to_y = [copy(d, y, x, a, 4) for d in slots]
        self.to_x = [copy(d, y, x, b, 2) for d in slots]
        self.own_x = [copy(d, y, x, a, 2) for d in slots]
        self.own_y = [copy(d, y, x, b, 4) for d in slots]
        self.far_x = [copy(d, 1 - y, x, a, 2) for d in slots]
        self.far_y = [copy(d, y, 1 - x, b, 4) for d in slots]
        self.pair = [pair(d) for d in slots]

    def send_z(self, d):
        self.along_z[d].start()

    def plane(self, d):
        if d:
            self.along_z[d].wait_recv()
        self.to_y[d].start()
        self.to_x[d].start()
        self.own_x[d].start()
        self.own_y[d].start()

    def across(self, d):
        self.to_y[d].wait_recv()
        self.far_x[d].start()
        self.to_x[d].wait_recv()
        self.far_y[d].start()

    def core(self, d):
        for copy in (self.own_x, self.own_y, self.far_x, self.far_y):
            copy[d].wait_recv()
        self.pair[d].start()

    def here(self, d):
        self.pair[d].wait_recv()

    def sent(self, d):
        for copy in (self.to_y, self.to_x, self.own_x, self.own_y, self.far_x, self.far_y, self.pair):
            copy[d].wait_send()
        if d == 0:
            for k in (1, 2, 3):
                self.along_z[k].wait_send()


class Reduce:
    def __init__(self, net, part, slots, bufs, r4):
        self.net, self.part, self.slots, self.r4 = net, part, slots, r4
        self.recv1, self.r2a, self.r2b, self.r3a, self.r3b = bufs
        x, y, c = net.x, net.y, net.c
        self.a, self.b = halves(*part.shape[-2:])
        planes = pl.ds(0, 4) if len(slots) == 4 else pl.ds(net.zs[slots[0]], 1)
        self.planes = range(4) if len(slots) == 4 else [net.zs[slots[0]]]
        a, b = self.a, self.b

        def one(yy, xx):
            return net.copy(lambda: (part.at[planes, yy, xx, 1 - c], self.recv1.at[:, yy, xx]), 1)

        self.s1 = {(fy, fx): one(1 - y if fy else y, 1 - x if fx else x) for fx in (1, 0) for fy in (1, 0)}

        def two_a(yy):
            return net.copy(lambda: (part.at[planes, yy, 1 - x, c, a[0], a[1]], self.r2a.at[:, yy]), 2)

        def two_b(xx):
            return net.copy(lambda: (part.at[planes, 1 - y, xx, c, b[0], b[1]], self.r2b.at[:, xx]), 4)

        self.s2a = [two_a(1 - y), two_a(y)]
        self.s2b = [two_b(1 - x), two_b(x)]
        self.s3a = net.copy(lambda: (part.at[planes, 1 - y, x, c, a[0], a[1]], self.r3a), 4)
        self.s3b = net.copy(lambda: (part.at[planes, y, 1 - x, c, b[0], b[1]], self.r3b), 2)

        def four(d):
            return net.copy(lambda: (part.at[net.zs[d], y, x, c], r4.at[d - 1]), d << 3)

        self.s4 = {d: four(d) for d in slots if d}

    def add(self, ref, other):
        ref[...] = (ref[...].astype(F32) + other[...].astype(F32)).astype(BF)

    def one(self):
        for copy in self.s1.values():
            copy.start()

    def two(self):
        net = self.net
        x, y, c = net.x, net.y, net.c

        def add_all(fy, fx):
            self.s1[fy, fx].wait_recv()
            yy, xx = (1 - y if fy else y), (1 - x if fx else x)
            for k, z in enumerate(self.planes):
                self.add(self.part.at[z, yy, xx, c], self.recv1.at[k, yy, xx])

        add_all(1, 1)
        self.s2a[0].start()
        self.s2b[0].start()
        add_all(0, 1)
        self.s2a[1].start()
        add_all(1, 0)
        self.s2b[1].start()
        add_all(0, 0)

    def three(self):
        net = self.net
        x, y, c = net.x, net.y, net.c
        a, b = self.a, self.b

        def add_half(yy, xx, half, buf, spot):
            for k, z in enumerate(self.planes):
                self.add(self.part.at[z, yy, xx, c, half[0], half[1]], buf.at[k, spot])

        self.s2a[0].wait_recv()
        add_half(1 - y, x, a, self.r2a, 1 - y)
        self.s3a.start()
        self.s2b[0].wait_recv()
        add_half(y, 1 - x, b, self.r2b, 1 - x)
        self.s3b.start()
        self.s2a[1].wait_recv()
        add_half(y, x, a, self.r2a, y)
        self.s2b[1].wait_recv()
        add_half(y, x, b, self.r2b, x)

    def four(self):
        net = self.net
        x, y, c = net.x, net.y, net.c
        for copy, half, buf in ((self.s3a, self.a, self.r3a), (self.s3b, self.b, self.r3b)):
            copy.wait_recv()
            for k, z in enumerate(self.planes):
                self.add(self.part.at[z, y, x, c, half[0], half[1]], buf.at[k])
        for copy in self.s4.values():
            copy.start()

    def sent(self):
        for copy in [*self.s1.values(), *self.s2a, *self.s2b, self.s3a, self.s3b, *self.s4.values()]:
            copy.wait_send()


def summed(net, part, reduces, r4):
    total = part[net.z, net.y, net.x, net.c].astype(F32)
    for job in reduces:
        for d, copy in job.s4.items():
            copy.wait_recv()
            total += r4[d - 1].astype(F32)
    return total


def reduce_buffers(rows, w, planes):
    a, b = halves(rows, w)
    sa, sb = (a[0].size, a[1].size), (b[0].size, b[1].size)
    shapes = [(planes, 2, 2, rows, w), (planes, 2) + sa, (planes, 2) + sb, (planes,) + sa, (planes,) + sb]
    return [pltpu.VMEM(s, BF) for s in shapes]


def block_kernel(remote, names, *refs):
    r = dict(zip(names, refs))
    images = r["tok"].shape[0] // PAD
    w1a, w1b, uw, vw = arrays = [r[k] for k in ("w1a", "w1b", "uw", "vw")]
    sem = r["sem"]
    cot_load = pltpu.make_async_copy(r["cot"], r["cotv"], sem.at[4])
    cot_load.start()
    x0 = r["hn4"]
    tok_load = pltpu.make_async_copy(r["tok"], x0, sem.at[6])
    tok_load.start()

    if remote:
        net = Net(r["send_sem"], r["recv_sem"])
        own = [buf.at[net.z, net.y, net.x, net.c] for buf in arrays]
        tall = [r["ge"].at[pl.ds(0, r[name].shape[0]), pl.ds(LANES * k, LANES)] for k, name in enumerate(FLAT[-2:])]
        loads = [pltpu.make_async_copy(r[name], ref, sem.at[k]) for k, (name, ref) in enumerate(zip(FLAT[-2:], tall))]
        for copy in loads:
            copy.start()
        places = small_places(net.me)
        assemble_attention(own[0], 0, r["in_one"], r["out_one"])
        assemble_small(own[0], places, r["small"][...])
        net.barrier()
        ga, gb, gu, gv = [Gather(net, buf) for buf in arrays]
        experts = [net.zs[d] for d in range(4)]
        for d in (1, 2, 3):
            ga.send_z(d)
        ga.plane(0)
        assemble_attention(own[1], 0, r["in_two"], r["out_two"])
        own[1][48:96, :] = chunk_rows(r["widen"][...], 0, 4).astype(BF)
        own[1][96:144, :] = picked(48, r["narrow"][...], lambda row, k: 3 * row + k).astype(BF)
    else:
        loads = [
            pltpu.make_async_copy(r[k + "_in"], buf, sem.at[j])
            for j, (k, buf) in enumerate(zip(("w1a", "w1b", "uw", "vw"), arrays))
        ]
        for copy in loads:
            copy.start()
        experts = range(4)
    x1, x2, x3, b, dhn = (r[k] for k in ("x1", "x2", "x3", "b", "dhn"))
    x4 = b
    valid, cot = r["valid"], r["cotv"]
    cot_load.wait()
    tok_load.wait()
    for i in range(images):
        rows = pl.ds(PAD * i, PAD)
        cot[rows, :] = (cot[rows, :].astype(F32) * valid[i].astype(F32)).astype(BF)
    dhn[...] = jnp.zeros_like(dhn)
    table = r["table"]
    win1, wout1, wid1, win2, wout2 = (r[k] for k in ("win1", "wout1", "wid1", "win2", "wout2"))

    def none():
        return None

    def batch(*steps):
        def tick():
            for step in steps:
                step()

        return tick if remote else none

    def both(step, d):
        return batch(lambda: getattr(gu, step)(d), lambda: getattr(gv, step)(d))

    if remote:
        ga.across(0)
        for d in (1, 2, 3):
            ga.plane(d)
        for d in (1, 2, 3):
            gb.send_z(d)
        gb.plane(0)
        for d in (1, 2, 3):
            ga.across(d)
        for d in range(4):
            ga.core(d)
        gb.across(0)
        gb.plane(1)
        for copy in loads:
            copy.wait()
        for j in range(FF // D):
            own[2][:, pl.ds(D * j, D)] = picked(48, tall[0][...], lambda row, k: 12 * row + 3 * j + k).astype(BF)
        own[3][...] = picked(192, tall[1][...], lambda row, k: 3 * row + k).astype(BF)
        both("send_z", 1)()
        both("send_z", 2)()
        for d in range(4):
            ga.here(d)
        gb.plane(2)
        gb.plane(3)
    else:
        loads[0].wait()

    decode(w1a, 0, (win1, wout1))
    decode_small(w1a, r["gains"], r["router"])
    gains = [r["gains"][pl.ds(k, 1), :] for k in range(4)]
    router = r["router"][...]
    ticks = [
        batch(lambda: gb.across(1), lambda: gb.across(2), lambda: gb.across(3), both("plane", 0)),
        batch(lambda: gb.core(0), lambda: gb.core(1), lambda: gb.core(2)),
        batch(lambda: gb.core(3), both("send_z", 3)),
        batch(both("across", 0)),
    ]
    attention_forward(images, x0, x1, gains[0], win1, wout1, r["hn1"], r["qkv1"], r["pb1"], r["o1"], ticks)
    if remote:
        for d in range(4):
            gb.here(d)
    else:
        loads[1].wait()
    decode(w1b, 48, (wid1,))
    decode(w1b, 0, (win2, wout2))
    ticks = [both("plane", 1), both("core", 0)]
    dense_forward(images, x1, x2, gains[1], wid1, w1b, r["hn2"], r["z1"], r["g1"], ticks)
    ticks = [none, both("across", 1), none, both("plane", 2)]
    attention_forward(images, x2, x3, gains[2], win2, wout2, r["hn3"], r["qkv2"], r["pb2"], r["o2"], ticks)
    router_forward(images, x3, x4, gains[3], router, r["routes"], r["hn4"], table)

    if remote:
        buffers = iter(r["rs"])
        take = lambda: [next(buffers) for _ in range(5)]
        bufs_u, bufs_v = [take(), take()], [take(), take()]
        ru = [Reduce(net, uw, [d], bufs_u[d % 2], r["r4u"]) for d in range(4)]
        rv = [Reduce(net, vw, [d], bufs_v[d % 2], r["r4v"]) for d in range(4)]
        rb = Reduce(net, w1b, [0, 1, 2, 3], take(), r["r4b"])
        ra = Reduce(net, w1a, [0, 1, 2, 3], take(), r["r4a"])
    else:
        loads[2].wait()
        loads[3].wait()

    def reduce_step(step, d):
        return batch(lambda: getattr(ru[d], step)(), lambda: getattr(rv[d], step)())

    def run_expert(d, ticks, late):
        if remote:
            gu.here(d)
            gv.here(d)
        before = batch(lambda: gu.sent(d), lambda: gv.sent(d))
        late = [*late, batch(lambda: ru[d].one())]
        expert_step(
            images, experts[d], x4, cot, dhn, uw, vw, r["hn4"], table, r["ze"], r["ge"], r["dy"], ticks, late, before
        )
        batch(lambda: rv[d].one())()

    both("core", 1)()
    run_expert(0, [both("across", 2), both("plane", 3)], [both("core", 2)])
    both("across", 3)()
    run_expert(1, [reduce_step("two", 0), both("core", 3)], [])
    reduce_step("three", 0)()
    run_expert(2, [reduce_step("two", 1), reduce_step("four", 0)], [])
    reduce_step("three", 1)()
    run_expert(3, [reduce_step("two", 2), reduce_step("four", 1)], [])
    reduce_step("three", 2)()
    out_cols = pl.ds(0, D)
    for i in range(images):
        rows = pl.ds(PAD * i, PAD)
        r["ge"][rows, out_cols] = (x4[rows, :] * valid[i].astype(F32)).astype(BF)
    out_store = pltpu.make_async_copy(r["ge"].at[:, out_cols], r["out"], sem.at[5])
    out_store.start()
    gs, dgain, drouter = r["gs"], r["dgain"], r["drouter"]
    gs[...] = jnp.zeros_like(gs)
    router_backward(images, b, cot, x3, gains[3], router, dhn, table, r["hn4"], drouter, dgain)
    tok_load.start()
    gs[pl.ds(4, EXPERTS), :] = drouter[pl.ds(0, EXPERTS), :]
    gs[pl.ds(3, 1), :] = dgain[...]
    dqkv, da = r["ze"], r["dy"]
    ticks = [reduce_step("two", 3), reduce_step("four", 2), reduce_step("three", 3)]
    attention_backward(images, b, x2, gains[2], win2, wout2, r["hn3"], r["qkv2"], r["pb2"], r["o2"], da, dqkv, dgain, win2, wout2, ticks)
    gs[pl.ds(2, 1), :] = dgain[...]
    batch(*(lambda d=d: gb.sent(d) for d in range(4)))()
    encode(w1b, 0, (win2, wout2))
    ticks = [reduce_step("four", 3)]
    dense_backward(images, b, x1, gains[1], wid1, w1b, r["hn2"], r["z1"], r["g1"], da, dgain, wid1, ticks)
    gs[pl.ds(1, 1), :] = dgain[...]
    encode(w1b, 48, (wid1,))
    if remote:
        rb.one()
    lanes = pl.ds(0, LANES)

    def leave(name, row, k):
        flat = r[name + "_out"]
        return pltpu.make_async_copy(table.at[pl.ds(row, flat.shape[0]), :], flat, sem.at[k])

    def tall_sum():
        scatter_rows(table, 0, lanes, summed(net, vw, rv, r["r4v"]))
        leave("tall_v", 0, 7).start()

    tok_load.wait()
    ticks = [batch(lambda: rb.two()), none, batch(lambda: rb.three()), batch(tall_sum, lambda: rb.four())]
    attention_backward(images, b, x0, gains[0], win1, wout1, r["hn1"], r["qkv1"], r["pb1"], r["o1"], da, dqkv, dgain, win1, wout1, ticks)
    gs[pl.ds(0, 1), :] = dgain[...]
    batch(*(lambda d=d: ga.sent(d) for d in range(4)))()
    encode(w1a, 0, (win1, wout1))
    encode_small(w1a, gs)
    if remote:
        ra.one()
    r["o1"][...] = b[...].astype(BF)
    delta_store = pltpu.make_async_copy(r["o1"], r["dtok"], sem.at[6])
    delta_store.start()
    if remote:
        leave("tall_v", 0, 7).wait()
        scatter_rows(table, 0, lanes, summed(net, uw, ru, r["r4u"]))
        leave("tall_u", 0, 8).start()
        ra.two()
        total = summed(net, w1b, [rb], r["r4b"])
        scatter_chunks(r["in_two_out"], 0, lanes, total, 0, 3)
        scatter_chunks(r["out_two_out"], 0, lanes, total, 3, 1)
        scatter_chunks(table, 576, lanes, total, 4, 4)
        leave("widen", 576, 9).start()
        scatter_rows(r["narrow_out"], 0, lanes, total[96:144])
        ra.three()
        ra.four()
        total = summed(net, w1a, [ra], r["r4a"])
        scatter_chunks(r["in_one_out"], 0, lanes, total, 0, 3)
        scatter_chunks(r["out_one_out"], 0, lanes, total, 3, 1)
        exact = dict(precision=lax.Precision.HIGHEST, preferred_element_type=F32)
        small = jnp.zeros((8, LANES), F32)
        for q, place in enumerate(places):
            line = jnp.broadcast_to(total[48 + q : 49 + q], (8, D))
            small += lax.dot_general(line, place, (((1,), (1,)), ((), ())), **exact)
        r["small_out"][...] = small
        leave("tall_u", 0, 8).wait()
        leave("widen", 576, 9).wait()
        for job in (*ru, *rv, rb, ra):
            job.sent()
    else:
        stores = [
            pltpu.make_async_copy(buf, r[k + "_out"], sem.at[j])
            for j, (k, buf) in enumerate(zip(("w1a", "w1b", "uw", "vw"), arrays))
        ]
        for copy in stores:
            copy.start()
        for copy in stores:
            copy.wait()
    out_store.wait()
    delta_store.wait()


PIECES = ((64, D), (144, D), (48, FF), (192, D))
AWAY = ("widen", "tall_u", "tall_v")
FLAT = ("in_one", "out_one", "widen", "narrow", "in_two", "out_two", "tall_u", "tall_v")


def run_blocks(remote, tok, cot, valid, routes, *weights):
    t = tok.shape[0]
    images = t // PAD
    v = pltpu.VMEM
    vmem, smem, hbm = (pl.BlockSpec(memory_space=m) for m in (pltpu.VMEM, pltpu.SMEM, pl.ANY))
    whole = [(4, 2, 2, 2) + s for s in PIECES]
    inputs = dict(
        tok=(tok, hbm), cot=(cot, hbm), valid=(valid, smem), routes=(routes, vmem),
    )
    if remote:
        inputs.update({name: (w, hbm if name in FLAT[-2:] else vmem) for name, w in zip((*FLAT, "small"), weights)})
    else:
        inputs.update({name + "_in": (w, hbm) for name, w in zip(("w1a", "w1b", "uw", "vw"), weights)})
    flat = jax.ShapeDtypeStruct(tok.shape, BF)
    outputs = dict(out=(flat, hbm), dtok=(flat, hbm))
    if remote:
        for name, w in zip(FLAT, weights):
            outputs[name + "_out"] = (jax.ShapeDtypeStruct(w.shape, F32), hbm if name in AWAY else vmem)
        outputs["small_out"] = (jax.ShapeDtypeStruct((8, LANES), F32), vmem)
    else:
        for name, full in zip(("w1a", "w1b", "uw", "vw"), whole):
            outputs[name + "_out"] = (jax.ShapeDtypeStruct(full, BF), hbm)
    scratch = dict(
        w1a=v(whole[0], BF), w1b=v(whole[1], BF), uw=v(whole[2], BF), vw=v(whole[3], BF),
        win1=v((D, 3 * D), BF), wout1=v((D, D), BF), wid1=v((D, FF), BF), win2=v((D, 3 * D), BF), wout2=v((D, D), BF),
        x1=v((t, D), F32), x2=v((t, D), F32), x3=v((t, D), F32), b=v((t, D), F32), dhn=v((t, D), F32),
        hn1=v((t, D), BF), hn2=v((t, D), BF), hn3=v((t, D), BF), hn4=v((t, D), BF),
        qkv1=v((t, 3 * D), BF), qkv2=v((t, 3 * D), BF), o1=v((t, D), BF), o2=v((t, D), BF),
        pb1=v((images * PAIRS, 2 * PAD, PAD), BF), pb2=v((images * PAIRS, 2 * PAD, PAD), BF),
        z1=v((t, FF), BF), g1=v((t, FF), BF), ze=v((t, FF), BF), ge=v((t, FF), BF), dy=v((t, D), BF), cotv=v((t, D), BF),
        table=v((t, LANES), F32),
        drouter=v((8, D), F32), dgain=v((1, D), F32), gs=v((16, D), F32), gains=v((8, D), F32), router=v((LANES, D), BF),
        sem=pltpu.SemaphoreType.DMA((16,)),
    )
    if remote:
        scratch["rs"] = [
            spec
            for piece, planes in [(PIECES[2], 1)] * 2 + [(PIECES[3], 1)] * 2 + [(PIECES[1], 4), (PIECES[0], 4)]
            for spec in reduce_buffers(*piece, planes)
        ]
        for k, piece in zip("abuv", PIECES):
            scratch["r4" + k] = v((3,) + piece, BF)
        scratch["send_sem"] = pltpu.SemaphoreType.DMA((256,))
        scratch["recv_sem"] = pltpu.SemaphoreType.DMA((256,))
    names = (*inputs, *outputs, *scratch)
    params = dict(collective_id=0, has_side_effects=True) if remote else {}
    return pl.pallas_call(
        functools.partial(block_kernel, remote, names),
        out_shape=tuple(o[0] for o in outputs.values()),
        in_specs=[i[1] for i in inputs.values()],
        out_specs=tuple(o[1] for o in outputs.values()),
        scratch_shapes=list(scratch.values()),
        compiler_params=pltpu.CompilerParams(vmem_limit_bytes=127 * 2**19, **params),
    )(*[i[0] for i in inputs.values()])


def hand_over(*arrays):
    count = len(arrays)

    def kernel(*refs):
        for k in range(count):
            refs[count + k][...] = refs[k][...]

    vmem = pl.BlockSpec(memory_space=pltpu.VMEM)
    return pl.pallas_call(
        kernel,
        out_shape=[jax.ShapeDtypeStruct(a.shape, a.dtype) for a in arrays],
        in_specs=[vmem] * count,
        out_specs=[vmem] * count,
    )(*arrays)


def all_pieces(norm_gains, in_one, out_one, widen, narrow, router, in_two, out_two, experts_widen, experts_narrow):
    def cut(*matrices):
        side = jnp.concatenate([m.reshape(D, -1) for m in matrices], axis=1)
        return side.reshape(SHARDS, ROWS, -1, D).transpose(0, 2, 1, 3).reshape(SHARDS, -1, D)

    small = jnp.zeros((SHARDS, 16, D), BF)
    small = small.at[:: SHARDS // 4, 0].set(norm_gains.reshape(4, D))
    small = small.at[0, 1 : 1 + EXPERTS].set(router.reshape(D, EXPERTS).T)
    parts = (
        jnp.concatenate([cut(in_one, out_one), small], axis=1),
        jnp.concatenate([cut(in_two, out_two), cut(widen), narrow.reshape(SHARDS, -1, D)], axis=1),
        experts_widen.reshape(SHARDS, -1, FF),
        experts_narrow.reshape(SHARDS, -1, D),
    )
    return [p.reshape((4, 2, 2, 2) + p.shape[1:]) for p in parts]


def all_deltas(*parts):
    w1a, w1b, uw, vw = (p.astype(F32).reshape((SHARDS,) + p.shape[-2:]) for p in parts)

    def join(part):
        return part.reshape(SHARDS, -1, ROWS, D).transpose(0, 2, 1, 3).reshape(D, -1)

    one, two = join(w1a[:, 0:48]), join(w1b[:, 0:48])
    whole = (
        w1a[:: SHARDS // 4, 48], one[:, : 3 * D], one[:, 3 * D :], join(w1b[:, 48:96]), w1b[:, 96:144], w1a[0, 49:53].T,
        two[:, : 3 * D], two[:, 3 * D :], uw, vw,
    )
    return [p.reshape(-1) for p in whole]


def on_device(shards, tokens, cotangent, image_valid, routes, *weights):
    images = tokens.shape[0] * tokens.shape[1]

    def padded(array):
        return jnp.pad(array, ((0, 0), (0, 0), (0, PAD - SEQ), (0, 0))).reshape(images * PAD, D)

    def cut(array):
        return array.reshape(tokens.shape[:2] + (PAD, D))[:, :, :SEQ]

    named = routes.reshape(images, SEQ, 2).transpose(0, 2, 1)
    named = jnp.pad(named, ((0, 0), (0, 6), (0, 2 * LANES - SEQ)))
    data = (padded(tokens), padded(cotangent), image_valid.reshape(images), named)
    if shards == SHARDS:
        gains, in_one, out_one, widen, narrow, router, in_two, out_two, tall_u, tall_v = weights
        flat = [w.reshape(-1, LANES) for w in (in_one, out_one, widen, narrow, in_two, out_two, tall_u, tall_v)]
        small = jnp.pad(jnp.concatenate([gains, router]), (0, LANES - 2 * gains.shape[0]))
        small = jnp.broadcast_to(small[None], (16, LANES))
        out, delta, *sums, small = run_blocks(True, *data, *flat, small)
        sums = [d.reshape(-1) for d in hand_over(*sums)]
        share = gains.shape[0]
        deltas = [small[0, :share], *sums[:4], small[0, share : 2 * share], *sums[4:]]
    else:
        whole = [lax.all_gather(w, "fsdp", axis=0, tiled=True) for w in weights]
        out, delta, *sums = run_blocks(False, *data, *all_pieces(*whole))
        deltas = [lax.psum_scatter(d, "fsdp", scatter_dimension=0, tiled=True) for d in all_deltas(*sums)]
    return (cut(out), cut(delta), *deltas)


def solution(mesh):
    split, flat = P(None, "fsdp", None, None), P("fsdp")
    return jax.shard_map(
        functools.partial(on_device, mesh.shape["fsdp"]),
        mesh=mesh,
        in_specs=(split, split, P(None, "fsdp"), split) + (flat,) * 10,
        out_specs=(split, split) + (flat,) * 10,
        check_vma=False,
    )
```
